32 devices in a mesh: dp: 16 (over z, y, core), blk: 2 (over x).
Axes of the slice: x: 2, y: 2, z: 4, core: 2. Of those that a mesh axis runs over, the one named last changes fastest.
Arguments:
- tokens: bfloat16 [32, 1024, 768], P('dp', 'blk'), may hold values from -6 to 6
- layout: int32 [32, 1024], P('dp'), may hold values from 0 to 255
- lengths: int32 [32], P('dp'), may hold values from 128 to 1024, as said below
- gain_attn: bfloat16 [768], P(('dp', 'blk')), may hold values from 0.5 to 1.5
- w_query: bfloat16 [768, 768], P(('dp', 'blk')), may hold values from -0.21875 to 0.21875
- w_key: bfloat16 [768, 768], P(('dp', 'blk')), may hold values from -0.21875 to 0.21875
- w_value: bfloat16 [768, 768], P(('dp', 'blk')), may hold values from -0.21875 to 0.21875
- w_output: bfloat16 [768, 768], P(('dp', 'blk')), may hold values from -2.5 to 2.5
- gain_ffn: bfloat16 [768], P(('dp', 'blk')), may hold values from 0.5 to 1.5
- w_in: bfloat16 [768, 3072], P(('dp', 'blk')), may hold values from -0.21875 to 0.21875
- w_out: bfloat16 [3072, 768], P(('dp', 'blk')), may hold values from -0.109375 to 0.109375
- rel_table: bfloat16 [32, 12], replicated, may hold values from -4 to 4
- grad_out: bfloat16 [32, 1024, 768], P('dp', 'blk'), may hold values from -6 to 6
Outputs:
- mixed: bfloat16 [32, 1024, 768], P('dp', 'blk')
- grad_tokens: bfloat16 [32, 1024, 768], P('dp', 'blk')
- grad_gain_attn: float32 [768], P(('dp', 'blk'))
- grad_w_query: float32 [768, 768], P(('dp', 'blk'))
- grad_w_key: float32 [768, 768], P(('dp', 'blk'))
- grad_w_value: float32 [768, 768], P(('dp', 'blk'))
- grad_w_output: float32 [768, 768], P(('dp', 'blk'))
- grad_gain_ffn: float32 [768], P(('dp', 'blk'))
- grad_w_in: float32 [768, 3072], P(('dp', 'blk'))
- grad_w_out: float32 [3072, 768], P(('dp', 'blk'))
- grad_rel_table: float32 [32, 12], replicated
The draws below stay inside these ranges and needn't reach their ends.
Inputs may be any that keep to these rules, and one draw needn't show every extreme that they name: `lengths`: among the 2 items of each index of dp, one has length 1024 and another 1024 // 8.
All inputs are finite; a program needn't handle non-finite values.
Results may differ from the reference program's by a relative error of at most 0.023.
Values may be sent and summed in bfloat16 or wider, within the bound.
A program may use at most 192 MiB of HBM per device.

```python
import jax
import jax.numpy as jnp
from jax import lax

D = 768
HEADS = 12
FF = 3072
BUCKETS = 32
SPAN = 256
L = 1024
SEQS = 2
ITEMS = 32


def draw_lengths(key, part):
    key = jax.random.fold_in(key, 7)
    key_base, key_first, key_offset = jax.random.split(key, 3)
    groups = ITEMS // SEQS
    base = jax.random.randint(key_base, (groups, SEQS), L // 8, L + 1)
    first = jax.random.randint(key_first, (groups, 1), 0, SEQS)
    offset = jax.random.randint(key_offset, (groups, 1), 1, SEQS)
    second = (first + offset) % SEQS
    column = jnp.arange(SEQS)[None, :]
    result = jnp.where(column == first, L, jnp.where(column == second, L // 8, base))
    return result.reshape(ITEMS).astype(jnp.int32)


def with_ends(values, rng, smallest, high):
    spot = [jax.random.randint(jax.random.fold_in(rng, axis), (), 0, length) for axis, length in enumerate(values.shape)]
    longest = values.shape.index(max(values.shape))
    beside = spot[:longest] + [(spot[longest] + 1) % values.shape[longest]] + spot[longest + 1:]
    return values.at[tuple(spot)].set(smallest).at[tuple(beside)].set(high)


def raised(values, key, source, target, shards_of, factor):
    def block_of(axis_at):
        return (jnp.arange(values.shape[axis_at]) // (values.shape[axis_at] // shards_of)).reshape((-1,) + (1,) * (values.ndim - 1 - axis_at))

    one_side = jax.random.permutation(key, shards_of)[block_of(target)]
    second = (block_of(target) + shards_of // 2) % shards_of
    return jnp.where((block_of(source) == one_side) | (block_of(source) == second), factor * values, values)


def level_of(key, dims, pieces, least, high):
    loudness = 1.0
    for position, shards_of in pieces:
        steps = jax.random.uniform(jax.random.fold_in(jax.random.fold_in(key, 6), position), (shards_of,), jnp.float32, least / len(pieces), high / len(pieces))
        loudness = loudness * jnp.repeat(jnp.exp(steps), dims[position] // shards_of).reshape((-1,) + (1,) * (len(dims) - 1 - position))
    return loudness


def normal_values(key, dims, deviation, bound, shards=(), kind=jnp.bfloat16):
    factor_of = level_of(key, dims, shards, -0.22, 0.18) if shards else 1.0
    entries = jax.random.normal(key, dims, jnp.float32) * deviation * factor_of
    return jnp.minimum(jnp.maximum(entries, -bound), bound).astype(kind)


def bell_draw_with(own_key, dims, scale, reach, pieces, heavy, held_as=jnp.bfloat16):
    values = scale * jax.random.normal(own_key, dims, jnp.float32)
    if pieces:
        values = values * level_of(own_key, dims, pieces, -0.22, 0.18)
    return jnp.clip(raised(values, jax.random.fold_in(own_key, 3), *heavy), -reach, reach).astype(held_as)


def setup_inputs(seed: int = 0) -> dict:
    splits = jax.random.split(jax.random.key(seed), 14)
    tokens = bell_draw_with(splits[0], (ITEMS, L, D), 1.0, 6.0, ((0, 16), (1, 2)), (0, 2, 16, 2.0))
    layout = with_ends(jax.random.randint(splits[1], (ITEMS, L), 0, SPAN), jax.random.fold_in(splits[1], 1), 0, SPAN - 1).astype(jnp.int32)
    lengths = draw_lengths(jax.random.fold_in(splits[13], 71), 0)
    gain_attn = jnp.clip(1.0 + 0.1 * jax.random.normal(splits[3], (D,), jnp.float32), 0.5, 1.5).astype(jnp.bfloat16)
    w_query = normal_values(splits[4], (D, D), D ** -0.5, 0.21875, ((0, 32),))
    w_key = normal_values(splits[5], (D, D), D ** -0.5, 0.21875, ((0, 32),))
    w_value = normal_values(splits[6], (D, D), D ** -0.5, 0.21875, ((0, 32),))
    w_output = normal_values(splits[7], (D, D), (D // 128) ** -0.5, 2.5, ((0, 32),))
    gain_ffn = jnp.clip(1.0 + 0.1 * jax.random.normal(splits[8], (D,), jnp.float32), 0.5, 1.5).astype(jnp.bfloat16)
    w_in = normal_values(splits[9], (D, FF), D ** -0.5, 0.21875, ((0, 32),))
    w_out = normal_values(splits[10], (FF, D), FF ** -0.5, 0.109375, ((0, 32),))
    rel_table = normal_values(splits[11], (BUCKETS, HEADS), 1.0, 4.0)
    grad_out = normal_values(splits[12], (ITEMS, L, D), 1.0, 6.0, ((0, 16), (1, 2)))
    return {"tokens": tokens, "layout": layout, "lengths": lengths, "gain_attn": gain_attn, "w_query": w_query, "w_key": w_key, "w_value": w_value, "w_output": w_output, "gain_ffn": gain_ffn, "w_in": w_in, "w_out": w_out, "rel_table": rel_table, "grad_out": grad_out}


EPSILON = 1e-06
SCALE = 0.125
NEGATIVE = -1e+30
THRESHOLDS = (12, 16, 23, 32, 46, 64, 91)

@jax.custom_vjp
def low(v):
    return lax.optimization_barrier(v.astype(jnp.bfloat16)).astype(jnp.float32)

@jax.custom_vjp
def low_back(v):
    return v

def low_keep(v):
    return (low(v), None)

def low_pass(kept, grad):
    return (grad,)

def back_keep(v):
    return (v, None)

def back_low(kept, grad):
    return (low(grad),)
low.defvjp(low_keep, low_pass)
low_back.defvjp(back_keep, back_low)

def bucket_of(relative):
    magnitude = jnp.abs(relative)
    larger = 8 + sum(((magnitude >= limit).astype(jnp.int32) for limit in THRESHOLDS))
    return jnp.where(magnitude < 8, magnitude, larger) + 16 * (relative > 0).astype(jnp.int32)

def rms_norm(values, gain):
    return values * lax.rsqrt(lax.optimization_barrier(jnp.mean(values * values, axis=-1, keepdims=True)) + EPSILON) * gain

def gelu_exact(values):
    return jax.nn.gelu(values, approximate=False)

def matmul(left, right):
    return jnp.dot(left, right, precision=lax.Precision.HIGHEST)

def encoder_layer(params, hidden, positions, length):
    gain_one, query_weight, key_weight, value_weight, output_weight, gain_two, inner_weight, outer_weight, table = params
    item_length, model_width = hidden.shape
    head_count = table.shape[1]
    head_size = model_width // head_count
    normed = low(rms_norm(hidden, gain_one))
    queries = low(low_back(matmul(normed, query_weight))).reshape(item_length, head_count, head_size)
    key_rows = low(low_back(matmul(normed, key_weight))).reshape(item_length, head_count, head_size)
    values = low(low_back(matmul(normed, value_weight))).reshape(item_length, head_count, head_size)
    key_valid = jnp.arange(item_length) < length
    block_rows = min(512, item_length)

    def attend(block):
        query_block, query_positions = block
        buckets = bucket_of(positions[None, :] - query_positions[:, None])
        bias = jnp.transpose(table[buckets], (2, 0, 1))
        scores = jnp.einsum('qhd,khd->hqk', query_block, key_rows, precision=lax.Precision.HIGHEST) * SCALE + bias
        scores = jnp.where(key_valid[None, None, :], low_back(scores), NEGATIVE)
        weights = low(jax.nn.softmax(scores, axis=-1))
        return jnp.einsum('hqk,khd->qhd', weights, values, precision=lax.Precision.HIGHEST)
    attended = lax.map(jax.checkpoint(attend), (queries.reshape(-1, block_rows, head_count, head_size), positions.reshape(-1, block_rows)))
    attended = low(low_back(attended.reshape(item_length, model_width)))
    resid = hidden + low_back(matmul(attended, output_weight))
    normed_two = low(rms_norm(resid, gain_two))
    pre_act = low_back(matmul(normed_two, inner_weight))
    activated = low(gelu_exact(pre_act))
    return resid + low_back(matmul(activated, outer_weight))

def reference(tokens, layout, lengths, gain_attn, w_query, w_key, w_value, w_output, gain_ffn, w_in, w_out, rel_table, grad_out):
    params = tuple((array.astype(jnp.float32) for array in (gain_attn, w_query, w_key, w_value, w_output, gain_ffn, w_in, w_out, rel_table)))
    inputs = tokens.astype(jnp.float32)
    cotangent = grad_out.astype(jnp.float32)

    def forward(weights, hidden_all):

        def one_item(item):
            hidden, positions, length = item
            return encoder_layer(weights, hidden, positions, length)
        return lax.map(jax.checkpoint(one_item), (hidden_all, layout, lengths))
    outputs, pullback = jax.vjp(forward, params, inputs)
    grad_params, grad_inputs = pullback(cotangent)
    return (outputs.astype(jnp.bfloat16), grad_inputs.astype(jnp.bfloat16), grad_params[0], grad_params[1], grad_params[2], grad_params[3], grad_params[4], grad_params[5], grad_params[6], grad_params[7], grad_params[8])
```

```python
import functools

import jax
import jax.numpy as jnp
import numpy as np
from jax import lax
from jax.experimental import pallas as pl
from jax.experimental.pallas import tpu as pltpu
from jax.sharding import PartitionSpec as P

F32=jnp.float32; BF=jnp.bfloat16
SPAN=256
CH=256
def dot(a,b): return lax.dot_general(a,b,(((1,),(0,)),((),())),preferred_element_type=F32)
def eye_of(row, width, reverse):
    spots=lax.broadcasted_iota(jnp.int32,(width,row.shape[1]),0)
    if reverse: spots=width-1-spots
    return (spots==row).astype(F32).astype(BF)

def attend(n,L,S,R,E,steps,far,*refs):
    q,kf,vf,ks,vs,layq,layf,lays,mask,u=refs[:10]
    if far:
        shards=refs[10:13]; o,p,l=refs[13:16]; wholes=refs[16:19]
        kcat,qcat,vt,s_ref,ohq,send,recv,local=refs[19:]
        at,chains=gather_plan(shards,wholes,(send,recv),local)
        tick=ticker(spread(chains,GATHER_BEGIN,GATHER_LAG,2*steps),steps,at)
    else:
        o,p,l,kcat,qcat,vt,s_ref,ohq=refs[10:]
        tick=lambda u:None
    W=2*E
    spans=[L]*(n-1)+[S]
    @pl.when(pl.program_id(0)==0)
    def _():
        base=0
        for i,m in enumerate(spans):
            row=layf[i] if i<n-1 else lays[...]
            kcat[base:base+m,W:]=jnp.transpose(eye_of(row,SPAN,False).astype(F32)).astype(BF)
            ohq[i]=eye_of(layq[i],SPAN,False)
            base+=m
        vt[:,E:]=jnp.ones((2,vt.shape[1]-E,vt.shape[2]),BF)
    pair=pl.program_id(0)
    base=0
    for i,m in enumerate(spans):
        ch=min(CH,m)
        kcat[base:base+m,:W]=kf[i] if i<n-1 else ks[...]
        v=vf[i] if i<n-1 else vs[...]
        vtr=jnp.transpose(v.astype(F32)).astype(BF)
        vt[0,:E,:m]=vtr[:E]
        vt[1,:E,:m]=vtr[E:]
        qt=jnp.transpose(q[i].astype(F32)).astype(BF)
        outs=[]
        for h in range(2):
            if i==0: tick(h)
            urow=u[0,h:h+1,:]
            toep=pltpu.roll(jnp.broadcast_to(urow,(SPAN,2*SPAN)),0,1,stride=1,stride_axis=0)[:,:SPAN].astype(BF)
            qcat[h*E:(h+1)*E]=qt[h*E:(h+1)*E]
            qcat[(1-h)*E:(2-h)*E]=jnp.zeros((E,R),BF)
            qcat[W:]=dot(toep,ohq[i]).astype(BF)
            m8=jnp.full((8,R),-jnp.inf,F32)
            for c in range(0,m,ch):
                s=dot(kcat[base+c:base+c+ch],qcat[...])
                if 0<i<n-1: s=s+mask[i,c:c+ch,:]
                s_ref[c:c+ch]=s
                m8=jnp.maximum(m8,jnp.max(s.reshape(ch//8,8,R),axis=0))
            top=jnp.max(m8,axis=0,keepdims=True)
            for c in range(0,m,ch):
                p[0,h,base+c:base+c+ch]=jnp.exp(s_ref[c:c+ch]-top).astype(BF)
            full=dot(vt[h,:,:m],p[0,h,base:base+m])
            total=full[E:E+1]
            l[i,0,h:h+1]=total
            outs.append(full[:E]/total)
        o[i]=jnp.transpose(jnp.concatenate(outs,axis=0)).astype(BF)
        base+=m
    tick(2)

def attend_call(q,kf,vf,ks,vs,layq,layf,lays,mask,u,shards=()):
    n,R,D=q.shape; L=kf.shape[1]; S=ks.shape[0]; H=u.shape[0]*2; E=D//H; W=2*E
    KT=(n-1)*L+S
    full=lambda a: pl.BlockSpec(a.shape,lambda j:(0,)*a.ndim)
    return pl.pallas_call(functools.partial(attend,n,L,S,R,E,H//2,bool(shards)),
      grid=(H//2,),
      in_specs=[pl.BlockSpec((n,R,W),lambda j:(0,0,j)),
        pl.BlockSpec((n-1,L,W),lambda j:(0,0,j)),pl.BlockSpec((n-1,L,W),lambda j:(0,0,j)),
        pl.BlockSpec((S,W),lambda j:(0,j)),pl.BlockSpec((S,W),lambda j:(0,j)),
        full(layq),full(layf),full(lays),full(mask),pl.BlockSpec((1,2,2*SPAN),lambda j:(j,0,0))]+[pl.BlockSpec(memory_space=pl.ANY)]*len(shards),
      out_specs=[pl.BlockSpec((n,R,W),lambda j:(0,0,j)),
        pl.BlockSpec((1,2,KT,R),lambda j:(j,0,0,0)),
        pl.BlockSpec((n,1,2,R),lambda j:(0,j,0,0))]+[pl.BlockSpec(memory_space=pl.ANY)]*len(shards),
      out_shape=[jax.ShapeDtypeStruct((n,R,D),BF),jax.ShapeDtypeStruct((H//2,2,KT,R),BF),jax.ShapeDtypeStruct((n,H//2,2,R),F32)]
        +[jax.ShapeDtypeStruct((4,2,2,2)+s.shape,BF) for s in shards],
      scratch_shapes=[pltpu.VMEM((KT,W+SPAN),BF),pltpu.VMEM((W+SPAN,R),BF),pltpu.VMEM((2,E+16,L),BF),pltpu.VMEM((L,R),F32),pltpu.VMEM((n,SPAN,R),BF)]
        +([pltpu.SemaphoreType.DMA((5*GATHER_COPIES,))]*2+[pltpu.SemaphoreType.DMA((5,))] if shards else []),
      compiler_params=pltpu.CompilerParams(vmem_limit_bytes=56*2**20,dimension_semantics=("arbitrary",),**(dict(collective_id=2,has_side_effects=True) if shards else {})),
      name="attend",
    )(q,kf,vf,ks,vs,layq,layf,lays,mask,u,*shards)

def attend_back(n,L,S,R,E,steps,far,*refs):
    q,kf,vf,ks,vs,layq,layf,lays,o,do,p,l=refs[:12]
    if far:
        parts=refs[12:15]; dq,dkf,dvf,dks,dvs,t=refs[15:21]; totals=refs[21:24]
        kq,vaug,rhs,ds,ohq,nacc,qm,dm=refs[24:32]; send,recv,local=refs[-3:]
        at,chains=sum_plan(parts,totals,refs[32:-3],(send,recv),local)
        tick=ticker(spread(chains,SUM_BEGIN,SUM_LAG,2*steps),steps,at)
    else:
        dq,dkf,dvf,dks,dvs,t,kq,vaug,rhs,ds,ohq,nacc,qm,dm=refs[12:]
        tick=lambda u:None
    W=2*E
    spans=[L]*(n-1)+[S]
    @pl.when(pl.program_id(0)==0)
    def _():
        base=0
        for i,m in enumerate(spans):
            row=layf[i] if i<n-1 else lays[...]
            kq[:SPAN,base:base+m]=eye_of(row,SPAN,True)
            ohq[i]=jnp.transpose(eye_of(layq[i],SPAN,False).astype(F32)).astype(BF)
            base+=m
        vaug[:,W:]=(lax.broadcasted_iota(jnp.int32,(vaug.shape[0],W),1)<2).astype(F32).astype(BF)
        rhs[...]=jnp.zeros_like(rhs)
    nacc[...]=jnp.zeros_like(nacc)
    base=0
    lane=lax.broadcasted_iota(jnp.int32,(R,W),1)
    for i,m in enumerate(spans):
        ch=min(CH,m)
        kk=kf[i] if i<n-1 else ks[...]
        vaug[:m,:W]=vf[i] if i<n-1 else vs[...]
        kt=jnp.transpose(kk.astype(F32)).astype(BF)
        dot_=jnp.transpose(do[i].astype(F32))
        ot=jnp.transpose(o[i].astype(F32))
        scaled=[];
        for h in range(2):
            inv=1.0/l[i,0,h:h+1]
            scaled.append((dot_[h*E:(h+1)*E]*inv).astype(BF))
        sc=jnp.concatenate(scaled,axis=0)
        don=jnp.transpose(sc.astype(F32)).astype(BF)
        qq=q[i]
        zero=jnp.zeros((R,W),BF)
        for h in range(2):
            mine=(lane<E) if h==0 else (lane>=E)
            qm[h*R:(h+1)*R]=jnp.where(mine,qq,zero)
            dm[h*R:(h+1)*R]=jnp.where(mine,don,zero)
        dqs=[]
        for h in range(2):
            if i==0: tick(h)
            rhs[h*E:(h+1)*E]=scaled[h]
            rhs[(1-h)*E:(2-h)*E]=jnp.zeros((E,R),BF)
            delta=jnp.sum(scaled[h].astype(F32)*ot[h*E:(h+1)*E],axis=0,keepdims=True)
            hi=delta.astype(BF).astype(F32)
            lo=delta-hi
            spot=lax.broadcasted_iota(jnp.int32,(16,R),0)
            rhs[W:W+16]=jnp.where(spot==0,-hi,jnp.where(spot==1,-lo,0.0)).astype(BF)
            for c in range(0,m,ch):
                g=dot(vaug[c:c+ch],rhs[...])
                ds[c:c+ch,h*R:(h+1)*R]=(p[0,h,base+c:base+c+ch].astype(F32)*g).astype(BF)
            kq[SPAN:,base:base+m]=kt[h*E:(h+1)*E]
            both=dot(kq[:,base:base+m],ds[:m,h*R:(h+1)*R])
            dqs.append(both[SPAN:]*0.125)
            nacc[h]+=dot(both[:SPAN].astype(BF),ohq[i])
        dq[i]=jnp.transpose(jnp.concatenate(dqs,axis=0)).astype(BF)
        for c in range(0,m,ch):
            dk=dot(ds[c:c+ch],qm[...])
            dv=dot(p[0,0,base+c:base+c+ch],dm[:R])+dot(p[0,1,base+c:base+c+ch],dm[R:])
            if i<n-1:
                dkf[i,c:c+ch]=dk.astype(BF); dvf[i,c:c+ch]=dv.astype(BF)
            else:
                dks[c:c+ch]=dk.astype(BF); dvs[c:c+ch]=dv.astype(BF)
        base+=m
    for h in range(2):
        wide=jnp.concatenate([nacc[h],jnp.zeros((SPAN,SPAN),F32)],axis=1)
        rolled=pltpu.roll(wide,0,1,stride=1,stride_axis=0)
        t[0,h:h+1]=jnp.sum(rolled,axis=0,keepdims=True)
    tick(2)

def attend_back_call(q,kf,vf,ks,vs,layq,layf,lays,o,do,p,l,parts=()):
    n,R,D=q.shape; L=kf.shape[1]; S=ks.shape[0]; H=p.shape[0]*2; E=D//H; W=2*E
    KT=(n-1)*L+S
    full=lambda a: pl.BlockSpec(a.shape,lambda j:(0,)*a.ndim)
    rows=lambda: pl.BlockSpec((n,R,W),lambda j:(0,0,j))
    kb=lambda: pl.BlockSpec((n-1,L,W),lambda j:(0,0,j))
    sb=lambda: pl.BlockSpec((S,W),lambda j:(0,j))
    return pl.pallas_call(functools.partial(attend_back,n,L,S,R,E,H//2,bool(parts)),
      grid=(H//2,),
      in_specs=[rows(),kb(),kb(),sb(),sb(),full(layq),full(layf),full(lays),rows(),rows(),
        pl.BlockSpec((1,2,KT,R),lambda j:(j,0,0,0)),pl.BlockSpec((n,1,2,R),lambda j:(0,j,0,0))]+[pl.BlockSpec(memory_space=pl.ANY)]*len(parts),
      out_specs=[rows(),kb(),kb(),sb(),sb(),pl.BlockSpec((1,2,2*SPAN),lambda j:(j,0,0))]+[pl.BlockSpec(s.shape[4:],lambda j:(0,0)) for s in parts],
      out_shape=[jax.ShapeDtypeStruct((n,R,D),BF),jax.ShapeDtypeStruct(kf.shape,BF),jax.ShapeDtypeStruct(kf.shape,BF),
        jax.ShapeDtypeStruct(ks.shape,BF),jax.ShapeDtypeStruct(ks.shape,BF),jax.ShapeDtypeStruct((H//2,2,2*SPAN),F32)]
        +[jax.ShapeDtypeStruct(s.shape[4:],F32) for s in parts],
      scratch_shapes=[pltpu.VMEM((SPAN+E,KT),BF),pltpu.VMEM((L,2*W),BF),pltpu.VMEM((2*W,R),BF),pltpu.VMEM((L,2*R),BF),
        pltpu.VMEM((n,R,SPAN),BF),pltpu.VMEM((2,SPAN,SPAN),F32),pltpu.VMEM((2*R,W),BF),pltpu.VMEM((2*R,W),BF)]
        +sum((sum_scratch(s.shape[4],s.shape[5]//k) for s,k in zip(parts,(2,2,1)) for _ in range(k)),[])
        +([pltpu.SemaphoreType.DMA((5*SUM_COPIES,))]*2+[pltpu.SemaphoreType.DMA((5,))] if parts else []),
      compiler_params=pltpu.CompilerParams(vmem_limit_bytes=58*2**20,dimension_semantics=("arbitrary",),**(dict(collective_id=3,has_side_effects=True) if parts else {})),
      name="attend_back",
    )(q,kf,vf,ks,vs,layq,layf,lays,o,do,p,l,*parts)


MESH = pl.DeviceIdType.MESH


class Place:
    def __init__(self):
        dp = lax.axis_index("dp")
        self.x = lax.axis_index("blk")
        self.z, self.y, self.c = dp // 4, (dp // 2) % 2, dp % 2
        self.y1, self.x1 = (self.y + 1 - self.c) % 2, (self.x + self.c) % 2
        self.y2, self.x2 = (self.y + self.c) % 2, (self.x + 1 - self.c) % 2

    def device(self, z, y, c, x):
        return ((z * 2 + y) * 2 + c, x)

    def along_z(self, d):
        return self.device((self.z + d) % 4, self.y, self.c, self.x)

    def along_x(self):
        return self.device(self.z, self.y, self.c, 1 - self.x)

    def along_y(self):
        return self.device(self.z, 1 - self.y, self.c, self.x)

    def first(self):
        return self.device(self.z, self.y1, self.c, self.x1)

    def second(self):
        return self.device(self.z, self.y2, self.c, self.x2)

    def core(self):
        return self.device(self.z, self.y, 1 - self.c, self.x)

    def greet(self):
        barrier = pltpu.get_barrier_semaphore()
        partners = [self.along_z(d) for d in (1, 2, 3)] + [self.first(), self.second(), self.core()]
        for partner in partners:
            pl.semaphore_signal(barrier, inc=1, device_id=partner, device_id_type=MESH)
        pl.semaphore_wait(barrier, len(partners))


def remote(src, dst, sems, k, device):
    return pltpu.make_async_remote_copy(
        src_ref=src, dst_ref=dst, send_sem=sems[0].at[k], recv_sem=sems[1].at[k], device_id=device, device_id_type=MESH
    )


GATHER_COPIES = 10


def gather_stages(at, shard, whole, sems, local, base, cols=None):
    z, y, c, x = at.z, at.y, at.c, at.x
    cols = pl.ds(0, shard.shape[1]) if cols is None else cols
    shard = shard.at[:, cols]
    own = whole.at[z, y, c, x, :, cols]

    def group(yy, xx):
        return whole.at[:, yy, c, xx, :, cols]

    def copy(k):
        if k < 3:
            return remote(shard, own, sems, base + k, at.along_z(k + 1))
        view, device = {
            3: (group(y, x), at.first()),
            4: (group(y, x), at.second()),
            5: (group(y, x), at.core()),
            6: (group(at.y1, at.x1), at.second()),
            7: (group(at.y1, at.x1), at.core()),
            8: (group(at.y2, at.x2), at.core()),
            9: (group(1 - y, 1 - x), at.core()),
        }[k]
        return remote(view, view, sems, base + k, device)

    keep = pltpu.make_async_copy(shard, own, local)

    def one():
        keep.start()
        for k in range(3):
            copy(k).start()

    def two():
        keep.wait()
        for k in range(3):
            copy(k).wait_recv()
        for k in (3, 4, 5):
            copy(k).start()

    def three():
        copy(3).wait_recv()
        for k in (6, 7):
            copy(k).start()

    def four():
        copy(4).wait_recv()
        copy(8).start()
        copy(6).wait_recv()
        copy(9).start()

    def five():
        for k in (5, 7, 8, 9):
            copy(k).wait_recv()
        for k in range(10):
            copy(k).wait_send()

    return [one, two, three, four, five]


def start_kernel(count, tok_long, tok_short, *refs):
    shards, (xf, xs), wholes = refs[:count], refs[count : count + 2], refs[count + 2 : 2 * count + 2]
    send, recv, local = refs[2 * count + 2 :]
    at = Place()
    at.greet()
    sems, spare = (send, recv), GATHER_COPIES * count
    chains = [gather_stages(at, s, w, sems, local.at[i], GATHER_COPIES * i) for i, (s, w) in enumerate(zip(shards, wholes))]
    rows = tok_long.shape[1]
    long = remote(tok_long, xf.at[:, rows:], sems, spare, at.along_x())
    short = remote(tok_short, xs, sems, spare + 1, at.along_x())
    keep_long = pltpu.make_async_copy(tok_long, xf.at[:, :rows], local.at[count])
    keep_short = pltpu.make_async_copy(tok_short, xs, local.at[count + 1])

    def tokens_start():
        long.start()
        keep_long.start()

        @pl.when(at.x == 0)
        def _():
            short.start()
            keep_short.start()

    plan = spread(chains, range(count), (0, 1, 2, 3, 100), 200)
    for tick in sorted(plan):
        for stage in plan[tick]:
            stage()
        if tick == 0:
            tokens_start()
    long.wait()
    keep_long.wait()

    @pl.when(at.x == 0)
    def _():
        short.wait_send()
        keep_short.wait()

    @pl.when(at.x == 1)
    def _():
        short.wait_recv()


def start_call(tok_long, tok_short, shards):
    count = len(shards)
    n, rows, width = tok_long.shape
    outs = [jax.ShapeDtypeStruct((n, 2 * rows, width), BF), jax.ShapeDtypeStruct(tok_short.shape, BF)]
    outs += [jax.ShapeDtypeStruct((4, 2, 2, 2) + s.shape, s.dtype) for s in shards]
    anywhere = pl.BlockSpec(memory_space=pl.ANY)
    copies = GATHER_COPIES * count + 2
    return pl.pallas_call(
        functools.partial(start_kernel, count),
        in_specs=[anywhere] * (count + 2),
        out_specs=[anywhere] * (count + 2),
        out_shape=outs,
        scratch_shapes=[pltpu.SemaphoreType.DMA((copies,)), pltpu.SemaphoreType.DMA((copies,)), pltpu.SemaphoreType.DMA((count + 2,))],
        compiler_params=pltpu.CompilerParams(collective_id=0, has_side_effects=True),
        name="gather_first",
    )(tok_long, tok_short, *shards)


SUM_COPIES = 7


def sum_scratch(rows, columns):
    slab = (rows, columns)
    return [pltpu.VMEM((4, 2, 2) + slab, BF)] * 2 + [pltpu.VMEM((4,) + slab, BF)] * 3 + [pltpu.VMEM((3,) + slab, BF)]


def sum_stages(at, part, total, held, got_core, got_diag, got_one, got_two, got_z, sems, local, base, cols=None):
    z, y, c, x = at.z, at.y, at.c, at.x
    cols = pl.ds(0, total.shape[1]) if cols is None else cols

    def copy(k):
        if k > 3:
            d = k - 3
            return remote(held.at[(z + d) % 4, y, x], got_z.at[d - 1], sems, base + k, at.along_z(d))
        src, dst, device = [
            (part.at[:, :, 1 - c, :, :, cols], got_core, at.core()),
            (held.at[:, 1 - y, 1 - x], got_diag, at.second()),
            (held.at[:, at.y2, at.x2], got_two, at.second()),
            (held.at[:, at.y1, at.x1], got_one, at.first()),
        ][k]
        return remote(src, dst, sems, base + k, device)

    keep = pltpu.make_async_copy(part.at[:, :, c, :, :, cols], held, local)

    def one():
        copy(0).start()
        keep.start()

    def two():
        keep.wait()
        copy(0).wait_recv()

        def add(i, _):
            held[i] = (held[i].astype(F32) + got_core[i].astype(F32)).astype(BF)
            return 0

        lax.fori_loop(0, 4, add, 0)
        copy(1).start()
        copy(2).start()

    def three():
        copy(1).wait_recv()
        held[:, at.y1, at.x1] = (held[:, at.y1, at.x1].astype(F32) + got_diag[...].astype(F32)).astype(BF)
        copy(3).start()

    def four():
        copy(2).wait_recv()
        copy(3).wait_recv()
        mine = held[:, y, x].astype(F32) + got_one[...].astype(F32) + got_two[...].astype(F32)
        held[:, y, x] = mine.astype(BF)
        for k in (4, 5, 6):
            copy(k).start()

    def five():
        out = held[z, y, x].astype(F32)
        for d in (1, 2, 3):
            copy(3 + d).wait_recv()
            out = out + got_z[d - 1].astype(F32)
        total[:, cols] = out
        for k in range(7):
            copy(k).wait_send()

    return [one, two, three, four, five]


def small_stages(at, part, total, held, got, sems, base):
    def copy(k):
        device = [at.core, at.along_y, at.along_x][k]() if k < 3 else at.along_z(k - 2)
        return remote(held.at[min(k, 3)], got.at[k], sems, base + k, device)

    def one():
        held[0] = part[...]
        copy(0).start()

    def add(k):
        def run():
            copy(k).wait_recv()
            held[k + 1] = held[k] + got[k]
            for following in (k + 1,) if k < 2 else (3, 4, 5):
                copy(following).start()

        return run

    def five():
        parts = [held[3]]
        for d in (1, 2, 3):
            copy(2 + d).wait_recv()
            parts.append(got[2 + d])
        out = jnp.zeros_like(parts[0])
        for spot in range(4):
            for d in range(4):
                out = out + jnp.where((at.z - d + 4) % 4 == spot, parts[d], 0.0)
        total[...] = out
        for k in range(6):
            copy(k).wait_send()

    return [one, add(0), add(1), add(2), five]


def sum_kernel(count, *refs):
    parts, small_part = refs[:count], refs[count]
    totals, small_total = refs[count + 1 : 2 * count + 1], refs[2 * count + 1]
    scratch = refs[2 * count + 2 :]
    small_held, small_got, send, recv, local = scratch[-5:]
    at = Place()
    at.greet()
    sems = (send, recv)
    chains = [
        sum_stages(at, parts[i], totals[i], *scratch[6 * i : 6 * i + 6], sems, local.at[i], SUM_COPIES * i)
        for i in range(count)
    ]
    chains.append(small_stages(at, small_part, small_total, small_held, small_got, sems, SUM_COPIES * count))
    for turn in range(count + 5):
        for i in range(count + 1):
            if 0 <= turn - i < 5:
                chains[i][turn - i]()


def sum_call(parts, small):
    count = len(parts)
    scratch = sum((sum_scratch(*p.shape[4:]) for p in parts), [])
    scratch += [pltpu.VMEM((4,) + small.shape, F32), pltpu.VMEM((6,) + small.shape, F32)]
    copies = SUM_COPIES * count + 6
    scratch += [pltpu.SemaphoreType.DMA((copies,)), pltpu.SemaphoreType.DMA((copies,)), pltpu.SemaphoreType.DMA((count,))]
    anywhere = pl.BlockSpec(memory_space=pl.ANY)
    vmem = pl.BlockSpec(memory_space=pltpu.VMEM)
    return pl.pallas_call(
        functools.partial(sum_kernel, count),
        in_specs=[anywhere] * count + [vmem],
        out_specs=[vmem] * (count + 1),
        out_shape=[jax.ShapeDtypeStruct(p.shape[4:], F32) for p in parts] + [jax.ShapeDtypeStruct(small.shape, F32)],
        scratch_shapes=scratch,
        compiler_params=pltpu.CompilerParams(collective_id=1, has_side_effects=True, vmem_limit_bytes=56 * 2**20),
        name="sum_gradients",
    )(*parts, small)


GATHER_BEGIN, GATHER_LAG = (0, 1, 5, 9, 13), (0, 3, 5, 7, 100)
SUM_BEGIN, SUM_LAG = (1, 5, 9, 13, 16), (-100, 0, 2, 4, 7)


def spread(chains, begins, lags, ticks):
    plan = {}
    for i, (begin, stages) in enumerate(zip(begins, chains)):
        for lag, stage in zip(lags, stages):
            plan.setdefault(min(max(begin + lag, 0), ticks), []).append((begin + lag, -i, stage))
    return {tick: [stage for _, _, stage in sorted(group, key=lambda e: e[:2])] for tick, group in plan.items()}


def halves(width):
    return [pl.ds(0, width // 2), pl.ds(width // 2, width // 2)]


def ticker(plan, steps, at):
    def tick(u):
        for t in sorted(plan):
            if t == 2 * steps and u == 2 or t < 2 * steps and t % 2 == u:

                @pl.when(pl.program_id(0) == min(t // 2, steps - 1))
                def _(t=t):
                    if t == 0:
                        at.greet()
                    for stage in plan[t]:
                        stage()

    return tick


def gather_plan(shards, wholes, sems, local):
    at = Place()
    chains = []
    for shard, whole, parts in zip(shards, wholes, (1, 2, 2)):
        for cols in [None] if parts == 1 else halves(shard.shape[1]):
            chains.append(gather_stages(at, shard, whole, sems, local.at[len(chains)], GATHER_COPIES * len(chains), cols))
    return at, chains


def sum_plan(parts, totals, scratch, sems, local):
    at = Place()
    chains = []
    for part, total, count in zip(parts, totals, (2, 2, 1)):
        for cols in [None] if count == 1 else halves(total.shape[1]):
            i = len(chains)
            chains.append(sum_stages(at, part, total, *scratch[6 * i : 6 * i + 6], sems, local.at[i], SUM_COPIES * i, cols))
    return at, chains


EPSILON = 1e-06
THRESHOLDS = (12, 16, 23, 32, 46, 64, 91)
BOTH = ("dp", "blk")


def bucket_np(relative):
    magnitude = np.abs(relative)
    larger = 8 + sum((magnitude >= limit).astype(np.int64) for limit in THRESHOLDS)
    return np.where(magnitude < 8, magnitude, larger) + 16 * (relative > 0)


def bucket_rows(distance, buckets):
    return (bucket_np(distance)[:, None] == np.arange(buckets)[None, :]).astype(np.float32)


def norm_parts(x, gain):
    back = lax.rsqrt(jnp.mean(x * x, axis=-1, keepdims=True) + EPSILON)
    return (x * back * gain).astype(BF), back


def norm_back(d, x, back, gain):
    a = gain * d
    grad_gain = jnp.sum(d * x * back, axis=0)
    return back * a - x * back**3 * jnp.mean(a * x, axis=-1, keepdims=True), grad_gain


def mm(a, b, dims):
    return lax.dot_general(a, b, (dims, ((), ())), preferred_element_type=F32)


def gather_weights(gain_one, wq, wk, wv, wo, gain_two, wi, wt):
    full = lambda a: lax.all_gather(a, BOTH, axis=0, tiled=True)
    packed = full(jnp.concatenate([wq, wk, wv, wo, wi], axis=1))
    width = wq.shape[1]
    gains = full(jnp.stack([gain_one, gain_two], axis=1))
    return packed[:, : 3 * width], packed[:, 3 * width : 4 * width], packed[:, 4 * width :], full(wt), gains[:, 0], gains[:, 1]


def scatter_sums(dqkv, dwo, dwi, dwt, dg1, dg2):
    take = lambda a: lax.psum_scatter(a, BOTH, scatter_dimension=0, tiled=True)
    width = dwo.shape[1]
    packed = take(jnp.concatenate([dqkv, dwo, dwi], axis=1).astype(BF)).astype(F32)
    gains = take(jnp.stack([dg1, dg2], axis=1))
    parts = [packed[:, i * width : (i + 1) * width] for i in range(4)]
    return parts, packed[:, 4 * width :], take(dwt.astype(BF)).astype(F32), gains[:, 0], gains[:, 1]


def on_device(tokens, layout, lengths, gain_one, wq, wk, wv, wo, gain_two, wi, wt, table, grad_out):
    n, R, D = tokens.shape
    H = table.shape[1]
    G = lax.axis_size("blk")
    me = lax.axis_index("blk")
    L = layout.shape[1]
    S = L // 8
    order = jnp.argsort(-lengths, stable=True)
    place = jnp.argsort(order)
    tok = tokens[order]
    gout = grad_out[order]
    lay = layout[order]
    lens = lengths[order]

    def from_step(x, s):
        return lax.ppermute(x, "blk", [(i, (i - s) % G) for i in range(G)])

    near = G == 2 and lax.axis_size("dp") == 16
    first = tok[-1, :S]
    columns = lambda a, count: jnp.pad(a, ((0, 0), (0, count - a.shape[1])))
    if near:
        gains = columns(jnp.stack([gain_one, gain_two], axis=1), 128)
        xf, xs, *firsts = start_call(tok[:-1], first, [gains, wq, wk, wv])
        rows_of = lambda a: a.reshape(-1, a.shape[-1])
        gains, wq_all, wk_all, wv_all = [rows_of(a) for a in firsts]
        g1, g2 = gains[:, 0], gains[:, 1]
    else:
        pieces = [tok[:-1]] + [from_step(tok[:-1], s) for s in range(1, G)]
        xf = jnp.concatenate(pieces, axis=1)
        xs = jnp.where(me == 0, first, sum(lax.ppermute(first, "blk", [(0, i)]) for i in range(1, G)))
        wqkv, wo_all, wi_all, wt_all, g1, g2 = gather_weights(gain_one, wq, wk, wv, wo, gain_two, wi, wt)
        wq_all, wk_all, wv_all = [wqkv[:, i * D : (i + 1) * D] for i in range(3)]
    lay_turned = jnp.roll(lay, -me * R, axis=1)
    layq = lay_turned[:, None, :R]
    layf = lay_turned[:-1, None, :]
    lays = lay[-1:, :S]
    spots = (jnp.arange(L) + me * R) % L
    mask = jnp.where(spots[None, :, None] < lens[:-1, None, None], 0.0, -1e30).astype(F32)

    g1 = g1.astype(F32)
    g2 = g2.astype(F32)
    hidden = tok.reshape(n * R, D).astype(F32)
    normed, r1 = norm_parts(hidden, g1)
    xkeys = jnp.concatenate([xf.reshape((n - 1) * L, D), xs], axis=0)
    nkeys, _ = norm_parts(xkeys.astype(F32), g1)
    q = (mm(normed, wq_all, ((1,), (0,))).astype(BF) * jnp.asarray(0.125, BF)).reshape(n, R, D)
    k = mm(nkeys, wk_all, ((1,), (0,))).astype(BF)
    v = mm(nkeys, wv_all, ((1,), (0,))).astype(BF)
    cut = (n - 1) * L
    kf, ks = k[:cut].reshape(n - 1, L, D), k[cut:]
    vf, vs = v[:cut].reshape(n - 1, L, D), v[cut:]
    lane = np.arange(2 * SPAN)
    turned = np.where(lane >= SPAN, lane - 2 * SPAN, lane)
    urow = mm(table, bucket_rows(-turned, table.shape[0]).astype(BF), ((0,), (1,))).reshape(H // 2, 2, 2 * SPAN)
    o, p, l, *rest = attend_call(q, kf, vf, ks, vs, layq, layf, lays, mask, urow, [wo, wi, wt] if near else [])
    if near:
        wo_all, wi_all, wt_all = [rows_of(a) for a in rest]

    attended = o.reshape(n * R, D)
    resid = hidden + mm(attended, wo_all, ((1,), (0,)))
    normed_two, r2 = norm_parts(resid, g2)
    pre = mm(normed_two, wi_all, ((1,), (0,)))
    act, act_back = jax.vjp(lambda x: jax.nn.gelu(x, approximate=False), pre)
    act = act.astype(BF)
    mixed = (resid + mm(act, wt_all, ((1,), (0,)))).astype(BF)
    up = gout.reshape(n * R, D)
    dwt = mm(act, up, ((0,), (0,)))
    (dpre,) = act_back(mm(up, wt_all, ((1,), (1,))))
    dpre = dpre.astype(BF)
    dwi = mm(normed_two, dpre, ((0,), (0,)))
    dn2 = mm(dpre, wi_all, ((1,), (1,)))
    dresid, dg2 = norm_back(dn2, resid, r2, g2)
    dresid = dresid + up.astype(F32)
    low = dresid.astype(BF)
    dwo = mm(attended, low, ((0,), (0,)))
    datt = mm(low, wo_all, ((1,), (1,))).astype(BF).reshape(n, R, D)

    slabs = lambda a: a.astype(BF).reshape(4, 2, 2, 2, -1, a.shape[-1])
    parts = [slabs(dwt), slabs(dwi), slabs(dwo)] if near else []
    dq, dkf, dvf, dks, dvs, t, *rest = attend_back_call(q, kf, vf, ks, vs, layq, layf, lays, o, datt, p, l, parts)
    dtable = jnp.einsum(
        "hj,jb->bh", t.reshape(H, 2 * SPAN), bucket_rows(SPAN - 1 - lane, table.shape[0]), precision=lax.Precision.HIGHEST
    )
    dq = dq.reshape(n * R, D)
    dk = jnp.concatenate([dkf.reshape(cut, D), dks], axis=0)
    dv = jnp.concatenate([dvf.reshape(cut, D), dvs], axis=0)
    dnk = mm(dk, wk_all, ((1,), (1,))) + mm(dv, wv_all, ((1,), (1,)))
    dnf = dnk[:cut].reshape(n - 1, L, D)
    dns = dnk[cut:].astype(BF)
    far = sum(
        lax.ppermute(dnf[:, s * R : (s + 1) * R].astype(BF), "blk", [(i, (i + s) % G) for i in range(G)]).astype(F32)
        for s in range(1, G)
    )
    back = jnp.where(
        me == 0, dnk[cut:] + sum(lax.ppermute(dns, "blk", [(i, 0)]).astype(F32) for i in range(1, G)), 0.0
    )
    extra = jnp.concatenate([dnf[:, :R] + far, jnp.pad(back, ((0, R - S), (0, 0)))[None]], axis=0).reshape(n * R, D)
    dn1 = mm(dq, wq_all, ((1,), (1,))) + extra
    dwq = mm(normed, dq, ((0,), (0,)))
    dwk = mm(nkeys, dk, ((0,), (0,)))
    dwv = mm(nkeys, dv, ((0,), (0,)))
    dx, dg1 = norm_back(dn1, hidden, r1, g1)
    gtok = (dresid + dx).astype(BF)
    if near:
        gwt, gwi, gwo = rest
        small = jnp.concatenate([dg1, dg2, dtable.reshape(-1)]).reshape(-1, 128)
        small = jnp.pad(small, ((0, -small.shape[0] % 8), (0, 0)))
        *parts, small = sum_call([slabs(dwq), slabs(dwk), slabs(dwv)], small)
        parts.append(gwo)
        small = small.reshape(-1)
        mine = (lax.axis_index("dp") * G + me) * (D // 32)
        gg1, gg2 = [lax.dynamic_slice_in_dim(small, mine + i * D, D // 32) for i in range(2)]
        dtable = small[2 * D : 2 * D + table.size].reshape(table.shape)
    else:
        parts, gwi, gwt, gg1, gg2 = scatter_sums(jnp.concatenate([dwq, dwk, dwv], axis=1), dwo, dwi, dwt, dg1, dg2)
        dtable = lax.psum(dtable, BOTH)
    return (
        mixed.reshape(n, R, D)[place],
        gtok.reshape(n, R, D)[place],
        gg1,
        parts[0],
        parts[1],
        parts[2],
        parts[3],
        gg2,
        gwi,
        gwt,
        dtable,
    )


def solution(mesh):
    rows = P(BOTH, None)
    items = P("dp", "blk", None)
    return jax.shard_map(
        on_device,
        mesh=mesh,
        in_specs=(items, P("dp", None), P("dp"), P(BOTH), rows, rows, rows, rows, P(BOTH), rows, rows, P(), items),
        out_specs=(items, items, P(BOTH), rows, rows, rows, rows, P(BOTH), rows, rows, P()),
        check_vma=False,
    )
```

```python
import functools
import math

import jax
import jax.numpy as jnp
import numpy as np
from jax import lax
from jax.experimental import pallas as pl
from jax.experimental.pallas import tpu as pltpu
from jax.sharding import PartitionSpec as P

F32=jnp.float32; BF=jnp.bfloat16
SPAN=256
CH=256
def dot(a,b): return lax.dot_general(a,b,(((1,),(0,)),((),())),preferred_element_type=F32)
def eye_of(row, width, reverse):
    spots=lax.broadcasted_iota(jnp.int32,(width,row.shape[1]),0)
    if reverse: spots=width-1-spots
    return (spots==row).astype(F32).astype(BF)

def attend(n,L,S,R,E,steps,far,*refs):
    q,kf,vf,ks,vs,layq,layf,lays,mask,u=refs[:10]
    if far:
        shards=refs[10:13]; o,p,l=refs[13:16]; wholes=refs[16:19]
        kcat,qcat,vt,s_ref,ohq,send,recv,local=refs[19:]
        at,chains=gather_plan(shards,wholes,(send,recv),local)
        tick=ticker(spread(chains,GATHER_BEGIN,GATHER_LAG,2*steps),steps,at)
    else:
        o,p,l,kcat,qcat,vt,s_ref,ohq=refs[10:]
        tick=lambda u:None
    W=2*E
    spans=[L]*(n-1)+[S]
    @pl.when(pl.program_id(0)==0)
    def _():
        base=0
        for i,m in enumerate(spans):
            row=layf[i] if i<n-1 else lays[...]
            kcat[base:base+m,W:]=jnp.transpose(eye_of(row,SPAN,False).astype(F32)).astype(BF)
            ohq[i]=eye_of(layq[i],SPAN,False)
            base+=m
        vt[:,E:]=jnp.ones((2,vt.shape[1]-E,vt.shape[2]),BF)
    pair=pl.program_id(0)
    base=0
    for i,m in enumerate(spans):
        ch=min(CH,m)
        kcat[base:base+m,:W]=kf[i] if i<n-1 else ks[...]
        v=vf[i] if i<n-1 else vs[...]
        vtr=jnp.transpose(v.astype(F32)).astype(BF)
        vt[0,:E,:m]=vtr[:E]
        vt[1,:E,:m]=vtr[E:]
        qt=jnp.transpose(q[i].astype(F32)).astype(BF)
        outs=[]
        for h in range(2):
            if i==0: tick(h)
            urow=u[0,h:h+1,:]
            toep=pltpu.roll(jnp.broadcast_to(urow,(SPAN,2*SPAN)),0,1,stride=1,stride_axis=0)[:,:SPAN].astype(BF)
            qcat[h*E:(h+1)*E]=qt[h*E:(h+1)*E]
            qcat[(1-h)*E:(2-h)*E]=jnp.zeros((E,R),BF)
            qcat[W:]=dot(toep,ohq[i]).astype(BF)
            m8=jnp.full((8,R),-jnp.inf,F32)
            for c in range(0,m,ch):
                s=dot(kcat[base+c:base+c+ch],qcat[...])
                if 0<i<n-1: s=s+mask[i,c:c+ch,:]
                s_ref[c:c+ch]=s
                m8=jnp.maximum(m8,jnp.max(s.reshape(ch//8,8,R),axis=0))
            top=jnp.max(m8,axis=0,keepdims=True)
            for c in range(0,m,ch):
                p[0,h,base+c:base+c+ch]=jnp.exp(s_ref[c:c+ch]-top).astype(BF)
            full=dot(vt[h,:,:m],p[0,h,base:base+m])
            total=full[E:E+1]
            l[i,0,h:h+1]=total
            outs.append(full[:E]/total)
        o[i]=jnp.transpose(jnp.concatenate(outs,axis=0)).astype(BF)
        base+=m
    tick(2)

def attend_call(q,kf,vf,ks,vs,layq,layf,lays,mask,u,shards=()):
    n,R,D=q.shape; L=kf.shape[1]; S=ks.shape[0]; H=u.shape[0]*2; E=D//H; W=2*E
    KT=(n-1)*L+S
    full=lambda a: pl.BlockSpec(a.shape,lambda j:(0,)*a.ndim)
    return pl.pallas_call(functools.partial(attend,n,L,S,R,E,H//2,bool(shards)),
      grid=(H//2,),
      in_specs=[pl.BlockSpec((n,R,W),lambda j:(0,0,j)),
        pl.BlockSpec((n-1,L,W),lambda j:(0,0,j)),pl.BlockSpec((n-1,L,W),lambda j:(0,0,j)),
        pl.BlockSpec((S,W),lambda j:(0,j)),pl.BlockSpec((S,W),lambda j:(0,j)),
        full(layq),full(layf),full(lays),full(mask),pl.BlockSpec((1,2,2*SPAN),lambda j:(j,0,0))]+[pl.BlockSpec(memory_space=pl.ANY)]*len(shards),
      out_specs=[pl.BlockSpec((n,R,W),lambda j:(0,0,j)),
        pl.BlockSpec((1,2,KT,R),lambda j:(j,0,0,0)),
        pl.BlockSpec((n,1,2,R),lambda j:(0,j,0,0))]+[pl.BlockSpec(memory_space=pl.ANY)]*len(shards),
      out_shape=[jax.ShapeDtypeStruct((n,R,D),BF),jax.ShapeDtypeStruct((H//2,2,KT,R),BF),jax.ShapeDtypeStruct((n,H//2,2,R),F32)]
        +[jax.ShapeDtypeStruct((4,2,2,2)+s.shape,BF) for s in shards],
      scratch_shapes=[pltpu.VMEM((KT,W+SPAN),BF),pltpu.VMEM((W+SPAN,R),BF),pltpu.VMEM((2,E+16,L),BF),pltpu.VMEM((L,R),F32),pltpu.VMEM((n,SPAN,R),BF)]
        +([pltpu.SemaphoreType.DMA((5*GATHER_COPIES,))]*2+[pltpu.SemaphoreType.DMA((5,))] if shards else []),
      compiler_params=pltpu.CompilerParams(vmem_limit_bytes=56*2**20,dimension_semantics=("arbitrary",),**(dict(collective_id=2,has_side_effects=True) if shards else {})),
      name="attend",
    )(q,kf,vf,ks,vs,layq,layf,lays,mask,u,*shards)

def attend_back(n,L,S,R,E,steps,far,*refs):
    q,kf,vf,ks,vs,layq,layf,lays,o,do,p,l=refs[:12]
    if far:
        parts=refs[12:15]; dq,dkf,dvf,dks,dvs,t=refs[15:21]; totals=refs[21:24]
        kq,vaug,rhs,ds,ohq,nacc,qm,dm=refs[24:32]; send,recv,local=refs[-3:]
        at,chains=sum_plan(parts,totals,refs[32:-3],(send,recv),local)
        tick=ticker(spread(chains,SUM_BEGIN,SUM_LAG,2*steps),steps,at)
    else:
        dq,dkf,dvf,dks,dvs,t,kq,vaug,rhs,ds,ohq,nacc,qm,dm=refs[12:]
        tick=lambda u:None
    W=2*E
    spans=[L]*(n-1)+[S]
    @pl.when(pl.program_id(0)==0)
    def _():
        base=0
        for i,m in enumerate(spans):
            row=layf[i] if i<n-1 else lays[...]
            kq[:SPAN,base:base+m]=eye_of(row,SPAN,True)
            ohq[i]=jnp.transpose(eye_of(layq[i],SPAN,False).astype(F32)).astype(BF)
            base+=m
        vaug[:,W:]=(lax.broadcasted_iota(jnp.int32,(vaug.shape[0],W),1)<2).astype(F32).astype(BF)
        rhs[...]=jnp.zeros_like(rhs)
    nacc[...]=jnp.zeros_like(nacc)
    base=0
    lane=lax.broadcasted_iota(jnp.int32,(R,W),1)
    for i,m in enumerate(spans):
        ch=min(CH,m)
        kk=kf[i] if i<n-1 else ks[...]
        vaug[:m,:W]=vf[i] if i<n-1 else vs[...]
        kt=jnp.transpose(kk.astype(F32)).astype(BF)
        dot_=jnp.transpose(do[i].astype(F32))
        ot=jnp.transpose(o[i].astype(F32))
        scaled=[];
        for h in range(2):
            inv=1.0/l[i,0,h:h+1]
            scaled.append((dot_[h*E:(h+1)*E]*inv).astype(BF))
        sc=jnp.concatenate(scaled,axis=0)
        don=jnp.transpose(sc.astype(F32)).astype(BF)
        qq=q[i]
        zero=jnp.zeros((R,W),BF)
        for h in range(2):
            mine=(lane<E) if h==0 else (lane>=E)
            qm[h*R:(h+1)*R]=jnp.where(mine,qq,zero)
            dm[h*R:(h+1)*R]=jnp.where(mine,don,zero)
        dqs=[]
        for h in range(2):
            if i==0: tick(h)
            rhs[h*E:(h+1)*E]=scaled[h]
            rhs[(1-h)*E:(2-h)*E]=jnp.zeros((E,R),BF)
            delta=jnp.sum(scaled[h].astype(F32)*ot[h*E:(h+1)*E],axis=0,keepdims=True)
            hi=delta.astype(BF).astype(F32)
            lo=delta-hi
            spot=lax.broadcasted_iota(jnp.int32,(16,R),0)
            rhs[W:W+16]=jnp.where(spot==0,-hi,jnp.where(spot==1,-lo,0.0)).astype(BF)
            for c in range(0,m,ch):
                g=dot(vaug[c:c+ch],rhs[...])
                ds[c:c+ch,h*R:(h+1)*R]=(p[0,h,base+c:base+c+ch].astype(F32)*g).astype(BF)
            kq[SPAN:,base:base+m]=kt[h*E:(h+1)*E]
            both=dot(kq[:,base:base+m],ds[:m,h*R:(h+1)*R])
            dqs.append(both[SPAN:]*0.125)
            nacc[h]+=dot(both[:SPAN].astype(BF),ohq[i])
        dq[i]=jnp.transpose(jnp.concatenate(dqs,axis=0)).astype(BF)
        for c in range(0,m,ch):
            dk=dot(ds[c:c+ch],qm[...])
            dv=dot(p[0,0,base+c:base+c+ch],dm[:R])+dot(p[0,1,base+c:base+c+ch],dm[R:])
            if i<n-1:
                dkf[i,c:c+ch]=dk.astype(BF); dvf[i,c:c+ch]=dv.astype(BF)
            else:
                dks[c:c+ch]=dk.astype(BF); dvs[c:c+ch]=dv.astype(BF)
        base+=m
    for h in range(2):
        wide=jnp.concatenate([nacc[h],jnp.zeros((SPAN,SPAN),F32)],axis=1)
        rolled=pltpu.roll(wide,0,1,stride=1,stride_axis=0)
        t[0,h:h+1]=jnp.sum(rolled,axis=0,keepdims=True)
    tick(2)

def attend_back_call(q,kf,vf,ks,vs,layq,layf,lays,o,do,p,l,parts=()):
    n,R,D=q.shape; L=kf.shape[1]; S=ks.shape[0]; H=p.shape[0]*2; E=D//H; W=2*E
    KT=(n-1)*L+S
    full=lambda a: pl.BlockSpec(a.shape,lambda j:(0,)*a.ndim)
    rows=lambda: pl.BlockSpec((n,R,W),lambda j:(0,0,j))
    kb=lambda: pl.BlockSpec((n-1,L,W),lambda j:(0,0,j))
    sb=lambda: pl.BlockSpec((S,W),lambda j:(0,j))
    return pl.pallas_call(functools.partial(attend_back,n,L,S,R,E,H//2,bool(parts)),
      grid=(H//2,),
      in_specs=[rows(),kb(),kb(),sb(),sb(),full(layq),full(layf),full(lays),rows(),rows(),
        pl.BlockSpec((1,2,KT,R),lambda j:(j,0,0,0)),pl.BlockSpec((n,1,2,R),lambda j:(0,j,0,0))]+[pl.BlockSpec(memory_space=pl.ANY)]*len(parts),
      out_specs=[rows(),kb(),kb(),sb(),sb(),pl.BlockSpec((1,2,2*SPAN),lambda j:(j,0,0))]+[pl.BlockSpec(s.shape[4:],lambda j:(0,0)) for s in parts],
      out_shape=[jax.ShapeDtypeStruct((n,R,D),BF),jax.ShapeDtypeStruct(kf.shape,BF),jax.ShapeDtypeStruct(kf.shape,BF),
        jax.ShapeDtypeStruct(ks.shape,BF),jax.ShapeDtypeStruct(ks.shape,BF),jax.ShapeDtypeStruct((H//2,2,2*SPAN),F32)]
        +[jax.ShapeDtypeStruct(s.shape[4:],F32) for s in parts],
      scratch_shapes=[pltpu.VMEM((SPAN+E,KT),BF),pltpu.VMEM((L,2*W),BF),pltpu.VMEM((2*W,R),BF),pltpu.VMEM((L,2*R),BF),
        pltpu.VMEM((n,R,SPAN),BF),pltpu.VMEM((2,SPAN,SPAN),F32),pltpu.VMEM((2*R,W),BF),pltpu.VMEM((2*R,W),BF)]
        +sum((sum_scratch(s.shape[4],s.shape[5]//k) for s,k in zip(parts,(2,2,1)) for _ in range(k)),[])
        +([pltpu.SemaphoreType.DMA((5*SUM_COPIES,))]*2+[pltpu.SemaphoreType.DMA((5,))] if parts else []),
      compiler_params=pltpu.CompilerParams(vmem_limit_bytes=58*2**20,dimension_semantics=("arbitrary",),**(dict(collective_id=3,has_side_effects=True) if parts else {})),
      name="attend_back",
    )(q,kf,vf,ks,vs,layq,layf,lays,o,do,p,l,*parts)


FFB, FFP = 512, 512


MESH = pl.DeviceIdType.MESH


class Place:
    def __init__(self):
        dp = lax.axis_index("dp")
        self.x = lax.axis_index("blk")
        self.z, self.y, self.c = dp // 4, (dp // 2) % 2, dp % 2
        self.y1, self.x1 = (self.y + 1 - self.c) % 2, (self.x + self.c) % 2
        self.y2, self.x2 = (self.y + self.c) % 2, (self.x + 1 - self.c) % 2

    def device(self, z, y, c, x):
        return ((z * 2 + y) * 2 + c, x)

    def along_z(self, d):
        return self.device((self.z + d) % 4, self.y, self.c, self.x)

    def along_x(self):
        return self.device(self.z, self.y, self.c, 1 - self.x)

    def along_y(self):
        return self.device(self.z, 1 - self.y, self.c, self.x)

    def first(self):
        return self.device(self.z, self.y1, self.c, self.x1)

    def second(self):
        return self.device(self.z, self.y2, self.c, self.x2)

    def core(self):
        return self.device(self.z, self.y, 1 - self.c, self.x)

    def greet(self):
        barrier = pltpu.get_barrier_semaphore()
        partners = [self.along_z(d) for d in (1, 2, 3)] + [self.first(), self.second(), self.core()]
        for partner in partners:
            pl.semaphore_signal(barrier, inc=1, device_id=partner, device_id_type=MESH)
        pl.semaphore_wait(barrier, len(partners))


def remote(src, dst, sems, k, device):
    return pltpu.make_async_remote_copy(
        src_ref=src, dst_ref=dst, send_sem=sems[0].at[k], recv_sem=sems[1].at[k], device_id=device, device_id_type=MESH
    )


GATHER_COPIES = 10


def gather_stages(at, shard, whole, sems, local, base, cols=None):
    z, y, c, x = at.z, at.y, at.c, at.x
    cols = pl.ds(0, shard.shape[1]) if cols is None else cols
    shard = shard.at[:, cols]
    own = whole.at[z, y, c, x, :, cols]

    def group(yy, xx):
        return whole.at[:, yy, c, xx, :, cols]

    def copy(k):
        if k < 3:
            return remote(shard, own, sems, base + k, at.along_z(k + 1))
        view, device = {
            3: (group(y, x), at.first()),
            4: (group(y, x), at.second()),
            5: (group(y, x), at.core()),
            6: (group(at.y1, at.x1), at.second()),
            7: (group(at.y1, at.x1), at.core()),
            8: (group(at.y2, at.x2), at.core()),
            9: (group(1 - y, 1 - x), at.core()),
        }[k]
        return remote(view, view, sems, base + k, device)

    keep = pltpu.make_async_copy(shard, own, local)

    def one():
        keep.start()
        for k in range(3):
            copy(k).start()

    def two():
        keep.wait()
        for k in range(3):
            copy(k).wait_recv()
        for k in (3, 4, 5):
            copy(k).start()

    def three():
        copy(3).wait_recv()
        for k in (6, 7):
            copy(k).start()

    def four():
        copy(4).wait_recv()
        copy(8).start()
        copy(6).wait_recv()
        copy(9).start()

    def five():
        for k in (5, 7, 8, 9):
            copy(k).wait_recv()
        for k in range(10):
            copy(k).wait_send()

    return [one, two, three, four, five]


def start_kernel(count, tok_long, tok_short, *refs):
    shards, (xf, xs), wholes = refs[:count], refs[count : count + 2], refs[count + 2 : 2 * count + 2]
    send, recv, local = refs[2 * count + 2 :]
    at = Place()
    at.greet()
    sems, spare = (send, recv), GATHER_COPIES * count
    chains = [gather_stages(at, s, w, sems, local.at[i], GATHER_COPIES * i) for i, (s, w) in enumerate(zip(shards, wholes))]
    rows = tok_long.shape[1]
    long = remote(tok_long, xf.at[:, rows:], sems, spare, at.along_x())
    short = remote(tok_short, xs, sems, spare + 1, at.along_x())
    keep_long = pltpu.make_async_copy(tok_long, xf.at[:, :rows], local.at[count])
    keep_short = pltpu.make_async_copy(tok_short, xs, local.at[count + 1])

    def tokens_start():
        long.start()
        keep_long.start()

        @pl.when(at.x == 0)
        def _():
            short.start()
            keep_short.start()

    plan = spread(chains, range(count), (0, 1, 2, 3, 100), 200)
    for tick in sorted(plan):
        for stage in plan[tick]:
            stage()
        if tick == 0:
            tokens_start()
    long.wait()
    keep_long.wait()

    @pl.when(at.x == 0)
    def _():
        short.wait_send()
        keep_short.wait()

    @pl.when(at.x == 1)
    def _():
        short.wait_recv()


def start_call(tok_long, tok_short, shards):
    count = len(shards)
    n, rows, width = tok_long.shape
    outs = [jax.ShapeDtypeStruct((n, 2 * rows, width), BF), jax.ShapeDtypeStruct(tok_short.shape, BF)]
    outs += [jax.ShapeDtypeStruct((4, 2, 2, 2) + s.shape, s.dtype) for s in shards]
    anywhere = pl.BlockSpec(memory_space=pl.ANY)
    copies = GATHER_COPIES * count + 2
    return pl.pallas_call(
        functools.partial(start_kernel, count),
        in_specs=[anywhere] * (count + 2),
        out_specs=[anywhere] * (count + 2),
        out_shape=outs,
        scratch_shapes=[pltpu.SemaphoreType.DMA((copies,)), pltpu.SemaphoreType.DMA((copies,)), pltpu.SemaphoreType.DMA((count + 2,))],
        compiler_params=pltpu.CompilerParams(collective_id=0, has_side_effects=True),
        name="gather_first",
    )(tok_long, tok_short, *shards)


SUM_COPIES = 7


def sum_scratch(rows, columns):
    slab = (rows, columns)
    return [pltpu.VMEM((4, 2, 2) + slab, BF)] * 2 + [pltpu.VMEM((4,) + slab, BF)] * 3 + [pltpu.VMEM((3,) + slab, BF)]


def sum_stages(at, part, total, held, got_core, got_diag, got_one, got_two, got_z, sems, local, base, cols=None):
    z, y, c, x = at.z, at.y, at.c, at.x
    cols = pl.ds(0, total.shape[1]) if cols is None else cols

    def copy(k):
        if k > 3:
            d = k - 3
            return remote(held.at[(z + d) % 4, y, x], got_z.at[d - 1], sems, base + k, at.along_z(d))
        src, dst, device = [
            (part.at[:, :, 1 - c, :, :, cols], got_core, at.core()),
            (held.at[:, 1 - y, 1 - x], got_diag, at.second()),
            (held.at[:, at.y2, at.x2], got_two, at.second()),
            (held.at[:, at.y1, at.x1], got_one, at.first()),
        ][k]
        return remote(src, dst, sems, base + k, device)

    keep = pltpu.make_async_copy(part.at[:, :, c, :, :, cols], held, local)

    def one():
        copy(0).start()
        keep.start()

    def two():
        keep.wait()
        copy(0).wait_recv()

        def add(i, _):
            held[i] = (held[i].astype(F32) + got_core[i].astype(F32)).astype(BF)
            return 0

        lax.fori_loop(0, 4, add, 0)
        copy(1).start()
        copy(2).start()

    def three():
        copy(1).wait_recv()
        held[:, at.y1, at.x1] = (held[:, at.y1, at.x1].astype(F32) + got_diag[...].astype(F32)).astype(BF)
        copy(3).start()

    def four():
        copy(2).wait_recv()
        copy(3).wait_recv()
        mine = held[:, y, x].astype(F32) + got_one[...].astype(F32) + got_two[...].astype(F32)
        held[:, y, x] = mine.astype(BF)
        for k in (4, 5, 6):
            copy(k).start()

    def five():
        out = held[z, y, x].astype(F32)
        for d in (1, 2, 3):
            copy(3 + d).wait_recv()
            out = out + got_z[d - 1].astype(F32)
        total[:, cols] = out
        for k in range(7):
            copy(k).wait_send()

    return [one, two, three, four, five]


def small_stages(at, part, total, held, got, sems, base):
    def copy(k):
        device = [at.core, at.along_y, at.along_x][k]() if k < 3 else at.along_z(k - 2)
        return remote(held.at[min(k, 3)], got.at[k], sems, base + k, device)

    def one():
        held[0] = part[...]
        copy(0).start()

    def add(k):
        def run():
            copy(k).wait_recv()
            held[k + 1] = held[k] + got[k]
            for following in (k + 1,) if k < 2 else (3, 4, 5):
                copy(following).start()

        return run

    def five():
        parts = [held[3]]
        for d in (1, 2, 3):
            copy(2 + d).wait_recv()
            parts.append(got[2 + d])
        out = jnp.zeros_like(parts[0])
        for spot in range(4):
            for d in range(4):
                out = out + jnp.where((at.z - d + 4) % 4 == spot, parts[d], 0.0)
        total[...] = out
        for k in range(6):
            copy(k).wait_send()

    return [one, add(0), add(1), add(2), five]


def sum_kernel(count, *refs):
    parts, small_part = refs[:count], refs[count]
    totals, small_total = refs[count + 1 : 2 * count + 1], refs[2 * count + 1]
    scratch = refs[2 * count + 2 :]
    small_held, small_got, send, recv, local = scratch[-5:]
    at = Place()
    at.greet()
    sems = (send, recv)
    chains = [
        sum_stages(at, parts[i], totals[i], *scratch[6 * i : 6 * i + 6], sems, local.at[i], SUM_COPIES * i)
        for i in range(count)
    ]
    chains.append(small_stages(at, small_part, small_total, small_held, small_got, sems, SUM_COPIES * count))
    for turn in range(count + 5):
        for i in range(count + 1):
            if 0 <= turn - i < 5:
                chains[i][turn - i]()


def sum_call(parts, small):
    count = len(parts)
    scratch = sum((sum_scratch(*p.shape[4:]) for p in parts), [])
    scratch += [pltpu.VMEM((4,) + small.shape, F32), pltpu.VMEM((6,) + small.shape, F32)]
    copies = SUM_COPIES * count + 6
    scratch += [pltpu.SemaphoreType.DMA((copies,)), pltpu.SemaphoreType.DMA((copies,)), pltpu.SemaphoreType.DMA((count,))]
    anywhere = pl.BlockSpec(memory_space=pl.ANY)
    vmem = pl.BlockSpec(memory_space=pltpu.VMEM)
    return pl.pallas_call(
        functools.partial(sum_kernel, count),
        in_specs=[anywhere] * count + [vmem],
        out_specs=[vmem] * (count + 1),
        out_shape=[jax.ShapeDtypeStruct(p.shape[4:], F32) for p in parts] + [jax.ShapeDtypeStruct(small.shape, F32)],
        scratch_shapes=scratch,
        compiler_params=pltpu.CompilerParams(collective_id=1, has_side_effects=True, vmem_limit_bytes=56 * 2**20),
        name="sum_gradients",
    )(*parts, small)


GATHER_BEGIN, GATHER_LAG = (0, 1, 5, 9, 13), (0, 3, 5, 7, 100)
SUM_BEGIN, SUM_LAG = (1, 5, 9, 13, 16), (-100, 0, 2, 4, 7)


def spread(chains, begins, lags, ticks):
    plan = {}
    for i, (begin, stages) in enumerate(zip(begins, chains)):
        for lag, stage in zip(lags, stages):
            plan.setdefault(min(max(begin + lag, 0), ticks), []).append((begin + lag, -i, stage))
    return {tick: [stage for _, _, stage in sorted(group, key=lambda e: e[:2])] for tick, group in plan.items()}


def halves(width):
    return [pl.ds(0, width // 2), pl.ds(width // 2, width // 2)]


def ticker(plan, steps, at):
    def tick(u):
        for t in sorted(plan):
            if t == 2 * steps and u == 2 or t < 2 * steps and t % 2 == u:

                @pl.when(pl.program_id(0) == min(t // 2, steps - 1))
                def _(t=t):
                    if t == 0:
                        at.greet()
                    for stage in plan[t]:
                        stage()

    return tick


def gather_plan(shards, wholes, sems, local):
    at = Place()
    chains = []
    for shard, whole, parts in zip(shards, wholes, (1, 2, 2)):
        for cols in [None] if parts == 1 else halves(shard.shape[1]):
            chains.append(gather_stages(at, shard, whole, sems, local.at[len(chains)], GATHER_COPIES * len(chains), cols))
    return at, chains


def sum_plan(parts, totals, scratch, sems, local):
    at = Place()
    chains = []
    for part, total, count in zip(parts, totals, (2, 2, 1)):
        for cols in [None] if count == 1 else halves(total.shape[1]):
            i = len(chains)
            chains.append(sum_stages(at, part, total, *scratch[6 * i : 6 * i + 6], sems, local.at[i], SUM_COPIES * i, cols))
    return at, chains


def norm_rows(x):
    return lax.rsqrt(jnp.mean(x * x, axis=1, keepdims=True) + EPSILON)


def dot_nt(a, b):
    return lax.dot_general(a, b, (((1,), (1,)), ((), ())), preferred_element_type=F32)


def flipped(a):
    return jnp.transpose(a.astype(F32)).astype(BF)


def feed_forward(steps, piece, att, tok, up, wo, gain, wi, wt, mixed, dres, datt, dwo, dwi, dwt, dgain, resid, n2, n2t, acc, dn2, low):
    rows, width = tok.shape
    blocks = [pl.ds(i, piece) for i in range(0, rows, piece)]
    step = pl.program_id(0)

    @pl.when(step == 0)
    def _():
        for b in blocks:
            x = tok[b].astype(F32) + dot(att[b], wo[...])
            resid[b] = x
            normed = (x * norm_rows(x) * gain[...]).astype(BF)
            n2[b] = normed
            n2t[:, b] = flipped(normed)
            acc[b] = x
            dn2[b] = jnp.zeros_like(x)

    for i, b in enumerate(blocks):
        pre = dot(n2[b], wi[...])
        dact = dot_nt(up[b], wt[...])
        half = 0.5 + 0.5 * lax.erf(pre * 0.7071067811865476)
        act = (pre * half).astype(BF)
        dpre = (dact * (half + pre * (jnp.exp(-0.5 * pre * pre) * 0.3989422804014327))).astype(BF)
        acc[b] += dot(act, wt[...])
        dn2[b] += dot_nt(dpre, wi[...])
        gi = dot(n2t[:, b], dpre)
        gt = dot(flipped(act), up[b])
        if i == 0:
            wi_sum, wt_sum = gi, gt
        else:
            wi_sum, wt_sum = wi_sum + gi, wt_sum + gt
    dwi[...] = wi_sum.astype(BF)
    dwt[...] = wt_sum.astype(BF)

    @pl.when(step == steps - 1)
    def _():
        total, wsum = None, None
        for b in blocks:
            mixed[b] = acc[b].astype(BF)
            x, d = resid[b], dn2[b]
            back = norm_rows(x)
            a = gain[...] * d
            part = jnp.sum(d * x * back, axis=0, keepdims=True)
            total = part if total is None else total + part
            g = up[b].astype(F32) + back * a - x * (back * back * back) * jnp.mean(a * x, axis=1, keepdims=True)
            dres[b] = g
            g = g.astype(BF)
            datt[b] = dot_nt(g, wo[...]).astype(BF)
            part = dot(flipped(att[b]), g)
            wsum = part if wsum is None else wsum + part
        dgain[...] = total
        dwo[...] = wsum.astype(BF)


def feed_forward_call(att, tok, up, wo, gain, wi, wt):
    rows, width = tok.shape
    hidden = wi.shape[1]
    block = math.gcd(hidden, FFB)
    piece = math.gcd(rows, FFP)
    steps = hidden // block
    whole = lambda a: pl.BlockSpec(a.shape, lambda j: (0, 0))
    act = jax.ShapeDtypeStruct((rows, width), BF)
    return pl.pallas_call(
        functools.partial(feed_forward, steps, piece),
        grid=(steps,),
        in_specs=[whole(att), whole(tok), whole(up), whole(wo), whole(gain)]
        + [pl.BlockSpec((width, block), lambda j: (0, j)), pl.BlockSpec((block, width), lambda j: (j, 0))],
        out_specs=[whole(tok)] * 3 + [whole(wo)]
        + [pl.BlockSpec((width, block), lambda j: (0, j)), pl.BlockSpec((block, width), lambda j: (j, 0)), whole(gain)],
        out_shape=[act, jax.ShapeDtypeStruct((rows, width), F32), act, jax.ShapeDtypeStruct(wo.shape, BF)]
        + [jax.ShapeDtypeStruct(wi.shape, BF), jax.ShapeDtypeStruct(wt.shape, BF), jax.ShapeDtypeStruct(gain.shape, F32)],
        scratch_shapes=[pltpu.VMEM((rows, width), F32), pltpu.VMEM((rows, width), BF), pltpu.VMEM((width, rows), BF)]
        + [pltpu.VMEM((rows, width), F32)] * 2 + [pltpu.VMEM((16, 128), BF)],
        compiler_params=pltpu.CompilerParams(vmem_limit_bytes=60 * 2**20, dimension_semantics=("arbitrary",)),
        name="feed_forward",
    )(att, tok, up, wo, gain, wi, wt)


TURNS_BEFORE = 7


def turn_plan(chains, lags=(0, 1, 2, 3, 4)):
    plan = {}
    for i, stages in enumerate(chains):
        for lag, stage in zip(lags, stages):
            plan.setdefault(i + lag, []).insert(0, stage)
    return plan


def together(*chains):
    def stage(s):
        def run():
            for chain in chains:
                chain[s]()

        return run

    return [stage(s) for s in range(len(chains[0]))]


def unslab(slabs, flat):
    rows = slabs.shape[4]
    for i in range(16):
        pair = [slabs[i // 4, i // 2 % 2, i % 2, x] for x in range(2)]
        flat[2 * rows * i : 2 * rows * (i + 1)] = jnp.concatenate(pair, axis=0)


def normed_rows(x, gain):
    x = x.astype(F32)
    return (x * norm_rows(x) * gain).astype(BF)


def forward_kernel(R, L, S, E, steps, *refs):
    tok, layt, lays, u = refs[:4]
    shards = refs[4:11]
    o, p, l, q, kf, vf, ks, vs, normed, nfar, nshort, grow = refs[11:23]
    wholes = refs[23:30]
    kcat, qcat, vt, s_ref, ohq, xfar, xshort, slab, flat, gslab, send, recv, local = refs[30:]
    W = 2 * E
    D = tok.shape[2]
    at = Place()
    sems = (send, recv)
    count = [0]

    def chain(i, cols=None):
        count[0] += 1
        k = count[0] - 1
        return gather_stages(at, shards[i], wholes[i], sems, local.at[k], GATHER_COPIES * k, cols)

    chains = [together(chain(0), chain(1)), chain(2), chain(3), chain(4)]
    chains += [chain(i, cols) for i in (5, 6) for cols in halves(shards[i].shape[1])]
    plan = turn_plan(chains)
    spare = GATHER_COPIES * count[0]
    long = remote(tok.at[0], xfar, sems, spare, at.along_x())
    short = remote(tok.at[1, pl.ds(0, S)], xshort, sems, spare + 1, at.along_x())

    def turn(t):
        for stage in plan[t]:
            stage()

    def fetch(whole, into, k):
        copy = pltpu.make_async_copy(whole, into, local.at[count[0] + k])
        copy.start()
        copy.wait()

    pair = pl.program_id(0)

    @pl.when(pair == 0)
    def _():
        at.greet()
        turn(0)
        long.start()

        @pl.when(at.x == 0)
        def _():
            short.start()
            xshort[...] = tok[1, :S]

        for i, (base, row) in enumerate([(0, layt[0]), (L, lays[...])]):
            kcat[base : base + row.shape[1], W:] = jnp.transpose(eye_of(row, SPAN, False).astype(F32)).astype(BF)
            ohq[i] = eye_of(layt[i, :, :R], SPAN, False)
        vt[:, E:] = jnp.ones((2, vt.shape[1] - E, vt.shape[2]), BF)
        for t in range(1, 5):
            turn(t)
        fetch(wholes[0], gslab, 0)
        fetch(wholes[1], slab, 1)
        columns = jnp.concatenate(
            [gslab[i // 8, i // 4 % 2, i // 2 % 2, i % 2].astype(F32) for i in range(32)], axis=0
        )
        grow[...] = jnp.transpose(columns)[:8]
        gain = grow[0:1]
        unslab(slab, flat)
        for i in range(2):
            normed[i] = normed_rows(tok[i], gain)
            q[i] = (dot(normed[i], flat[...]).astype(BF).astype(F32) * 0.125).astype(BF)
        turn(5)
        fetch(wholes[2], slab, 2)
        unslab(slab, flat)
        kf[:R] = dot(normed[0], flat[...]).astype(BF)
        long.wait()

        @pl.when(at.x == 0)
        def _():
            short.wait_send()

        @pl.when(at.x == 1)
        def _():
            short.wait_recv()

        nfar[...] = normed_rows(xfar[...], gain)
        nshort[...] = normed_rows(xshort[...], gain)
        kf[R:] = dot(nfar[...], flat[...]).astype(BF)
        ks[...] = dot(nshort[...], flat[...]).astype(BF)
        turn(6)
        fetch(wholes[3], slab, 3)
        unslab(slab, flat)
        vf[:R] = dot(normed[0], flat[...]).astype(BF)
        vf[R:] = dot(nfar[...], flat[...]).astype(BF)
        vs[...] = dot(nshort[...], flat[...]).astype(BF)

    later = {t: spot for t, spot in zip(range(TURNS_BEFORE, max(plan) + 1), (2, 6, 10, 12, 12, 12, 12))}

    def tick(spot):
        for t, when in later.items():
            if when == 2 * steps and spot == 2 or when < 2 * steps and when % 2 == spot:

                @pl.when(pair == min(when // 2, steps - 1))
                def _(t=t):
                    turn(t)

    here = pl.ds(pl.multiple_of(pair * W, W), W)
    for i, (base, keys, values) in enumerate([(0, kf, vf), (L, ks, vs)]):
        m = keys.shape[0]
        ch = min(CH, m)
        kcat[base : base + m, :W] = keys[:, here]
        vt[0, :E, :m], vt[1, :E, :m] = jnp.split(flipped(values[:, here]), 2, axis=0)
        qt = flipped(q[i, :, here])
        outs = []
        for h in range(2):
            if i == 0:
                tick(h)
            toep = pltpu.roll(jnp.broadcast_to(u[0, h : h + 1], (SPAN, 2 * SPAN)), 0, 1, stride=1, stride_axis=0)
            qcat[h * E : (h + 1) * E] = qt[h * E : (h + 1) * E]
            qcat[(1 - h) * E : (2 - h) * E] = jnp.zeros((E, R), BF)
            qcat[W:] = dot(toep[:, :SPAN].astype(BF), ohq[i]).astype(BF)
            top = jnp.full((8, R), -jnp.inf, F32)
            for c in range(0, m, ch):
                s = dot(kcat[base + c : base + c + ch], qcat[...])
                s_ref[c : c + ch] = s
                top = jnp.maximum(top, jnp.max(s.reshape(ch // 8, 8, R), axis=0))
            top = jnp.max(top, axis=0, keepdims=True)
            for c in range(0, m, ch):
                p[0, h, base + c : base + c + ch] = jnp.exp(s_ref[c : c + ch] - top).astype(BF)
            full = dot(vt[h, :, :m], p[0, h, base : base + m])
            total = full[E : E + 1]
            l[i, 0, h : h + 1] = total
            outs.append(full[:E] / total)
        o[i] = jnp.transpose(jnp.concatenate(outs, axis=0)).astype(BF)
    tick(2)


def forward_call(tok, layt, lays, u, shards, S):
    n, R, D = tok.shape
    L = layt.shape[2]
    steps = u.shape[0]
    E = D // (2 * steps)
    W = 2 * E
    KT = L + S
    whole = lambda shape: pl.BlockSpec(shape, lambda j: (0,) * len(shape))
    anywhere = pl.BlockSpec(memory_space=pl.ANY)
    held = [(n, R, D), (L, D), (L, D), (S, D), (S, D), (n, R, D), (R, D), (S, D)]
    slab = (4, 2, 2, 2) + shards[1].shape
    copies = GATHER_COPIES * 9 + 2
    return pl.pallas_call(
        functools.partial(forward_kernel, R, L, S, E, steps),
        grid=(steps,),
        in_specs=[whole(tok.shape), whole(layt.shape), whole(lays.shape), pl.BlockSpec((1, 2, 2 * SPAN), lambda j: (j, 0, 0))]
        + [anywhere] * 7,
        out_specs=[
            pl.BlockSpec((n, R, W), lambda j: (0, 0, j)),
            pl.BlockSpec((1, 2, KT, R), lambda j: (j, 0, 0, 0)),
            pl.BlockSpec((n, 1, 2, R), lambda j: (0, j, 0, 0)),
        ]
        + [whole(s) for s in held]
        + [whole((8, D))]
        + [anywhere] * 7,
        out_shape=[
            jax.ShapeDtypeStruct((n, R, D), BF),
            jax.ShapeDtypeStruct((steps, 2, KT, R), BF),
            jax.ShapeDtypeStruct((n, steps, 2, R), F32),
        ]
        + [jax.ShapeDtypeStruct(s, BF) for s in held]
        + [jax.ShapeDtypeStruct((8, D), F32)]
        + [jax.ShapeDtypeStruct((4, 2, 2, 2) + s.shape, BF) for s in shards],
        scratch_shapes=[
            pltpu.VMEM((KT, W + SPAN), BF),
            pltpu.VMEM((W + SPAN, R), BF),
            pltpu.VMEM((2, E + 16, L), BF),
            pltpu.VMEM((L, R), F32),
            pltpu.VMEM((n, SPAN, R), BF),
            pltpu.VMEM((R, D), BF),
            pltpu.VMEM((S, D), BF),
            pltpu.VMEM(slab, BF),
            pltpu.VMEM((D, D), BF),
            pltpu.VMEM((4, 2, 2, 2) + shards[0].shape, BF),
            pltpu.SemaphoreType.DMA((copies,)),
            pltpu.SemaphoreType.DMA((copies,)),
            pltpu.SemaphoreType.DMA((14,)),
        ],
        compiler_params=pltpu.CompilerParams(
            vmem_limit_bytes=58 * 2**20, dimension_semantics=("arbitrary",), collective_id=0, has_side_effects=True
        ),
        name="forward",
    )(tok, layt, lays, u, *shards)


EPSILON = 1e-06
THRESHOLDS = (12, 16, 23, 32, 46, 64, 91)
BOTH = ("dp", "blk")


def bucket_np(relative):
    magnitude = np.abs(relative)
    larger = 8 + sum((magnitude >= limit).astype(np.int64) for limit in THRESHOLDS)
    return np.where(magnitude < 8, magnitude, larger) + 16 * (relative > 0)


def bucket_rows(distance, buckets):
    return (bucket_np(distance)[:, None] == np.arange(buckets)[None, :]).astype(np.float32)


def norm_parts(x, gain):
    back = lax.rsqrt(jnp.mean(x * x, axis=-1, keepdims=True) + EPSILON)
    return (x * back * gain).astype(BF), back


def norm_back(d, x, back, gain):
    a = gain * d
    grad_gain = jnp.sum(d * x * back, axis=0)
    return back * a - x * back**3 * jnp.mean(a * x, axis=-1, keepdims=True), grad_gain


def mm(a, b, dims):
    return lax.dot_general(a, b, (dims, ((), ())), preferred_element_type=F32)


def gather_weights(gain_one, wq, wk, wv, wo, gain_two, wi, wt):
    full = lambda a: lax.all_gather(a, BOTH, axis=0, tiled=True)
    packed = full(jnp.concatenate([wq, wk, wv, wo, wi], axis=1))
    width = wq.shape[1]
    gains = full(jnp.stack([gain_one, gain_two], axis=1))
    return packed[:, : 3 * width], packed[:, 3 * width : 4 * width], packed[:, 4 * width :], full(wt), gains[:, 0], gains[:, 1]


def scatter_sums(dqkv, dwo, dwi, dwt, dg1, dg2):
    take = lambda a: lax.psum_scatter(a, BOTH, scatter_dimension=0, tiled=True)
    width = dwo.shape[1]
    packed = take(jnp.concatenate([dqkv, dwo, dwi], axis=1).astype(BF)).astype(F32)
    gains = take(jnp.stack([dg1, dg2], axis=1))
    parts = [packed[:, i * width : (i + 1) * width] for i in range(4)]
    return parts, packed[:, 4 * width :], take(dwt.astype(BF)).astype(F32), gains[:, 0], gains[:, 1]


def on_any_device(tokens, layout, lengths, gain_one, wq, wk, wv, wo, gain_two, wi, wt, table, grad_out):
    n, R, D = tokens.shape
    H = table.shape[1]
    G = lax.axis_size("blk")
    me = lax.axis_index("blk")
    L = layout.shape[1]
    S = L // 8
    order = jnp.argsort(-lengths, stable=True)
    place = jnp.argsort(order)
    tok = tokens[order]
    gout = grad_out[order]
    lay = layout[order]
    lens = lengths[order]

    def from_step(x, s):
        return lax.ppermute(x, "blk", [(i, (i - s) % G) for i in range(G)])

    pieces = [tok[:-1]] + [from_step(tok[:-1], s) for s in range(1, G)]
    xf = jnp.concatenate(pieces, axis=1)
    first = tok[-1, :S]
    xs = jnp.where(me == 0, first, sum(lax.ppermute(first, "blk", [(0, i)]) for i in range(1, G)))
    lay_turned = jnp.roll(lay, -me * R, axis=1)
    layq = lay_turned[:, None, :R]
    layf = lay_turned[:-1, None, :]
    lays = lay[-1:, :S]
    spots = (jnp.arange(L) + me * R) % L
    mask = jnp.where(spots[None, :, None] < lens[:-1, None, None], 0.0, -1e30).astype(F32)

    wqkv, wo_all, wi_all, wt_all, g1, g2 = gather_weights(gain_one, wq, wk, wv, wo, gain_two, wi, wt)
    g1 = g1.astype(F32)
    g2 = g2.astype(F32)
    hidden = tok.reshape(n * R, D).astype(F32)
    normed, r1 = norm_parts(hidden, g1)
    xkeys = jnp.concatenate([xf.reshape((n - 1) * L, D), xs], axis=0)
    nkeys, _ = norm_parts(xkeys.astype(F32), g1)
    q = (mm(normed, wqkv[:, :D], ((1,), (0,))).astype(BF) * jnp.asarray(0.125, BF)).reshape(n, R, D)
    k = mm(nkeys, wqkv[:, D : 2 * D], ((1,), (0,))).astype(BF)
    v = mm(nkeys, wqkv[:, 2 * D :], ((1,), (0,))).astype(BF)
    cut = (n - 1) * L
    kf, ks = k[:cut].reshape(n - 1, L, D), k[cut:]
    vf, vs = v[:cut].reshape(n - 1, L, D), v[cut:]
    lane = np.arange(2 * SPAN)
    turned = np.where(lane >= SPAN, lane - 2 * SPAN, lane)
    urow = mm(table, bucket_rows(-turned, table.shape[0]).astype(BF), ((0,), (1,))).reshape(H // 2, 2, 2 * SPAN)
    o, p, l = attend_call(q, kf, vf, ks, vs, layq, layf, lays, mask, urow)

    attended = o.reshape(n * R, D)
    resid = hidden + mm(attended, wo_all, ((1,), (0,)))
    normed_two, r2 = norm_parts(resid, g2)
    pre = mm(normed_two, wi_all, ((1,), (0,)))
    act, act_back = jax.vjp(lambda x: jax.nn.gelu(x, approximate=False), pre)
    act = act.astype(BF)
    mixed = (resid + mm(act, wt_all, ((1,), (0,)))).astype(BF)
    up = gout.reshape(n * R, D)
    dwt = mm(act, up, ((0,), (0,)))
    (dpre,) = act_back(mm(up, wt_all, ((1,), (1,))))
    dpre = dpre.astype(BF)
    dwi = mm(normed_two, dpre, ((0,), (0,)))
    dn2 = mm(dpre, wi_all, ((1,), (1,)))
    dresid, dg2 = norm_back(dn2, resid, r2, g2)
    dresid = dresid + up.astype(F32)
    low = dresid.astype(BF)
    dwo = mm(attended, low, ((0,), (0,)))
    datt = mm(low, wo_all, ((1,), (1,))).astype(BF).reshape(n, R, D)

    dq, dkf, dvf, dks, dvs, t = attend_back_call(q, kf, vf, ks, vs, layq, layf, lays, o, datt, p, l)
    dtable = jnp.einsum(
        "hj,jb->bh", t.reshape(H, 2 * SPAN), bucket_rows(SPAN - 1 - lane, table.shape[0]), precision=lax.Precision.HIGHEST
    )
    dq = dq.reshape(n * R, D)
    dk = jnp.concatenate([dkf.reshape(cut, D), dks], axis=0)
    dv = jnp.concatenate([dvf.reshape(cut, D), dvs], axis=0)
    dnk = mm(dk, wqkv[:, D : 2 * D], ((1,), (1,))) + mm(dv, wqkv[:, 2 * D :], ((1,), (1,)))
    dnf = dnk[:cut].reshape(n - 1, L, D)
    dns = dnk[cut:].astype(BF)
    far = sum(
        lax.ppermute(dnf[:, s * R : (s + 1) * R].astype(BF), "blk", [(i, (i + s) % G) for i in range(G)]).astype(F32)
        for s in range(1, G)
    )
    near = jnp.where(
        me == 0, dnk[cut:] + sum(lax.ppermute(dns, "blk", [(i, 0)]).astype(F32) for i in range(1, G)), 0.0
    )
    extra = jnp.concatenate([dnf[:, :R] + far, jnp.pad(near, ((0, R - S), (0, 0)))[None]], axis=0).reshape(n * R, D)
    dn1 = mm(dq, wqkv[:, :D], ((1,), (1,))) + extra
    dwq = mm(normed, dq, ((0,), (0,)))
    dwk = mm(nkeys, dk, ((0,), (0,)))
    dwv = mm(nkeys, dv, ((0,), (0,)))
    dx, dg1 = norm_back(dn1, hidden, r1, g1)
    gtok = (dresid + dx).astype(BF)
    parts, gwi, gwt, gg1, gg2 = scatter_sums(jnp.concatenate([dwq, dwk, dwv], axis=1), dwo, dwi, dwt, dg1, dg2)
    dtable = lax.psum(dtable, BOTH)
    return (
        mixed.reshape(n, R, D)[place],
        gtok.reshape(n, R, D)[place],
        gg1,
        parts[0],
        parts[1],
        parts[2],
        parts[3],
        gg2,
        gwi,
        gwt,
        dtable,
    )


def on_device(tokens, layout, lengths, gain_one, wq, wk, wv, wo, gain_two, wi, wt, table, grad_out):
    n, R, D = tokens.shape
    H = table.shape[1]
    G = lax.axis_size("blk")
    me = lax.axis_index("blk")
    L = layout.shape[1]
    S = L // 8
    swap = lengths[0] < lengths[1]
    pick = lambda a: jnp.where(swap, a[::-1], a)
    tok = pick(tokens)
    up = pick(grad_out).reshape(n * R, D)
    lay = pick(layout)
    layt = jnp.where(me == 0, lay, jnp.roll(lay, R, axis=1))[:, None, :]
    lays = lay[1:, :S]
    lane = np.arange(2 * SPAN)
    turned = np.where(lane >= SPAN, lane - 2 * SPAN, lane)
    urow = mm(table, bucket_rows(-turned, table.shape[0]).astype(BF), ((0,), (1,))).reshape(H // 2, 2, 2 * SPAN)
    gains = jnp.pad(jnp.stack([gain_one, gain_two], axis=1), ((0, 0), (0, 126)))
    o, p, l, q, kf, vf, ks, vs, normed, nfar, nshort, grow, *wholes = forward_call(
        tok, layt, lays, urow, [gains, wq, wk, wv, wo, wi, wt], S
    )
    _, wq_all, wk_all, wv_all, wo_all, wi_all, wt_all = [a.reshape(-1, a.shape[-1]) for a in wholes]
    g1 = grow[0]
    hidden = tok.reshape(n * R, D)
    mixed, dresid, datt, dwo, dwi, dwt, dg2 = feed_forward_call(
        o.reshape(n * R, D), hidden, up, wo_all, grow[1:2], wi_all, wt_all
    )
    slabs = lambda a: a.reshape(4, 2, 2, 2, -1, a.shape[-1])
    dq, dkf, dvf, dks, dvs, t, gwt, gwi, gwo = attend_back_call(
        q, kf[None], vf[None], ks, vs, layt[:, :, :R], layt[:1], lays, o, datt.reshape(n, R, D), p, l, [slabs(dwt), slabs(dwi), slabs(dwo)]
    )
    dtable = jnp.einsum(
        "hj,jb->bh", t.reshape(H, 2 * SPAN), bucket_rows(SPAN - 1 - lane, table.shape[0]), precision=lax.Precision.HIGHEST
    )
    dq = dq.reshape(n * R, D)
    dk = jnp.concatenate([dkf[0], dks], axis=0)
    dv = jnp.concatenate([dvf[0], dvs], axis=0)
    nkeys = jnp.concatenate([normed[0], nfar, nshort], axis=0)
    dnk = mm(dk, wk_all, ((1,), (1,))) + mm(dv, wv_all, ((1,), (1,)))
    far = lax.ppermute(dnk[R:L].astype(BF), "blk", [(0, 1), (1, 0)]).astype(F32)
    near = lax.ppermute(dnk[L:].astype(BF), "blk", [(1, 0)]).astype(F32)
    near = jnp.where(me == 0, dnk[L:] + near, 0.0)
    extra = jnp.concatenate([dnk[:R] + far, jnp.pad(near, ((0, R - S), (0, 0)))], axis=0)
    dn1 = mm(dq, wq_all, ((1,), (1,))) + extra
    dwq = mm(normed.reshape(n * R, D), dq, ((0,), (0,))).astype(BF)
    dwk = mm(nkeys, dk, ((0,), (0,))).astype(BF)
    dwv = mm(nkeys, dv, ((0,), (0,))).astype(BF)
    hidden = hidden.astype(F32)
    r1 = lax.rsqrt(jnp.mean(hidden * hidden, axis=-1, keepdims=True) + EPSILON)
    dx, dg1 = norm_back(dn1, hidden, r1, g1)
    gtok = (dresid + dx).astype(BF).reshape(n, R, D)
    small = jnp.concatenate([dg1, dg2[0], dtable.reshape(-1)]).reshape(-1, 128)
    small = jnp.pad(small, ((0, -small.shape[0] % 8), (0, 0)))
    gwq, gwk, gwv, small = sum_call([slabs(dwq), slabs(dwk), slabs(dwv)], small)
    small = small.reshape(-1)
    mine = (lax.axis_index("dp") * G + me) * (D // 32)
    gg1, gg2 = [lax.dynamic_slice_in_dim(small, mine + i * D, D // 32) for i in range(2)]
    dtable = small[2 * D : 2 * D + table.size].reshape(table.shape)
    return pick(mixed.reshape(n, R, D)), pick(gtok), gg1, gwq, gwk, gwv, gwo, gg2, gwi, gwt, dtable


def solution(mesh):
    rows = P(BOTH, None)
    items = P("dp", "blk", None)
    known = dict(mesh.shape) == {"dp": 16, "blk": 2}

    def body(tokens, *rest):
        return (on_device if known and tokens.shape[0] == 2 else on_any_device)(tokens, *rest)

    return jax.shard_map(
        body,
        mesh=mesh,
        in_specs=(items, P("dp", None), P("dp"), P(BOTH), rows, rows, rows, rows, P(BOTH), rows, rows, P(), items),
        out_specs=(items, items, P(BOTH), rows, rows, rows, rows, P(BOTH), rows, rows, P()),
        check_vma=False,
    )
```

```python
import functools
import math

import jax
import jax.numpy as jnp
import numpy as np
from jax import lax
from jax.experimental import pallas as pl
from jax.experimental.pallas import tpu as pltpu
from jax.sharding import PartitionSpec as P

F32=jnp.float32; BF=jnp.bfloat16
SPAN=256
CH=256
def dot(a,b): return lax.dot_general(a,b,(((1,),(0,)),((),())),preferred_element_type=F32)
def eye_of(row, width, reverse):
    spots=lax.broadcasted_iota(jnp.int32,(width,row.shape[1]),0)
    if reverse: spots=width-1-spots
    return (spots==row).astype(F32).astype(BF)

def attend(n,L,S,R,E, q,kf,vf,ks,vs,layq,layf,lays,mask,u,o,p,l, kcat,qcat,vt,s_ref,ohq):
    W=2*E
    spans=[L]*(n-1)+[S]
    @pl.when(pl.program_id(0)==0)
    def _():
        base=0
        for i,m in enumerate(spans):
            row=layf[i] if i<n-1 else lays[...]
            kcat[base:base+m,W:]=jnp.transpose(eye_of(row,SPAN,False).astype(F32)).astype(BF)
            ohq[i]=eye_of(layq[i],SPAN,False)
            base+=m
        vt[:,E:]=jnp.ones((2,vt.shape[1]-E,vt.shape[2]),BF)
    pair=pl.program_id(0)
    base=0
    for i,m in enumerate(spans):
        ch=min(CH,m)
        kcat[base:base+m,:W]=kf[i] if i<n-1 else ks[...]
        v=vf[i] if i<n-1 else vs[...]
        vtr=jnp.transpose(v.astype(F32)).astype(BF)
        vt[0,:E,:m]=vtr[:E]
        vt[1,:E,:m]=vtr[E:]
        qt=jnp.transpose(q[i].astype(F32)).astype(BF)
        outs=[]
        for h in range(2):
            urow=u[pl.ds(0,1),h,:] if False else u[0,h:h+1,:]
            toep=pltpu.roll(jnp.broadcast_to(urow,(SPAN,2*SPAN)),0,1,stride=1,stride_axis=0)[:,:SPAN].astype(BF)
            qcat[h*E:(h+1)*E]=qt[h*E:(h+1)*E]
            qcat[(1-h)*E:(2-h)*E]=jnp.zeros((E,R),BF)
            qcat[W:]=dot(toep,ohq[i]).astype(BF)
            m8=jnp.full((8,R),-jnp.inf,F32)
            for c in range(0,m,ch):
                s=dot(kcat[base+c:base+c+ch],qcat[...])
                if 0<i<n-1: s=s+mask[i,c:c+ch,:]
                s_ref[c:c+ch]=s
                m8=jnp.maximum(m8,jnp.max(s.reshape(ch//8,8,R),axis=0))
            top=jnp.max(m8,axis=0,keepdims=True)
            for c in range(0,m,ch):
                p[0,h,base+c:base+c+ch]=jnp.exp(s_ref[c:c+ch]-top).astype(BF)
            full=dot(vt[h,:,:m],p[0,h,base:base+m])
            total=full[E:E+1]
            l[i,0,h:h+1]=total
            outs.append(full[:E]/total)
        o[i]=jnp.transpose(jnp.concatenate(outs,axis=0)).astype(BF)
        base+=m

def attend_call(q,kf,vf,ks,vs,layq,layf,lays,mask,u):
    n,R,D=q.shape; L=kf.shape[1]; S=ks.shape[0]; H=u.shape[0]*2; E=D//H; W=2*E
    KT=(n-1)*L+S
    full=lambda a: pl.BlockSpec(a.shape,lambda j:(0,)*a.ndim)
    return pl.pallas_call(functools.partial(attend,n,L,S,R,E),
      grid=(H//2,),
      in_specs=[pl.BlockSpec((n,R,W),lambda j:(0,0,j)),
        pl.BlockSpec((n-1,L,W),lambda j:(0,0,j)),pl.BlockSpec((n-1,L,W),lambda j:(0,0,j)),
        pl.BlockSpec((S,W),lambda j:(0,j)),pl.BlockSpec((S,W),lambda j:(0,j)),
        full(layq),full(layf),full(lays),full(mask),pl.BlockSpec((1,2,2*SPAN),lambda j:(j,0,0))],
      out_specs=[pl.BlockSpec((n,R,W),lambda j:(0,0,j)),
        pl.BlockSpec((1,2,KT,R),lambda j:(j,0,0,0)),
        pl.BlockSpec((n,1,2,R),lambda j:(0,j,0,0))],
      out_shape=[jax.ShapeDtypeStruct((n,R,D),BF),jax.ShapeDtypeStruct((H//2,2,KT,R),BF),jax.ShapeDtypeStruct((n,H//2,2,R),F32)],
      scratch_shapes=[pltpu.VMEM((KT,W+SPAN),BF),pltpu.VMEM((W+SPAN,R),BF),pltpu.VMEM((2,E+16,L),BF),pltpu.VMEM((L,R),F32),pltpu.VMEM((n,SPAN,R),BF)],
      compiler_params=pltpu.CompilerParams(vmem_limit_bytes=56*2**20,dimension_semantics=("arbitrary",)),
      name="attend",
    )(q,kf,vf,ks,vs,layq,layf,lays,mask,u)

def attend_back(n,L,S,R,E, q,kf,vf,ks,vs,layq,layf,lays,o,do,p,l, dq,dkf,dvf,dks,dvs,t, kq,vaug,rhs,ds,ohq,nacc,qm,dm):
    W=2*E
    spans=[L]*(n-1)+[S]
    @pl.when(pl.program_id(0)==0)
    def _():
        base=0
        for i,m in enumerate(spans):
            row=layf[i] if i<n-1 else lays[...]
            kq[:SPAN,base:base+m]=eye_of(row,SPAN,True)
            ohq[i]=jnp.transpose(eye_of(layq[i],SPAN,False).astype(F32)).astype(BF)
            base+=m
        vaug[:,W:]=(lax.broadcasted_iota(jnp.int32,(vaug.shape[0],W),1)<2).astype(F32).astype(BF)
        rhs[...]=jnp.zeros_like(rhs)
    nacc[...]=jnp.zeros_like(nacc)
    base=0
    lane=lax.broadcasted_iota(jnp.int32,(R,W),1)
    for i,m in enumerate(spans):
        ch=min(CH,m)
        kk=kf[i] if i<n-1 else ks[...]
        vaug[:m,:W]=vf[i] if i<n-1 else vs[...]
        kt=jnp.transpose(kk.astype(F32)).astype(BF)
        dot_=jnp.transpose(do[i].astype(F32))
        ot=jnp.transpose(o[i].astype(F32))
        scaled=[];
        for h in range(2):
            inv=1.0/l[i,0,h:h+1]
            scaled.append((dot_[h*E:(h+1)*E]*inv).astype(BF))
        sc=jnp.concatenate(scaled,axis=0)
        don=jnp.transpose(sc.astype(F32)).astype(BF)
        qq=q[i]
        zero=jnp.zeros((R,W),BF)
        for h in range(2):
            mine=(lane<E) if h==0 else (lane>=E)
            qm[h*R:(h+1)*R]=jnp.where(mine,qq,zero)
            dm[h*R:(h+1)*R]=jnp.where(mine,don,zero)
        dqs=[]
        for h in range(2):
            rhs[h*E:(h+1)*E]=scaled[h]
            rhs[(1-h)*E:(2-h)*E]=jnp.zeros((E,R),BF)
            delta=jnp.sum(scaled[h].astype(F32)*ot[h*E:(h+1)*E],axis=0,keepdims=True)
            hi=delta.astype(BF).astype(F32)
            lo=delta-hi
            spot=lax.broadcasted_iota(jnp.int32,(16,R),0)
            rhs[W:W+16]=jnp.where(spot==0,-hi,jnp.where(spot==1,-lo,0.0)).astype(BF)
            for c in range(0,m,ch):
                g=dot(vaug[c:c+ch],rhs[...])
                ds[c:c+ch,h*R:(h+1)*R]=(p[0,h,base+c:base+c+ch].astype(F32)*g).astype(BF)
            kq[SPAN:,base:base+m]=kt[h*E:(h+1)*E]
            both=dot(kq[:,base:base+m],ds[:m,h*R:(h+1)*R])
            dqs.append(both[SPAN:]*0.125)
            nacc[h]+=dot(both[:SPAN].astype(BF),ohq[i])
        dq[i]=jnp.transpose(jnp.concatenate(dqs,axis=0)).astype(BF)
        for c in range(0,m,ch):
            dk=dot(ds[c:c+ch],qm[...])
            dv=dot(p[0,0,base+c:base+c+ch],dm[:R])+dot(p[0,1,base+c:base+c+ch],dm[R:])
            if i<n-1:
                dkf[i,c:c+ch]=dk.astype(BF); dvf[i,c:c+ch]=dv.astype(BF)
            else:
                dks[c:c+ch]=dk.astype(BF); dvs[c:c+ch]=dv.astype(BF)
        base+=m
    for h in range(2):
        wide=jnp.concatenate([nacc[h],jnp.zeros((SPAN,SPAN),F32)],axis=1)
        rolled=pltpu.roll(wide,0,1,stride=1,stride_axis=0)
        t[0,h:h+1]=jnp.sum(rolled,axis=0,keepdims=True)

def attend_back_call(q,kf,vf,ks,vs,layq,layf,lays,o,do,p,l):
    n,R,D=q.shape; L=kf.shape[1]; S=ks.shape[0]; H=p.shape[0]*2; E=D//H; W=2*E
    KT=(n-1)*L+S
    full=lambda a: pl.BlockSpec(a.shape,lambda j:(0,)*a.ndim)
    rows=lambda: pl.BlockSpec((n,R,W),lambda j:(0,0,j))
    kb=lambda: pl.BlockSpec((n-1,L,W),lambda j:(0,0,j))
    sb=lambda: pl.BlockSpec((S,W),lambda j:(0,j))
    return pl.pallas_call(functools.partial(attend_back,n,L,S,R,E),
      grid=(H//2,),
      in_specs=[rows(),kb(),kb(),sb(),sb(),full(layq),full(layf),full(lays),rows(),rows(),
        pl.BlockSpec((1,2,KT,R),lambda j:(j,0,0,0)),pl.BlockSpec((n,1,2,R),lambda j:(0,j,0,0))],
      out_specs=[rows(),kb(),kb(),sb(),sb(),pl.BlockSpec((1,2,2*SPAN),lambda j:(j,0,0))],
      out_shape=[jax.ShapeDtypeStruct((n,R,D),BF),jax.ShapeDtypeStruct(kf.shape,BF),jax.ShapeDtypeStruct(kf.shape,BF),
        jax.ShapeDtypeStruct(ks.shape,BF),jax.ShapeDtypeStruct(ks.shape,BF),jax.ShapeDtypeStruct((H//2,2,2*SPAN),F32)],
      scratch_shapes=[pltpu.VMEM((SPAN+E,KT),BF),pltpu.VMEM((L,2*W),BF),pltpu.VMEM((2*W,R),BF),pltpu.VMEM((L,2*R),BF),
        pltpu.VMEM((n,R,SPAN),BF),pltpu.VMEM((2,SPAN,SPAN),F32),pltpu.VMEM((2*R,W),BF),pltpu.VMEM((2*R,W),BF)],
      compiler_params=pltpu.CompilerParams(vmem_limit_bytes=56*2**20,dimension_semantics=("arbitrary",)),
      name="attend_back",
    )(q,kf,vf,ks,vs,layq,layf,lays,o,do,p,l)


EPSILON = 1e-06
FORWARD_PIECES = 2
FORWARD_WAYS = (0,) * 9
FORWARD_AT = (
    (-9, -8, -7, -6, -5),
    (-8, -7, -6, -5, -4),
    (-7, -6, -5, -4, -3),
    (-6, -5, -4, -3, -2),
    (-5, -4, -3, -2, 6),
    (-4, -3, -2, 6, 12),
    (-3, -2, 6, 12, 18),
    (-2, 6, 12, 18, 24),
)
FF_SUMS = 3
FF_SUM = (0, 2)
FF_SUM_LAG = (0, 3, 7, 11, 16)
BACK_SUM = (2, 2, 4)


MESH = pl.DeviceIdType.MESH


class Place:
    def __init__(self, mostly_y=False):
        dp = lax.axis_index("dp")
        self.x = lax.axis_index("blk")
        self.z, self.y, self.c = dp // 4, (dp // 2) % 2, dp % 2
        c = 1 if mostly_y else self.c
        self.y1, self.x1 = (self.y + 1 - c) % 2, (self.x + c) % 2
        self.y2, self.x2 = (self.y + c) % 2, (self.x + 1 - c) % 2

    def device(self, z, y, c, x):
        return ((z * 2 + y) * 2 + c, x)

    def along_z(self, d):
        return self.device((self.z + d) % 4, self.y, self.c, self.x)

    def along_x(self):
        return self.device(self.z, self.y, self.c, 1 - self.x)

    def along_y(self):
        return self.device(self.z, 1 - self.y, self.c, self.x)

    def first(self):
        return self.device(self.z, self.y1, self.c, self.x1)

    def second(self):
        return self.device(self.z, self.y2, self.c, self.x2)

    def core(self):
        return self.device(self.z, self.y, 1 - self.c, self.x)

    def greet(self):
        barrier = pltpu.get_barrier_semaphore()
        partners = [self.along_z(d) for d in (1, 2, 3)] + [self.first(), self.second(), self.core()]
        for partner in partners:
            pl.semaphore_signal(barrier, inc=1, device_id=partner, device_id_type=MESH)
        pl.semaphore_wait(barrier, len(partners))


def remote(src, dst, sems, k, device):
    return pltpu.make_async_remote_copy(
        src_ref=src, dst_ref=dst, send_sem=sems[0].at[k], recv_sem=sems[1].at[k], device_id=device, device_id_type=MESH
    )


GATHER_COPIES = 10


def gather_stages(at, shard, whole, sems, local, base, cols=None, plane=None):
    z, y, c, x = at.z, at.y, at.c, at.x
    cols = pl.ds(0, shard.shape[1]) if cols is None else cols
    shard = shard.at[:, cols]
    own = whole.at[z if plane is None else 0, y, c, x]
    keep = pltpu.make_async_copy(shard, own, local)

    def group(yy, xx):
        return whole.at[:, yy, c, xx]

    def copy(k):
        if k < 3:
            return remote(shard, own, sems, base + k, at.along_z(k + 1))
        view, device = {
            3: (group(y, x), at.first()),
            4: (group(y, x), at.second()),
            5: (group(y, x), at.core()),
            6: (group(at.y1, at.x1), at.second()),
            7: (group(at.y1, at.x1), at.core()),
            8: (group(at.y2, at.x2), at.core()),
            9: (group(1 - y, 1 - x), at.core()),
        }[k]
        return remote(view, view, sems, base + k, device)

    def one():
        def start():
            keep.start()
            for k in range(3):
                copy(k).start()

        start() if plane is None else pl.when(z == plane)(start)

    def two():
        if plane is None:
            keep.wait()
            for k in range(3):
                copy(k).wait_recv()
        else:
            pl.when(z == plane)(keep.wait)
            d = (z - plane + 4) % 4
            arrival = remote(shard, own, sems, base + d - 1, at.along_z(1))
            pl.when(z != plane)(arrival.wait_recv)
        for k in (3, 4, 5):
            copy(k).start()

    def three():
        copy(3).wait_recv()
        for k in (6, 7):
            copy(k).start()

    def four():
        copy(4).wait_recv()
        copy(8).start()
        copy(6).wait_recv()
        copy(9).start()

    def five():
        for k in (5, 7, 8, 9):
            copy(k).wait_recv()
        for k in range(3, 10):
            copy(k).wait_send()

        def sent():
            for k in range(3):
                copy(k).wait_send()

        sent() if plane is None else pl.when(z == plane)(sent)

    return [one, two, three, four, five]


def gather_stages_x(at, shard, whole, sems, local, base):
    z, y, c, x = at.z, at.y, at.c, at.x
    own = whole.at[z, y, c, x]
    keep = pltpu.make_async_copy(shard, own, local)

    def copy(k):
        if k == 0:
            return remote(shard, own, sems, base, at.along_x())
        view, device = {
            1: (whole.at[z, y, c], at.along_z(1)),
            2: (whole.at[z, y, c], at.along_z(2)),
            3: (whole.at[z, y, c], at.along_z(3)),
            4: (whole.at[:, y, c], at.along_y()),
            5: (whole.at[:, y, c], at.core()),
            6: (whole.at[:, 1 - y, c], at.core()),
        }[k]
        return remote(view, view, sems, base + k, device)

    def step(arrivals, starts):
        def run():
            for k in arrivals:
                copy(k).wait_recv()
            for k in starts:
                copy(k).start()

        return run

    def one():
        keep.start()
        copy(0).start()

    def two():
        keep.wait()
        step((0,), (1, 2, 3))()

    def five():
        step((5, 6), ())()
        for k in range(7):
            copy(k).wait_send()

    return [one, two, step((1, 2, 3), (4, 5)), step((4,), (6,)), five]


def small_stages(at, part, total, held, got, sems, base):
    def copy(k):
        device = [at.core, at.along_y, at.along_x][k]() if k < 3 else at.along_z(k - 2)
        return remote(held.at[min(k, 3)], got.at[k], sems, base + k, device)

    def one():
        held[0] = part[...]
        copy(0).start()

    def add(k):
        def run():
            copy(k).wait_recv()
            held[k + 1] = held[k] + got[k]
            for following in (k + 1,) if k < 2 else (3, 4, 5):
                copy(following).start()

        return run

    def five():
        parts = [held[3]]
        for d in (1, 2, 3):
            copy(2 + d).wait_recv()
            parts.append(got[2 + d])
        out = jnp.zeros_like(parts[0])
        for spot in range(4):
            for d in range(4):
                out = out + jnp.where((at.z - d + 4) % 4 == spot, parts[d], 0.0)
        total[...] = out
        for k in range(6):
            copy(k).wait_send()

    return [one, add(0), add(1), add(2), five]


def norm_rows(x):
    return lax.rsqrt(jnp.mean(x * x, axis=1, keepdims=True) + EPSILON)


def dot_nt(a, b):
    return lax.dot_general(a, b, (((1,), (1,)), ((), ())), preferred_element_type=F32)


def flipped(a):
    return jnp.transpose(a.astype(F32)).astype(BF)


TICKS = 6


def feed_forward_plan(sums):
    events = []
    for i, (stages, j) in enumerate(sums):
        for s, lag in enumerate(FF_SUM_LAG):
            events.append((TICKS * (j + 1) + FF_SUM[i % 2] + lag, stages[s]))
    plan = {}
    for when, stage in sorted(events, key=lambda e: e[0]):
        plan.setdefault(when, []).append(stage)
    return plan


def feed_forward(R, blocks, *refs):
    flag, att_, tok_, up_, wo_, grow = refs[:6]
    given = refs[6:8]
    refs = list(refs[8:])
    take = lambda k: [refs.pop(0) for _ in range(k)]
    mixed, dres, datt, dwo = take(4)
    last = FF_SUMS
    handed = [take(2) for _ in range(last, blocks)]
    (dgain,) = take(1)
    totals_in = take(last)
    (total_out,) = take(1)
    att, tok, up, wo, wbi, wbt, n2, n2t, resid, acc, dn2, act_t, dpre_s, parts_in, parts_out = take(15)
    sum_scratch = [take(5) for _ in range(2 * last)]
    send, recv, local = take(3)
    rows, width = att.shape
    block = wbi.shape[2]
    piece = rows // 4
    pieces = [pl.ds(i, piece) for i in range(0, rows, piece)]
    step = pl.program_id(0)
    slot = lax.rem(step, 2)
    at = Place()
    sems = (send, recv)

    sums = []
    for j in range(last):
        for which, (part, total) in enumerate([(parts_in.at[j], totals_in[j]), (parts_out.at[j], total_out)]):
            i = len(sums)
            chain = Sum(at, part, total, sum_scratch[i], sems, None, Sum.COPIES * i, None, j if which else None)
            sums.append((chain.stages, j))
    plan = feed_forward_plan(sums)

    def local_copy(a, b, k):
        return pltpu.make_async_copy(a, b, local.at[k])

    def weights(j):
        hidden = pl.ds(j * block, block)
        return [local_copy(given[0].at[:, hidden], wbi.at[j % 2], 4), local_copy(given[1].at[hidden], wbt.at[j % 2], 5)]

    def tick(t):
        for when in plan:
            if when < TICKS * blocks and when % TICKS == t:

                @pl.when(step == when // TICKS)
                def _(when=when):
                    for stage in plan[when]:
                        stage()

    @pl.when(step == 0)
    def _():
        loads = [local_copy(a, b, i) for i, (a, b) in enumerate([(tok_, tok), (att_, att), (wo_, wo), (up_, up)])]
        for load in loads + weights(0):
            load.start()
        at.greet()
        for load in loads:
            load.wait()
        for a in (tok, up):
            a[:R], a[R:] = swapped(flag, a[:R], a[R:])
        for b in pieces:
            x = tok[b].astype(F32) + dot(att[b], wo[...])
            resid[b] = x
            normed = (x * norm_rows(x) * grow[1:2]).astype(BF)
            n2[b] = normed
            n2t[:, b] = flipped(normed)
            acc[b] = x
            dn2[b] = jnp.zeros_like(x)

    for j in range(blocks):

        @pl.when(step == j)
        def _(j=j):
            for load in weights(j):
                load.wait()
            if j + 1 < blocks:
                for load in weights(j + 1):
                    load.start()

    for i, b in enumerate(pieces):
        tick(i)
        pre = dot(n2[b], wbi[slot])
        dact = dot_nt(up[b], wbt[slot])
        half = 0.5 + 0.5 * lax.erf(pre * 0.7071067811865476)
        act = (pre * half).astype(BF)
        dpre = (dact * (half + pre * (jnp.exp(-0.5 * pre * pre) * 0.3989422804014327))).astype(BF)
        acc[b] += dot(act, wbt[slot])
        dn2[b] += dot_nt(dpre, wbi[slot])
        act_t[:, b] = flipped(act)
        dpre_s[b] = dpre
    tick(4)
    grad_in = dot(n2t[...], dpre_s[...])
    tick(5)
    grad_out = dot(act_t[...], up[...])

    into_slabs(grad_in, parts_in.at[step])
    count = parts_out.shape[5]
    for i in range(8):
        parts_out[step, 0, i // 4, i // 2 % 2, i % 2] = grad_out[count * i : count * (i + 1)].astype(BF)
    hand = [
        [local_copy(parts_in.at[j], handed[j - last][0], 6 + 2 * j), local_copy(parts_out.at[j], handed[j - last][1], 7 + 2 * j)]
        for j in range(last, blocks)
    ]
    for j in range(last, blocks):

        @pl.when(step == j)
        def _(j=j):
            for copy in hand[j - last]:
                copy.start()

    @pl.when(step == blocks - 1)
    def _():
        rest = [stage for t in sorted(plan) if t >= TICKS * blocks for stage in plan[t]]

        def some(count):
            for _ in range(min(count, len(rest))):
                rest.pop(0)()

        ends = []
        some(2)
        for i, b in enumerate(pieces):
            n2[b] = acc[b].astype(BF)
        n2[:R], n2[R:] = swapped(flag, n2[:R], n2[R:])
        ends.append(local_copy(n2, mixed, 2))
        ends[-1].start()
        total = None
        for b in pieces:
            x, d = resid[b], dn2[b]
            back = norm_rows(x)
            a = grow[1:2] * d
            part = jnp.sum(d * x * back, axis=0, keepdims=True)
            total = part if total is None else total + part
            g = up[b].astype(F32) + back * a - x * (back * back * back) * jnp.mean(a * x, axis=1, keepdims=True)
            dn2[b] = g
            g = g.astype(BF)
            up[b] = g
            tok[b] = dot_nt(g, wo[...]).astype(BF)
            act_t[:width, b] = flipped(att[b])
            some(1)
        dgain[...] = total
        ends += [local_copy(dn2, dres, 3), local_copy(tok, datt, 4)]
        ends[-1].start()
        ends[-2].start()
        dpre_s[:width, :width] = dot(act_t[:width], up[...]).astype(BF)
        ends.append(local_copy(dpre_s.at[pl.ds(0, width), pl.ds(0, width)], dwo, 5))
        ends[-1].start()
        some(100)
        for end in ends + sum(hand, []):
            end.wait()


def feed_forward_call(flag, att, tokens, up, wo, grow, wi, wt):
    rows, D = tokens.shape
    R = rows // 2
    blocks = 4
    last = FF_SUMS
    block = wi.shape[1] // blocks
    share_in, share_out = (D // 32, block), (wt.shape[0] // 32, D)
    anywhere = pl.BlockSpec(memory_space=pl.ANY)
    whole = lambda shape: pl.BlockSpec(shape, lambda j: (0,) * len(shape))
    vmem = lambda *s: pltpu.VMEM(s, BF)
    wide = lambda *s: pltpu.VMEM(s, F32)
    slab_in, slab_out = (4, 2, 2, 2) + share_in, (1, 2, 2, 2) + share_out
    outs = [((rows, D), BF), ((rows, D), F32), ((rows, D), BF), ((D, D), BF)] + [(slab_in, BF), (slab_out, BF)] * (blocks - last)
    small = [((1, D), F32)] + [(share_in, F32)] * last + [(share_out, F32)]
    copies = max(Sum.COPIES * 2 * last, 1)
    scratch = [vmem(rows, D)] * 3 + [vmem(D, D), vmem(2, D, block), vmem(2, block, D), vmem(rows, D), vmem(D, rows)]
    scratch += [wide(rows, D)] * 3 + [vmem(block, rows), vmem(rows, block), vmem(blocks, *slab_in), vmem(blocks, *slab_out)]
    scratch += (Sum.scratch(4, *share_in, 0) + Sum.scratch(1, *share_out, 0)) * last
    scratch += [pltpu.SemaphoreType.DMA((copies,))] * 2 + [pltpu.SemaphoreType.DMA((6 + 2 * blocks,))]
    return pl.pallas_call(
        functools.partial(feed_forward, R, blocks),
        grid=(blocks,),
        in_specs=[whole(flag.shape)] + [anywhere] * 4 + [whole(grow.shape)] + [anywhere] * 2,
        out_specs=[anywhere] * len(outs) + [whole(s) for s, _ in small],
        out_shape=[jax.ShapeDtypeStruct(*s) for s in outs + small],
        scratch_shapes=scratch,
        compiler_params=pltpu.CompilerParams(
            vmem_limit_bytes=60 * 2**20, dimension_semantics=("arbitrary",), collective_id=2, has_side_effects=True
        ),
        name="feed_forward",
    )(flag, att, tokens, up, wo, grow, wi, wt)


def turn_plan(chains, places):
    plan = {}
    for chain, at in zip(chains, places):
        for place, stage in zip(at, chain):
            plan.setdefault(place, []).insert(0, stage)
    return plan


def together(*chains):
    def stage(s):
        def run():
            for chain in chains:
                chain[s]()

        return run

    return [stage(s) for s in range(len(chains[0]))]


def unslab(slabs, flat):
    rows = slabs.shape[4]
    for i in range(16):
        pair = [slabs[i // 4, i // 2 % 2, i % 2, x] for x in range(2)]
        flat[2 * rows * i : 2 * rows * (i + 1)] = jnp.concatenate(pair, axis=0)


def normed_rows(x, gain):
    x = x.astype(F32)
    return (x * norm_rows(x) * gain).astype(BF)


def block_chain(ats, shard_in, shard_out, j, whole_in, whole_out, sems, local, k):
    width = whole_in.shape[5]
    return [
        gather_stages(ats[0], shard_in, whole_in, sems, local.at[k], GATHER_COPIES * k, pl.ds(j * width, width)),
        gather_stages(ats[1], shard_out, whole_out, sems, local.at[k + 1], GATHER_COPIES * (k + 1), None, j),
    ]


def swapped(flag, a, b):
    turn = flag[0:1, 0:1] > 0
    return jnp.where(turn, b, a), jnp.where(turn, a, b)


def forward_kernel(R, L, S, E, pairs, *refs):
    flag, tokens, layt, lays, u = refs[:5]
    shards = refs[5:12]
    refs = list(refs[12:])
    take = lambda k: [refs.pop(0) for _ in range(k)]
    o, pa, pb, cs, grow = take(5)
    kept = take(7)
    wholes = take(6)
    kcat, qcat, vt, s_ref, ohq, xfar, xshort, flat, normed, tok, held, stats = take(12)
    q, kf, vf, ks, vs, nkt, nst = inner = take(7)
    slabs = take(4)
    send, recv, local = take(3)
    W = 2 * E
    D = tok.shape[2]
    at = Place()
    sems = (send, recv)
    ways = [(at, Place(True))[i] for i in FORWARD_WAYS]
    targets = slabs + wholes[3:]
    chains = []
    for i, cols in [(i, None) for i in range(5)] + [(i, cols) for i in (5, 6) for cols in pieces_of(shards[i].shape[1])]:
        k = len(chains)
        view = targets[i] if cols is None else targets[i].at[:, :, :, :, :, cols]
        chains.append(gather_stages(ways[k], shards[i], view, sems, local.at[k], GATHER_COPIES * k, cols))
    count = len(chains)
    chains = [together(chains[0], chains[1])] + chains[2:]
    plan = turn_plan(chains, FORWARD_AT)
    spare = GATHER_COPIES * count
    long = remote(tok.at[0], xfar, sems, spare, at.along_x())
    short = remote(tok.at[1, pl.ds(0, S)], xshort, sems, spare + 1, at.along_x())
    out = lambda i, a, b: pltpu.make_async_copy(a, b, local.at[count + i])
    weights_out = [out(i, slabs[1 + i], wholes[i]) for i in range(3)]
    kept_out = [out(3 + i, a, b) for i, (a, b) in enumerate(zip(inner, kept))]

    def send_tokens():
        long.start()
        pl.when(at.x == 0)(short.start)

    def turn(t):
        for stage in plan.get(t, []):
            stage()

    step = pl.program_id(0)
    pair = lax.rem(step, pairs)

    @pl.when(step == 0)
    def _():
        at.greet()
        turn(-9)
        tok[0], tok[1] = swapped(flag, tokens[0], tokens[1])
        send_tokens()
        for i, (base, row) in enumerate([(0, layt[0]), (L, lays[...])]):
            kcat[base : base + row.shape[1], W:] = jnp.transpose(eye_of(row, SPAN, False).astype(F32)).astype(BF)
            ohq[i] = eye_of(layt[i, :, :R], SPAN, False)
        vt[:, E:] = jnp.ones((2, vt.shape[1] - E, vt.shape[2]), BF)
        for t in range(-8, -4):
            turn(t)
        gslab = slabs[0]
        columns = jnp.concatenate(
            [gslab[i // 8, i // 4 % 2, i // 2 % 2, i % 2].astype(F32) for i in range(32)], axis=0
        )
        grow[...] = jnp.transpose(columns)[:8]
        gain = grow[0:1]
        weights_out[0].start()
        unslab(slabs[1], flat.at[0])
        for i in range(2):
            normed[i] = normed_rows(tok[i], gain)
            q[i] = (dot(normed[i], flat[0]).astype(BF).astype(F32) * 0.125).astype(BF)
        turn(-4)
        weights_out[1].start()
        unslab(slabs[2], flat.at[0])
        kf[:R] = dot(normed[0], flat[0]).astype(BF)
        turn(-3)
        weights_out[2].start()
        unslab(slabs[3], flat.at[1])
        vf[:R] = dot(normed[0], flat[1]).astype(BF)
        kept_out[0].start()
        turn(-2)

    @pl.when(step == pairs)
    def _():
        nkt[:, :R] = flipped(normed[0])
        nst[...] = flipped(normed[1])
        long.wait()

        @pl.when(at.x == 0)
        def _():
            short.wait_send()

        @pl.when(at.x == 1)
        def _():
            short.wait_recv()

        @pl.when(at.x == 0)
        def _():
            xshort[...] = tok[1, :S]

        gain = grow[0:1]
        normed[0] = normed_rows(xfar[...], gain)
        normed[1, :S] = normed_rows(xshort[...], gain)
        kf[R:] = dot(normed[0], flat[0]).astype(BF)
        vf[R:] = dot(normed[0], flat[1]).astype(BF)
        ks[...] = dot(normed[1, :S], flat[0]).astype(BF)
        vs[...] = dot(normed[1, :S], flat[1]).astype(BF)
        nkt[:, R:L] = flipped(normed[0])
        nkt[:, L:] = flipped(normed[1, :S])
        for copy in kept_out[1:]:
            copy.start()

    steps = 2 * pairs

    def tick(spot):
        for t in sorted(plan):
            if t >= 2 * steps and spot == 2 or 0 <= t < 2 * steps and t % 2 == spot:

                @pl.when(step == min(t // 2, steps - 1))
                def _(t=t):
                    turn(t)

    here = pl.ds(pl.multiple_of(pair * W, W), W)

    def attend_to(i, base, m, keys, values, into, ticking):
        ch = min(CH, m)
        kcat[base : base + m, :W] = keys
        vt[0, :E, :m], vt[1, :E, :m] = jnp.split(flipped(values), 2, axis=0)
        qt = flipped(q[i, :, here])
        found = []
        for h in range(2):
            if ticking:
                tick(h)
            toep = pltpu.roll(jnp.broadcast_to(u[0, h : h + 1], (SPAN, 2 * SPAN)), 0, 1, stride=1, stride_axis=0)
            qcat[h * E : (h + 1) * E] = qt[h * E : (h + 1) * E]
            qcat[(1 - h) * E : (2 - h) * E] = jnp.zeros((E, R), BF)
            qcat[W:] = dot(toep[:, :SPAN].astype(BF), ohq[i]).astype(BF)
            top = jnp.full((8, R), -jnp.inf, F32)
            for c in range(0, m, ch):
                s = dot(kcat[base + c : base + c + ch], qcat[...])
                s_ref[c : c + ch] = s
                top = jnp.maximum(top, jnp.max(s.reshape(ch // 8, 8, R), axis=0))
            top = jnp.max(top, axis=0, keepdims=True)
            for c in range(0, m, ch):
                into[h, c : c + ch] = jnp.exp(s_ref[c : c + ch] - top).astype(BF)
            full = dot(vt[h, :, :m], into[h, :m])
            found.append((top, full[E : E + 1], full[:E]))
        return found

    def heads(parts):
        return jnp.transpose(jnp.concatenate(parts, axis=0)).astype(BF)

    @pl.when(step < pairs)
    def _():
        found = attend_to(0, 0, R, kf[:R, here], vf[:R, here], pa.at[0], True)
        for h, (top, total, full) in enumerate(found):
            stats[pair, 2 * h : 2 * h + 1] = top
            stats[pair, 2 * h + 1 : 2 * h + 2] = total
            held[pair, h * E : (h + 1) * E] = full

    @pl.when(step >= pairs)
    def _():
        m = L - R
        found = attend_to(0, R, m, kf[R:, here], vf[R:, here], pb.at[0, :, pl.ds(0, m)], True)
        parts = []
        for h, (top, total, full) in enumerate(found):
            first, first_total = stats[pair, 2 * h : 2 * h + 1], stats[pair, 2 * h + 1 : 2 * h + 2]
            most = jnp.maximum(first, top)
            a, b = jnp.exp(first - most), jnp.exp(top - most)
            back = 1.0 / (a * first_total + b * total)
            cs[0, 0, h : h + 1] = a * back
            cs[1, 0, h : h + 1] = b * back
            parts.append(held[pair, h * E : (h + 1) * E] * (a * back) + full * (b * back))
        o[0] = heads(parts)
        found = attend_to(1, L, S, ks[:, here], vs[:, here], pb.at[0, :, pl.ds(m, S)], False)
        for h, (top, total, full) in enumerate(found):
            cs[2, 0, h : h + 1] = 1.0 / total
        o[1] = heads([full / total for _, total, full in found])

    tick(2)

    @pl.when(step == steps - 1)
    def _():
        for copy in weights_out + kept_out:
            copy.wait()


def pieces_of(width):
    return [pl.ds(i * width // FORWARD_PIECES, width // FORWARD_PIECES) for i in range(FORWARD_PIECES)]


def forward_call(flag, tokens, layt, lays, u, shards, S):
    n, R, D = tokens.shape
    L = layt.shape[2]
    pairs = u.shape[0]
    E = D // (2 * pairs)
    W = 2 * E
    KT = L + S
    whole = lambda shape: pl.BlockSpec(shape, lambda j: (0,) * len(shape))
    anywhere = pl.BlockSpec(memory_space=pl.ANY)
    vmem = lambda *s: pltpu.VMEM(s, BF)
    wide = lambda *s: pltpu.VMEM(s, F32)
    early = lambda j: jnp.minimum(j, pairs - 1)
    late = lambda j: jnp.maximum(j - pairs, 0)
    kept = [(n, R, D), (L, D), (L, D), (S, D), (S, D), (D, KT), (D, R)]
    chains = 5 + 2 * FORWARD_PIECES
    copies = GATHER_COPIES * chains + 2
    gathered = [(4, 2, 2, 2) + s.shape for s in shards]
    filled = gathered[1:]
    blocked = [
        ((n, R, D), BF, pl.BlockSpec((n, R, W), lambda j: (0, 0, late(j)))),
        ((pairs, 2, R, R), BF, pl.BlockSpec((1, 2, R, R), lambda j: (early(j), 0, 0, 0))),
        ((pairs, 2, KT - R, R), BF, pl.BlockSpec((1, 2, KT - R, R), lambda j: (late(j), 0, 0, 0))),
        ((3, pairs, 2, R), F32, pl.BlockSpec((3, 1, 2, R), lambda j: (0, late(j), 0, 0))),
        ((8, D), F32, whole((8, D))),
    ]
    return pl.pallas_call(
        functools.partial(forward_kernel, R, L, S, E, pairs),
        grid=(2 * pairs,),
        in_specs=[whole(flag.shape), whole(tokens.shape), whole(layt.shape), whole(lays.shape)]
        + [pl.BlockSpec((1, 2, 2 * SPAN), lambda j: (lax.rem(j, pairs), 0, 0))]
        + [anywhere] * 7,
        out_specs=[b[2] for b in blocked] + [anywhere] * (len(kept) + len(filled)),
        out_shape=[jax.ShapeDtypeStruct(*b[:2]) for b in blocked] + [jax.ShapeDtypeStruct(s, BF) for s in kept + filled],
        scratch_shapes=[vmem(KT, W + SPAN), vmem(W + SPAN, R), vmem(2, E + 16, R), wide(R, R), vmem(n, SPAN, R)]
        + [vmem(R, D), vmem(S, D), vmem(2, D, D), vmem(n, R, D), vmem(n, R, D), wide(pairs, W, R), wide(pairs, 8, R)]
        + [vmem(*s) for s in kept]
        + [vmem(*s) for s in gathered[:4]]
        + [pltpu.SemaphoreType.DMA((copies,))] * 2
        + [pltpu.SemaphoreType.DMA((chains + 10,))],
        compiler_params=pltpu.CompilerParams(
            vmem_limit_bytes=60 * 2**20, dimension_semantics=("arbitrary",), collective_id=0, has_side_effects=True
        ),
        name="forward",
    )(flag, tokens, layt, lays, u, *shards)


class Sum:
    COPIES = 7

    def __init__(self, at, part, total, scratch, sems, local, base, cols=None, plane=None):
        self.at, self.part, self.total, self.sems, self.base, self.plane = at, part, total, sems, base, plane
        self.cols = pl.ds(0, total.shape[1]) if cols is None else cols
        self.acc, self.got_diag, self.got_one, self.got_two, self.got_z = scratch[:5]
        self.held = scratch[5] if len(scratch) > 5 else None
        if self.held is not None:
            self.keep = pltpu.make_async_copy(part.at[:, :, at.c, :, :, self.cols], self.held, local)
        self.stages = [self.one, self.two, self.three, self.four, self.five]

    @staticmethod
    def scratch(depth, rows, columns, held):
        slab = (rows, columns)
        shapes = [(depth, 2, 2) + slab] + [(depth,) + slab] * 3 + [(3,) + slab] + [(depth, 2, 2) + slab] * held
        return [pltpu.VMEM(s, BF) for s in shapes]

    def send(self, k):
        at, acc = self.at, self.acc
        if k > 3:
            d = k - 3
            src, dst, device = acc.at[(at.z + d) % 4, at.y, at.x], self.got_z.at[d - 1], at.along_z(d)
        else:
            src, dst, device = [
                (self.part.at[:, :, 1 - at.c, :, :, self.cols], acc, at.core()),
                (acc.at[:, 1 - at.y, 1 - at.x], self.got_diag, at.second()),
                (acc.at[:, at.y2, at.x2], self.got_two, at.second()),
                (acc.at[:, at.y1, at.x1], self.got_one, at.first()),
            ][k]
        return remote(src, dst, self.sems, self.base + k, device)

    def to_plane(self):
        at = self.at
        d = (self.plane - at.z + 4) % 4
        k = self.base + 3 + d
        return pltpu.make_async_remote_copy(
            src_ref=self.acc.at[0, at.y, at.x],
            dst_ref=self.got_z.at[d - 1],
            send_sem=self.sems[0].at[k],
            recv_sem=self.sems[1].at[k],
            device_id=at.device(self.plane, at.y, at.c, at.x),
            device_id_type=MESH,
        )

    def one(self):
        self.send(0).start()
        if self.held is not None:
            self.keep.start()

    def two(self):
        at, acc = self.at, self.acc
        if self.held is not None:
            self.keep.wait()
        self.send(0).wait_recv()

        def add(i, _):
            for yy in range(2):
                own = self.held[i, yy] if self.held is not None else self.part[i, yy, at.c, :, :, self.cols]
                acc[i, yy] = (acc[i, yy].astype(F32) + own.astype(F32)).astype(BF)
            return 0

        lax.fori_loop(0, acc.shape[0], add, 0)
        self.send(1).start()
        self.send(2).start()

    def three(self):
        at, acc = self.at, self.acc
        self.send(1).wait_recv()
        acc[:, at.y1, at.x1] = (acc[:, at.y1, at.x1].astype(F32) + self.got_diag[...].astype(F32)).astype(BF)
        self.send(3).start()

    def four(self):
        at, acc = self.at, self.acc
        self.send(2).wait_recv()
        self.send(3).wait_recv()
        mine = acc[:, at.y, at.x].astype(F32) + self.got_one[...].astype(F32) + self.got_two[...].astype(F32)
        acc[:, at.y, at.x] = mine.astype(BF)
        if self.plane is None:
            for k in (4, 5, 6):
                self.send(k).start()
        else:

            @pl.when(at.z != self.plane)
            def _():
                self.to_plane().start()

    def five(self):
        at = self.at

        def collect():
            out = self.acc[at.z if self.plane is None else 0, at.y, at.x].astype(F32)
            for d in (1, 2, 3):
                arrival = remote(self.got_z.at[d - 1], self.got_z.at[d - 1], self.sems, self.base + 3 + d, at.along_z(d))
                arrival.wait_recv()
                out = out + self.got_z[d - 1].astype(F32)
            self.total[:, self.cols] = out

        for k in range(4):
            self.send(k).wait_send()
        if self.plane is None:
            collect()
            for k in (4, 5, 6):
                self.send(k).wait_send()
        else:
            pl.when(at.z == self.plane)(collect)

            @pl.when(at.z != self.plane)
            def _():
                self.to_plane().wait_send()


def into_slabs(flat, slabs):
    rows = slabs.shape[4]
    for i in range(32):
        slabs[i // 8, i // 4 % 2, i // 2 % 2, i % 2] = flat[rows * i : rows * (i + 1)].astype(BF)


def backward_kernel(R, L, S, E, pairs, planes, *refs):
    flag, q, kf, vf, ks, vs, o, do, pa, pb, cs, layt, lays = refs[:13]
    refs = list(refs[13:])
    take = lambda k: [refs.pop(0) for _ in range(k)]
    parts = take(len(planes))
    nkt_, nst_, wq, wk, wv, tok, dres, grow, dg2 = take(9)
    gtok, small_total = take(2)
    totals = take(3 + len(planes))
    kq, vaug, rhs, ds, ohq, nacc, qm, dm, held = take(9)
    dq, dk, dv, nkt, nst, ws, toks, dress = take(8)
    far, fars, gfar, gshort, ends = take(5)
    tsum, small, small_held, small_got = take(4)
    send, recv, local = take(3)
    W = 2 * E
    D = ws.shape[1]
    at = Place()
    sems = (send, recv)
    sums = []

    def summed(part, total, held, plane=None):
        i = len(sums)
        sums.append(Sum(at, part, total, take(5 + held), sems, local.at[i], Sum.COPIES * i, None, plane))

    for part, total, plane in zip(parts, totals, planes):
        summed(part, total, 1, plane)
    early = len(sums)
    mats = take(3)
    for part, total in zip(mats, totals[early:]):
        summed(part, total, 0)
    base = Sum.COPIES * len(sums)
    small_chain = small_stages(at, small, small_total, small_held, small_got, sems, base)
    long = remote(far, gfar, sems, base + 6, at.along_x())
    short = remote(fars, gshort, sems, base + 7, at.along_x())
    loads = [(w, ws.at[i]) for i, w in enumerate((wq, wk, wv))] + [(nkt_, nkt), (nst_, nst), (tok, toks), (dres, dress)]
    loads = [pltpu.make_async_copy(a, b, local.at[len(sums) + i]) for i, (a, b) in enumerate(loads)]

    step = pl.program_id(0)
    pair = lax.rem(step, pairs)
    steps = 2 * pairs
    plan = {}
    for i in range(early):
        for s in range(5):
            when = 0 if s == 0 else int(BACK_SUM[0] + BACK_SUM[1] * i + BACK_SUM[2] * (s - 1))
            plan.setdefault(when, []).insert(0, sums[i].stages[s])

    def tick(spot):
        for t in plan:
            if t < 2 * steps and t % 2 == spot:

                @pl.when(step == t // 2)
                def _(t=t):
                    for stage in plan[t]:
                        stage()

    @pl.when(step == 0)
    def _():
        at.greet()
        for load in loads:
            load.start()
        for i, (base, row) in enumerate([(0, layt[0]), (L, lays[...])]):
            kq[:SPAN, base : base + row.shape[1]] = eye_of(row, SPAN, True)
            ohq[i] = jnp.transpose(eye_of(layt[i, :, :R], SPAN, False).astype(F32)).astype(BF)
        vaug[:, W:] = (lax.broadcasted_iota(jnp.int32, (R, W), 1) < 2).astype(F32).astype(BF)
        rhs[...] = jnp.zeros_like(rhs)

    @pl.when(step == pairs)
    def _():
        for load in loads[:3]:
            load.wait()
        far[...] = (dot_nt(dk[R:L], ws[1]) + dot_nt(dv[R:L], ws[2])).astype(BF)
        long.start()
        ends[...] = dot_nt(dk[L:], ws[1]) + dot_nt(dv[L:], ws[2])
        fars[...] = ends[...].astype(BF)
        pl.when(at.x == 1)(short.start)

    nacc[...] = jnp.zeros_like(nacc)
    lane = lax.broadcasted_iota(jnp.int32, (R, W), 1)
    spot = lax.broadcasted_iota(jnp.int32, (16, R), 0)
    here = pl.ds(pl.multiple_of(pair * W, W), W)

    def attend_to(i, base, m, keys, values, p, scale, ticking):
        ch = min(CH, m)
        vaug[:m, :W] = values
        kt = flipped(keys)
        dot_, ot = jnp.transpose(do[i].astype(F32)), jnp.transpose(o[i].astype(F32))
        scaled = [(dot_[h * E : (h + 1) * E] * cs[scale, 0, h : h + 1]).astype(BF) for h in range(2)]
        don = flipped(jnp.concatenate(scaled, axis=0))
        qq = q[i]
        zero = jnp.zeros((R, W), BF)
        for h in range(2):
            mine = (lane < E) if h == 0 else (lane >= E)
            qm[h * R : (h + 1) * R] = jnp.where(mine, qq, zero)
            dm[h * R : (h + 1) * R] = jnp.where(mine, don, zero)
        dqs = []
        for h in range(2):
            if ticking:
                tick(h)
            rhs[h * E : (h + 1) * E] = scaled[h]
            rhs[(1 - h) * E : (2 - h) * E] = jnp.zeros((E, R), BF)
            delta = jnp.sum(scaled[h].astype(F32) * ot[h * E : (h + 1) * E], axis=0, keepdims=True)
            hi = delta.astype(BF).astype(F32)
            rhs[W : W + 16] = jnp.where(spot == 0, -hi, jnp.where(spot == 1, hi - delta, 0.0)).astype(BF)
            for c in range(0, m, ch):
                g = dot(vaug[c : c + ch], rhs[...])
                ds[c : c + ch, h * R : (h + 1) * R] = (p[h, c : c + ch].astype(F32) * g).astype(BF)
            kq[SPAN:, base : base + m] = kt[h * E : (h + 1) * E]
            both = dot(kq[:, base : base + m], ds[:m, h * R : (h + 1) * R])
            dqs.append(both[SPAN:] * 0.125)
            nacc[h] += dot(both[:SPAN].astype(BF), ohq[i])
        for c in range(0, m, ch):
            dk[base + c : base + c + ch, here] = dot(ds[c : c + ch], qm[...]).astype(BF)
            both = dot(p[0, c : c + ch], dm[:R]) + dot(p[1, c : c + ch], dm[R:])
            dv[base + c : base + c + ch, here] = both.astype(BF)
        return jnp.concatenate(dqs, axis=0)

    def diagonals(h):
        wide = jnp.concatenate([nacc[h], jnp.zeros((SPAN, SPAN), F32)], axis=1)
        return jnp.sum(pltpu.roll(wide, 0, 1, stride=1, stride_axis=0), axis=0, keepdims=True)

    @pl.when(step < pairs)
    def _():
        m = L - R
        held[pair] = attend_to(0, R, m, kf[R:], vf[R:], pb.at[0, :, pl.ds(0, m)], 1, True)
        dq[1, :, here] = flipped(attend_to(1, L, S, ks[...], vs[...], pb.at[0, :, pl.ds(m, S)], 2, False))
        for h in range(2):
            tsum[2 * pair + h] = diagonals(h)

    @pl.when(step >= pairs)
    def _():
        dq[0, :, here] = flipped(held[pair] + attend_to(0, 0, R, kf[:R], vf[:R], pa.at[0], 0, True))
        for h in range(2):
            tsum[2 * pair + h] = tsum[2 * pair + h] + diagonals(h)

    @pl.when(step == steps - 1)
    def _():
        rest = [stage for t in sorted(plan) if t >= 2 * steps for stage in plan[t]]

        def some(count):
            for _ in range(min(count, len(rest))):
                rest.pop(0)()

        for load in loads[3:]:
            load.wait()
        later = sums[early:]
        into_slabs(dot(nkt[...], dv[...]), mats[2])
        later[2].one()
        some(2)
        into_slabs(dot(nkt[...], dk[...]), mats[1])
        later[1].one()
        some(2)
        into_slabs(dot(nkt[:, :R], dq[0]) + dot(nst[...], dq[1]), mats[0])
        later[0].one()
        some(100)
        later[2].two()
        toks[0], toks[1] = swapped(flag, toks[0], toks[1])
        own = [dot_nt(dq[0], ws[0]) + dot_nt(dk[:R], ws[1]) + dot_nt(dv[:R], ws[2]), dot_nt(dq[1], ws[0])]
        later[1].two()
        later[2].three()
        long.wait()
        pl.when(at.x == 1)(short.wait_send)
        pl.when(at.x == 0)(short.wait_recv)
        gain = grow[0:1]
        keys = jnp.where(at.x == 0, ends[...] + gshort[...].astype(F32), 0.0)
        total = jnp.zeros((1, D), F32)
        for i in range(2):
            d = own[i] + (gfar[...].astype(F32) if i == 0 else jnp.concatenate([keys, jnp.zeros((R - S, D), F32)], axis=0))
            x = toks[i].astype(F32)
            back = norm_rows(x)
            a = gain * d
            total = total + jnp.sum(d * x * back, axis=0, keepdims=True)
            part = back * a - x * (back * back * back) * jnp.mean(a * x, axis=1, keepdims=True)
            toks[i] = (dress[i * R : (i + 1) * R] + part).astype(BF)
        toks[0], toks[1] = swapped(flag, toks[0], toks[1])
        finish = pltpu.make_async_copy(toks, gtok, local.at[len(sums) + len(loads)])
        finish.start()
        small[...] = jnp.zeros_like(small)
        lines = D // 128
        for i in range(lines):
            small[i : i + 1] = total[:, 128 * i : 128 * (i + 1)]
            small[lines + i : lines + i + 1] = dg2[:, 128 * i : 128 * (i + 1)]
        for h in range(2 * pairs):
            for i in range(4):
                spots = 2 * lines + 4 * h + i
                small[spots : spots + 1] = tsum[h, :, 128 * i : 128 * (i + 1)]
        small_chain[0]()
        later[0].two()
        later[1].three()
        small_chain[1]()
        later[2].four()
        later[0].three()
        small_chain[2]()
        later[1].four()
        small_chain[3]()
        later[0].four()
        for s in later[::-1]:
            s.five()
        small_chain[4]()
        finish.wait()


def backward_call(flag, q, kf, vf, ks, vs, o, do, pa, pb, cs, layt, lays, parts, planes, nkt, nst, wq, wk, wv, tok, dres, grow, dg2):
    n, R, D = q.shape
    L, S = kf.shape[0], ks.shape[0]
    pairs = pa.shape[0]
    E = D // (2 * pairs)
    W = 2 * E
    KT = L + S
    whole = lambda a: pl.BlockSpec(a.shape, lambda j: (0,) * len(a.shape))
    anywhere = pl.BlockSpec(memory_space=pl.ANY)
    early = lambda j: jnp.minimum(j, pairs - 1)
    late = lambda j: jnp.maximum(j - pairs, 0)
    rows = pl.BlockSpec((n, R, W), lambda j: (0, 0, lax.rem(j, pairs)))
    keys = lambda a: pl.BlockSpec((a.shape[0], W), lambda j: (0, lax.rem(j, pairs)))
    shares = [p_.shape[4:] for p_ in parts] + [(D // 32, D)] * 3
    lines = -(-(2 * D // 128 + 8 * pairs) // 8) * 8
    outs = [jax.ShapeDtypeStruct((n, R, D), BF), jax.ShapeDtypeStruct((lines, 128), F32)]
    outs += [jax.ShapeDtypeStruct(s, F32) for s in shares]
    vmem = lambda *s: pltpu.VMEM(s, BF)
    wide = lambda *s: pltpu.VMEM(s, F32)
    scratch = [vmem(SPAN + E, KT), vmem(R, 2 * W), vmem(2 * W, R), vmem(R, 2 * R), vmem(n, R, SPAN)]
    scratch += [wide(2, SPAN, SPAN), vmem(2 * R, W), vmem(2 * R, W), wide(pairs, W, R)]
    scratch += [vmem(n, R, D), vmem(KT, D), vmem(KT, D), vmem(D, KT), vmem(D, R)]
    scratch += [vmem(3, D, D), vmem(n, R, D), wide(n * R, D)]
    scratch += [vmem(R, D), vmem(S, D), vmem(R, D), vmem(S, D), wide(S, D)]
    scratch += [wide(2 * pairs, 1, 2 * SPAN), wide(lines, 128), wide(4, lines, 128), wide(6, lines, 128)]
    chunks = [(p_.shape[0],) + p_.shape[4:] for p_ in parts]
    copies = Sum.COPIES * (len(chunks) + 3) + 8
    scratch += [pltpu.SemaphoreType.DMA((copies,)), pltpu.SemaphoreType.DMA((copies,)), pltpu.SemaphoreType.DMA((len(chunks) + 12,))]
    scratch += sum([Sum.scratch(*s, 1) for s in chunks], [])
    scratch += [vmem(4, 2, 2, 2, D // 32, D)] * 3
    scratch += sum([Sum.scratch(4, *s, 0) for s in shares[len(parts):]], [])
    return pl.pallas_call(
        functools.partial(backward_kernel, R, L, S, E, pairs, planes),
        grid=(2 * pairs,),
        in_specs=[whole(flag), rows, keys(kf), keys(vf), keys(ks), keys(vs), rows, rows]
        + [pl.BlockSpec((1, 2, R, R), lambda j: (late(j), 0, 0, 0)), pl.BlockSpec((1, 2, KT - R, R), lambda j: (early(j), 0, 0, 0))]
        + [pl.BlockSpec((3, 1, 2, R), lambda j: (0, lax.rem(j, pairs), 0, 0)), whole(layt), whole(lays)]
        + [anywhere] * (len(parts) + 7)
        + [whole(grow), whole(dg2)],
        out_specs=[anywhere] + [whole(s) for s in outs[1:]],
        out_shape=outs,
        scratch_shapes=scratch,
        compiler_params=pltpu.CompilerParams(
            vmem_limit_bytes=60 * 2**20, dimension_semantics=("arbitrary",), collective_id=1, has_side_effects=True
        ),
        name="backward",
    )(flag, q, kf, vf, ks, vs, o, do, pa, pb, cs, layt, lays, *parts, nkt, nst, wq, wk, wv, tok, dres, grow, dg2)


EPSILON = 1e-06
THRESHOLDS = (12, 16, 23, 32, 46, 64, 91)
BOTH = ("dp", "blk")


def bucket_np(relative):
    magnitude = np.abs(relative)
    larger = 8 + sum((magnitude >= limit).astype(np.int64) for limit in THRESHOLDS)
    return np.where(magnitude < 8, magnitude, larger) + 16 * (relative > 0)


def bucket_rows(distance, buckets):
    return (bucket_np(distance)[:, None] == np.arange(buckets)[None, :]).astype(np.float32)


def norm_parts(x, gain):
    back = lax.rsqrt(jnp.mean(x * x, axis=-1, keepdims=True) + EPSILON)
    return (x * back * gain).astype(BF), back


def norm_back(d, x, back, gain):
    a = gain * d
    grad_gain = jnp.sum(d * x * back, axis=0)
    return back * a - x * back**3 * jnp.mean(a * x, axis=-1, keepdims=True), grad_gain


def mm(a, b, dims):
    return lax.dot_general(a, b, (dims, ((), ())), preferred_element_type=F32)


def gather_weights(gain_one, wq, wk, wv, wo, gain_two, wi, wt):
    full = lambda a: lax.all_gather(a, BOTH, axis=0, tiled=True)
    packed = full(jnp.concatenate([wq, wk, wv, wo, wi], axis=1))
    width = wq.shape[1]
    gains = full(jnp.stack([gain_one, gain_two], axis=1))
    return packed[:, : 3 * width], packed[:, 3 * width : 4 * width], packed[:, 4 * width :], full(wt), gains[:, 0], gains[:, 1]


def scatter_sums(dqkv, dwo, dwi, dwt, dg1, dg2):
    take = lambda a: lax.psum_scatter(a, BOTH, scatter_dimension=0, tiled=True)
    width = dwo.shape[1]
    packed = take(jnp.concatenate([dqkv, dwo, dwi], axis=1).astype(BF)).astype(F32)
    gains = take(jnp.stack([dg1, dg2], axis=1))
    parts = [packed[:, i * width : (i + 1) * width] for i in range(4)]
    return parts, packed[:, 4 * width :], take(dwt.astype(BF)).astype(F32), gains[:, 0], gains[:, 1]


def on_any_device(tokens, layout, lengths, gain_one, wq, wk, wv, wo, gain_two, wi, wt, table, grad_out):
    n, R, D = tokens.shape
    H = table.shape[1]
    G = lax.axis_size("blk")
    me = lax.axis_index("blk")
    L = layout.shape[1]
    S = L // 8
    order = jnp.argsort(-lengths, stable=True)
    place = jnp.argsort(order)
    tok = tokens[order]
    gout = grad_out[order]
    lay = layout[order]
    lens = lengths[order]

    def from_step(x, s):
        return lax.ppermute(x, "blk", [(i, (i - s) % G) for i in range(G)])

    pieces = [tok[:-1]] + [from_step(tok[:-1], s) for s in range(1, G)]
    xf = jnp.concatenate(pieces, axis=1)
    first = tok[-1, :S]
    xs = jnp.where(me == 0, first, sum(lax.ppermute(first, "blk", [(0, i)]) for i in range(1, G)))
    lay_turned = jnp.roll(lay, -me * R, axis=1)
    layq = lay_turned[:, None, :R]
    layf = lay_turned[:-1, None, :]
    lays = lay[-1:, :S]
    spots = (jnp.arange(L) + me * R) % L
    mask = jnp.where(spots[None, :, None] < lens[:-1, None, None], 0.0, -1e30).astype(F32)

    wqkv, wo_all, wi_all, wt_all, g1, g2 = gather_weights(gain_one, wq, wk, wv, wo, gain_two, wi, wt)
    g1 = g1.astype(F32)
    g2 = g2.astype(F32)
    hidden = tok.reshape(n * R, D).astype(F32)
    normed, r1 = norm_parts(hidden, g1)
    xkeys = jnp.concatenate([xf.reshape((n - 1) * L, D), xs], axis=0)
    nkeys, _ = norm_parts(xkeys.astype(F32), g1)
    q = (mm(normed, wqkv[:, :D], ((1,), (0,))).astype(BF) * jnp.asarray(0.125, BF)).reshape(n, R, D)
    k = mm(nkeys, wqkv[:, D : 2 * D], ((1,), (0,))).astype(BF)
    v = mm(nkeys, wqkv[:, 2 * D :], ((1,), (0,))).astype(BF)
    cut = (n - 1) * L
    kf, ks = k[:cut].reshape(n - 1, L, D), k[cut:]
    vf, vs = v[:cut].reshape(n - 1, L, D), v[cut:]
    lane = np.arange(2 * SPAN)
    turned = np.where(lane >= SPAN, lane - 2 * SPAN, lane)
    urow = mm(table, bucket_rows(-turned, table.shape[0]).astype(BF), ((0,), (1,))).reshape(H // 2, 2, 2 * SPAN)
    o, p, l = attend_call(q, kf, vf, ks, vs, layq, layf, lays, mask, urow)

    attended = o.reshape(n * R, D)
    resid = hidden + mm(attended, wo_all, ((1,), (0,)))
    normed_two, r2 = norm_parts(resid, g2)
    pre = mm(normed_two, wi_all, ((1,), (0,)))
    act, act_back = jax.vjp(lambda x: jax.nn.gelu(x, approximate=False), pre)
    act = act.astype(BF)
    mixed = (resid + mm(act, wt_all, ((1,), (0,)))).astype(BF)
    up = gout.reshape(n * R, D)
    dwt = mm(act, up, ((0,), (0,)))
    (dpre,) = act_back(mm(up, wt_all, ((1,), (1,))))
    dpre = dpre.astype(BF)
    dwi = mm(normed_two, dpre, ((0,), (0,)))
    dn2 = mm(dpre, wi_all, ((1,), (1,)))
    dresid, dg2 = norm_back(dn2, resid, r2, g2)
    dresid = dresid + up.astype(F32)
    low = dresid.astype(BF)
    dwo = mm(attended, low, ((0,), (0,)))
    datt = mm(low, wo_all, ((1,), (1,))).astype(BF).reshape(n, R, D)

    dq, dkf, dvf, dks, dvs, t = attend_back_call(q, kf, vf, ks, vs, layq, layf, lays, o, datt, p, l)
    dtable = jnp.einsum(
        "hj,jb->bh", t.reshape(H, 2 * SPAN), bucket_rows(SPAN - 1 - lane, table.shape[0]), precision=lax.Precision.HIGHEST
    )
    dq = dq.reshape(n * R, D)
    dk = jnp.concatenate([dkf.reshape(cut, D), dks], axis=0)
    dv = jnp.concatenate([dvf.reshape(cut, D), dvs], axis=0)
    dnk = mm(dk, wqkv[:, D : 2 * D], ((1,), (1,))) + mm(dv, wqkv[:, 2 * D :], ((1,), (1,)))
    dnf = dnk[:cut].reshape(n - 1, L, D)
    dns = dnk[cut:].astype(BF)
    far = sum(
        lax.ppermute(dnf[:, s * R : (s + 1) * R].astype(BF), "blk", [(i, (i + s) % G) for i in range(G)]).astype(F32)
        for s in range(1, G)
    )
    near = jnp.where(
        me == 0, dnk[cut:] + sum(lax.ppermute(dns, "blk", [(i, 0)]).astype(F32) for i in range(1, G)), 0.0
    )
    extra = jnp.concatenate([dnf[:, :R] + far, jnp.pad(near, ((0, R - S), (0, 0)))[None]], axis=0).reshape(n * R, D)
    dn1 = mm(dq, wqkv[:, :D], ((1,), (1,))) + extra
    dwq = mm(normed, dq, ((0,), (0,)))
    dwk = mm(nkeys, dk, ((0,), (0,)))
    dwv = mm(nkeys, dv, ((0,), (0,)))
    dx, dg1 = norm_back(dn1, hidden, r1, g1)
    gtok = (dresid + dx).astype(BF)
    parts, gwi, gwt, gg1, gg2 = scatter_sums(jnp.concatenate([dwq, dwk, dwv], axis=1), dwo, dwi, dwt, dg1, dg2)
    dtable = lax.psum(dtable, BOTH)
    return (
        mixed.reshape(n, R, D)[place],
        gtok.reshape(n, R, D)[place],
        gg1,
        parts[0],
        parts[1],
        parts[2],
        parts[3],
        gg2,
        gwi,
        gwt,
        dtable,
    )


def on_device(tokens, layout, lengths, gain_one, wq, wk, wv, wo, gain_two, wi, wt, table, grad_out):
    n, R, D = tokens.shape
    H = table.shape[1]
    G = lax.axis_size("blk")
    me = lax.axis_index("blk")
    L = layout.shape[1]
    S = L // 8
    swap = lengths[0] < lengths[1]
    flag = jnp.broadcast_to(swap.astype(jnp.int32), (8, 128))
    lay = jnp.where(swap, layout[::-1], layout)
    layt = jnp.where(me == 0, lay, jnp.roll(lay, R, axis=1))[:, None, :]
    lays = lay[1:, :S]
    lane = np.arange(2 * SPAN)
    turned = np.where(lane >= SPAN, lane - 2 * SPAN, lane)
    urow = mm(table, bucket_rows(-turned, table.shape[0]).astype(BF), ((0,), (1,))).reshape(H // 2, 2, 2 * SPAN)
    gains = jnp.pad(jnp.stack([gain_one, gain_two], axis=1), ((0, 0), (0, 126)))
    o, pa, pb, cs, grow, q, kf, vf, ks, vs, nkt, nst, *wholes = forward_call(
        flag, tokens, layt, lays, urow, [gains, wq, wk, wv, wo, wi, wt], S
    )
    flat = lambda a: a.reshape(-1, a.shape[-1])
    wq_all, wk_all, wv_all, wo_all, wi_all, wt_all = [flat(a) for a in wholes]
    rows = lambda a: a.reshape(n * R, D)
    mixed, dresid, datt, dwo, *handed = feed_forward_call(
        flag, rows(o), rows(tokens), rows(grad_out), wo_all, grow, wi_all, wt_all
    )
    count = 2 * (4 - FF_SUMS)
    dg2, done = handed[count], handed[count + 1 :]
    planes = sum([(None, j) for j in range(FF_SUMS, 4)], ()) + (None,)
    gtok, small, *sums = backward_call(
        flag, q, kf, vf, ks, vs, o, datt.reshape(n, R, D), pa, pb, cs, layt, lays,
        handed[:count] + [dwo.reshape(4, 2, 2, 2, -1, D)], planes,
        nkt, nst, wq_all, wk_all, wv_all, tokens, dresid, grow, dg2,
    )
    gwo, gwq, gwk, gwv = sums[count:]
    gwi = jnp.concatenate(done[:FF_SUMS] + sums[0:count:2], axis=1)
    gwt = done[FF_SUMS]
    for j in range(FF_SUMS, 4):
        gwt = jnp.where(lax.axis_index("dp") // 4 == j, sums[2 * (j - FF_SUMS) + 1], gwt)
    small = small.reshape(-1)
    mine = (lax.axis_index("dp") * G + me) * (D // 32)
    gg1, gg2 = [lax.dynamic_slice_in_dim(small, mine + i * D, D // 32) for i in range(2)]
    t = small[2 * D : 2 * D + H * 2 * SPAN].reshape(H, 2 * SPAN)
    dtable = jnp.einsum(
        "hj,jb->bh", t, bucket_rows(SPAN - 1 - lane, table.shape[0]), precision=lax.Precision.HIGHEST
    )
    return mixed.reshape(n, R, D), gtok, gg1, gwq, gwk, gwv, gwo, gg2, gwi, gwt, dtable


def solution(mesh):
    rows = P(BOTH, None)
    items = P("dp", "blk", None)
    known = dict(mesh.shape) == {"dp": 16, "blk": 2}

    def body(tokens, *rest):
        return (on_device if known and tokens.shape[0] == 2 else on_any_device)(tokens, *rest)

    return jax.shard_map(
        body,
        mesh=mesh,
        in_specs=(items, P("dp", None), P("dp"), P(BOTH), rows, rows, rows, rows, P(BOTH), rows, rows, P(), items),
        out_specs=(items, items, P(BOTH), rows, rows, rows, rows, P(BOTH), rows, rows, P()),
        check_vma=False,
    )
```

```python
import functools
import math

import jax
import jax.numpy as jnp
import numpy as np
from jax import lax
from jax.experimental import pallas as pl
from jax.experimental.pallas import tpu as pltpu
from jax.sharding import PartitionSpec as P

F32=jnp.float32; BF=jnp.bfloat16
SPAN=256
CH=256
def dot(a,b): return lax.dot_general(a,b,(((1,),(0,)),((),())),preferred_element_type=F32)
def eye_of(row, width, reverse):
    spots=lax.broadcasted_iota(jnp.int32,(width,row.shape[1]),0)
    if reverse: spots=width-1-spots
    return (spots==row).astype(F32).astype(BF)

def attend(n,L,S,R,E, q,kf,vf,ks,vs,layq,layf,lays,mask,u,o,p,l, kcat,qcat,vt,s_ref,ohq):
    W=2*E
    spans=[L]*(n-1)+[S]
    @pl.when(pl.program_id(0)==0)
    def _():
        base=0
        for i,m in enumerate(spans):
            row=layf[i] if i<n-1 else lays[...]
            kcat[base:base+m,W:]=jnp.transpose(eye_of(row,SPAN,False).astype(F32)).astype(BF)
            ohq[i]=eye_of(layq[i],SPAN,False)
            base+=m
        vt[:,E:]=jnp.ones((2,vt.shape[1]-E,vt.shape[2]),BF)
    pair=pl.program_id(0)
    base=0
    for i,m in enumerate(spans):
        ch=min(CH,m)
        kcat[base:base+m,:W]=kf[i] if i<n-1 else ks[...]
        v=vf[i] if i<n-1 else vs[...]
        vtr=jnp.transpose(v.astype(F32)).astype(BF)
        vt[0,:E,:m]=vtr[:E]
        vt[1,:E,:m]=vtr[E:]
        qt=jnp.transpose(q[i].astype(F32)).astype(BF)
        outs=[]
        for h in range(2):
            urow=u[pl.ds(0,1),h,:] if False else u[0,h:h+1,:]
            toep=pltpu.roll(jnp.broadcast_to(urow,(SPAN,2*SPAN)),0,1,stride=1,stride_axis=0)[:,:SPAN].astype(BF)
            qcat[h*E:(h+1)*E]=qt[h*E:(h+1)*E]
            qcat[(1-h)*E:(2-h)*E]=jnp.zeros((E,R),BF)
            qcat[W:]=dot(toep,ohq[i]).astype(BF)
            m8=jnp.full((8,R),-jnp.inf,F32)
            for c in range(0,m,ch):
                s=dot(kcat[base+c:base+c+ch],qcat[...])
                if 0<i<n-1: s=s+mask[i,c:c+ch,:]
                s_ref[c:c+ch]=s
                m8=jnp.maximum(m8,jnp.max(s.reshape(ch//8,8,R),axis=0))
            top=jnp.max(m8,axis=0,keepdims=True)
            for c in range(0,m,ch):
                p[0,h,base+c:base+c+ch]=jnp.exp(s_ref[c:c+ch]-top).astype(BF)
            full=dot(vt[h,:,:m],p[0,h,base:base+m])
            total=full[E:E+1]
            l[i,0,h:h+1]=total
            outs.append(full[:E]/total)
        o[i]=jnp.transpose(jnp.concatenate(outs,axis=0)).astype(BF)
        base+=m

def attend_call(q,kf,vf,ks,vs,layq,layf,lays,mask,u):
    n,R,D=q.shape; L=kf.shape[1]; S=ks.shape[0]; H=u.shape[0]*2; E=D//H; W=2*E
    KT=(n-1)*L+S
    full=lambda a: pl.BlockSpec(a.shape,lambda j:(0,)*a.ndim)
    return pl.pallas_call(functools.partial(attend,n,L,S,R,E),
      grid=(H//2,),
      in_specs=[pl.BlockSpec((n,R,W),lambda j:(0,0,j)),
        pl.BlockSpec((n-1,L,W),lambda j:(0,0,j)),pl.BlockSpec((n-1,L,W),lambda j:(0,0,j)),
        pl.BlockSpec((S,W),lambda j:(0,j)),pl.BlockSpec((S,W),lambda j:(0,j)),
        full(layq),full(layf),full(lays),full(mask),pl.BlockSpec((1,2,2*SPAN),lambda j:(j,0,0))],
      out_specs=[pl.BlockSpec((n,R,W),lambda j:(0,0,j)),
        pl.BlockSpec((1,2,KT,R),lambda j:(j,0,0,0)),
        pl.BlockSpec((n,1,2,R),lambda j:(0,j,0,0))],
      out_shape=[jax.ShapeDtypeStruct((n,R,D),BF),jax.ShapeDtypeStruct((H//2,2,KT,R),BF),jax.ShapeDtypeStruct((n,H//2,2,R),F32)],
      scratch_shapes=[pltpu.VMEM((KT,W+SPAN),BF),pltpu.VMEM((W+SPAN,R),BF),pltpu.VMEM((2,E+16,L),BF),pltpu.VMEM((L,R),F32),pltpu.VMEM((n,SPAN,R),BF)],
      compiler_params=pltpu.CompilerParams(vmem_limit_bytes=56*2**20,dimension_semantics=("arbitrary",)),
      name="attend",
    )(q,kf,vf,ks,vs,layq,layf,lays,mask,u)

def attend_back(n,L,S,R,E, q,kf,vf,ks,vs,layq,layf,lays,o,do,p,l, dq,dkf,dvf,dks,dvs,t, kq,vaug,rhs,ds,ohq,nacc,qm,dm):
    W=2*E
    spans=[L]*(n-1)+[S]
    @pl.when(pl.program_id(0)==0)
    def _():
        base=0
        for i,m in enumerate(spans):
            row=layf[i] if i<n-1 else lays[...]
            kq[:SPAN,base:base+m]=eye_of(row,SPAN,True)
            ohq[i]=jnp.transpose(eye_of(layq[i],SPAN,False).astype(F32)).astype(BF)
            base+=m
        vaug[:,W:]=(lax.broadcasted_iota(jnp.int32,(vaug.shape[0],W),1)<2).astype(F32).astype(BF)
        rhs[...]=jnp.zeros_like(rhs)
    nacc[...]=jnp.zeros_like(nacc)
    base=0
    lane=lax.broadcasted_iota(jnp.int32,(R,W),1)
    for i,m in enumerate(spans):
        ch=min(CH,m)
        kk=kf[i] if i<n-1 else ks[...]
        vaug[:m,:W]=vf[i] if i<n-1 else vs[...]
        kt=jnp.transpose(kk.astype(F32)).astype(BF)
        dot_=jnp.transpose(do[i].astype(F32))
        ot=jnp.transpose(o[i].astype(F32))
        scaled=[];
        for h in range(2):
            inv=1.0/l[i,0,h:h+1]
            scaled.append((dot_[h*E:(h+1)*E]*inv).astype(BF))
        sc=jnp.concatenate(scaled,axis=0)
        don=jnp.transpose(sc.astype(F32)).astype(BF)
        qq=q[i]
        zero=jnp.zeros((R,W),BF)
        for h in range(2):
            mine=(lane<E) if h==0 else (lane>=E)
            qm[h*R:(h+1)*R]=jnp.where(mine,qq,zero)
            dm[h*R:(h+1)*R]=jnp.where(mine,don,zero)
        dqs=[]
        for h in range(2):
            rhs[h*E:(h+1)*E]=scaled[h]
            rhs[(1-h)*E:(2-h)*E]=jnp.zeros((E,R),BF)
            delta=jnp.sum(scaled[h].astype(F32)*ot[h*E:(h+1)*E],axis=0,keepdims=True)
            hi=delta.astype(BF).astype(F32)
            lo=delta-hi
            spot=lax.broadcasted_iota(jnp.int32,(16,R),0)
            rhs[W:W+16]=jnp.where(spot==0,-hi,jnp.where(spot==1,-lo,0.0)).astype(BF)
            for c in range(0,m,ch):
                g=dot(vaug[c:c+ch],rhs[...])
                ds[c:c+ch,h*R:(h+1)*R]=(p[0,h,base+c:base+c+ch].astype(F32)*g).astype(BF)
            kq[SPAN:,base:base+m]=kt[h*E:(h+1)*E]
            both=dot(kq[:,base:base+m],ds[:m,h*R:(h+1)*R])
            dqs.append(both[SPAN:]*0.125)
            nacc[h]+=dot(both[:SPAN].astype(BF),ohq[i])
        dq[i]=jnp.transpose(jnp.concatenate(dqs,axis=0)).astype(BF)
        for c in range(0,m,ch):
            dk=dot(ds[c:c+ch],qm[...])
            dv=dot(p[0,0,base+c:base+c+ch],dm[:R])+dot(p[0,1,base+c:base+c+ch],dm[R:])
            if i<n-1:
                dkf[i,c:c+ch]=dk.astype(BF); dvf[i,c:c+ch]=dv.astype(BF)
            else:
                dks[c:c+ch]=dk.astype(BF); dvs[c:c+ch]=dv.astype(BF)
        base+=m
    for h in range(2):
        wide=jnp.concatenate([nacc[h],jnp.zeros((SPAN,SPAN),F32)],axis=1)
        rolled=pltpu.roll(wide,0,1,stride=1,stride_axis=0)
        t[0,h:h+1]=jnp.sum(rolled,axis=0,keepdims=True)

def attend_back_call(q,kf,vf,ks,vs,layq,layf,lays,o,do,p,l):
    n,R,D=q.shape; L=kf.shape[1]; S=ks.shape[0]; H=p.shape[0]*2; E=D//H; W=2*E
    KT=(n-1)*L+S
    full=lambda a: pl.BlockSpec(a.shape,lambda j:(0,)*a.ndim)
    rows=lambda: pl.BlockSpec((n,R,W),lambda j:(0,0,j))
    kb=lambda: pl.BlockSpec((n-1,L,W),lambda j:(0,0,j))
    sb=lambda: pl.BlockSpec((S,W),lambda j:(0,j))
    return pl.pallas_call(functools.partial(attend_back,n,L,S,R,E),
      grid=(H//2,),
      in_specs=[rows(),kb(),kb(),sb(),sb(),full(layq),full(layf),full(lays),rows(),rows(),
        pl.BlockSpec((1,2,KT,R),lambda j:(j,0,0,0)),pl.BlockSpec((n,1,2,R),lambda j:(0,j,0,0))],
      out_specs=[rows(),kb(),kb(),sb(),sb(),pl.BlockSpec((1,2,2*SPAN),lambda j:(j,0,0))],
      out_shape=[jax.ShapeDtypeStruct((n,R,D),BF),jax.ShapeDtypeStruct(kf.shape,BF),jax.ShapeDtypeStruct(kf.shape,BF),
        jax.ShapeDtypeStruct(ks.shape,BF),jax.ShapeDtypeStruct(ks.shape,BF),jax.ShapeDtypeStruct((H//2,2,2*SPAN),F32)],
      scratch_shapes=[pltpu.VMEM((SPAN+E,KT),BF),pltpu.VMEM((L,2*W),BF),pltpu.VMEM((2*W,R),BF),pltpu.VMEM((L,2*R),BF),
        pltpu.VMEM((n,R,SPAN),BF),pltpu.VMEM((2,SPAN,SPAN),F32),pltpu.VMEM((2*R,W),BF),pltpu.VMEM((2*R,W),BF)],
      compiler_params=pltpu.CompilerParams(vmem_limit_bytes=56*2**20,dimension_semantics=("arbitrary",)),
      name="attend_back",
    )(q,kf,vf,ks,vs,layq,layf,lays,o,do,p,l)


EPSILON = 1e-06
FORWARD_PIECES = 3
FORWARD_WAYS = (0,) * 11
FORWARD_AT = (
    (-9, -8, -7, -6, -5),
    (-8, -7, -6, -5, -4),
    (-7, -6, -5, -4, -3),
    (-6, -5, -4, -3, -2),
    (-5, -4, -3, -2, 4),
    (-4, -3, -2, 4, 8),
    (-3, -2, 4, 8, 12),
    (-2, 4, 8, 12, 16),
    (4, 8, 12, 16, 20),
    (8, 12, 16, 20, 24),
)
FF_SUMS = 3
FF_SUM = (0, 2)
FF_SUM_LAG = (0, 3, 7, 11, 16)
BACK_SUM = (2, 2, 4)


MESH = pl.DeviceIdType.MESH


class Place:
    def __init__(self, mostly_y=False):
        dp = lax.axis_index("dp")
        self.x = lax.axis_index("blk")
        self.z, self.y, self.c = dp // 4, (dp // 2) % 2, dp % 2
        c = 1 if mostly_y else self.c
        self.y1, self.x1 = (self.y + 1 - c) % 2, (self.x + c) % 2
        self.y2, self.x2 = (self.y + c) % 2, (self.x + 1 - c) % 2

    def device(self, z, y, c, x):
        return ((z * 2 + y) * 2 + c, x)

    def along_z(self, d):
        return self.device((self.z + d) % 4, self.y, self.c, self.x)

    def along_x(self):
        return self.device(self.z, self.y, self.c, 1 - self.x)

    def along_y(self):
        return self.device(self.z, 1 - self.y, self.c, self.x)

    def first(self):
        return self.device(self.z, self.y1, self.c, self.x1)

    def second(self):
        return self.device(self.z, self.y2, self.c, self.x2)

    def core(self):
        return self.device(self.z, self.y, 1 - self.c, self.x)

    def greet(self):
        barrier = pltpu.get_barrier_semaphore()
        partners = [self.along_z(d) for d in (1, 2, 3)] + [self.first(), self.second(), self.core()]
        for partner in partners:
            pl.semaphore_signal(barrier, inc=1, device_id=partner, device_id_type=MESH)
        pl.semaphore_wait(barrier, len(partners))


def remote(src, dst, sems, k, device):
    return pltpu.make_async_remote_copy(
        src_ref=src, dst_ref=dst, send_sem=sems[0].at[k], recv_sem=sems[1].at[k], device_id=device, device_id_type=MESH
    )


GATHER_COPIES = 10


def gather_stages(at, shard, whole, sems, local, base, cols=None, plane=None):
    z, y, c, x = at.z, at.y, at.c, at.x
    cols = pl.ds(0, shard.shape[1]) if cols is None else cols
    shard = shard.at[:, cols]
    own = whole.at[z if plane is None else 0, y, c, x]
    keep = pltpu.make_async_copy(shard, own, local)

    def group(yy, xx):
        return whole.at[:, yy, c, xx]

    def copy(k):
        if k < 3:
            return remote(shard, own, sems, base + k, at.along_z(k + 1))
        view, device = {
            3: (group(y, x), at.first()),
            4: (group(y, x), at.second()),
            5: (group(y, x), at.core()),
            6: (group(at.y1, at.x1), at.second()),
            7: (group(at.y1, at.x1), at.core()),
            8: (group(at.y2, at.x2), at.core()),
            9: (group(1 - y, 1 - x), at.core()),
        }[k]
        return remote(view, view, sems, base + k, device)

    def one():
        def start():
            keep.start()
            for k in range(3):
                copy(k).start()

        start() if plane is None else pl.when(z == plane)(start)

    def two():
        if plane is None:
            keep.wait()
            for k in range(3):
                copy(k).wait_recv()
        else:
            pl.when(z == plane)(keep.wait)
            d = (z - plane + 4) % 4
            arrival = remote(shard, own, sems, base + d - 1, at.along_z(1))
            pl.when(z != plane)(arrival.wait_recv)
        for k in (3, 4, 5):
            copy(k).start()

    def three():
        copy(3).wait_recv()
        for k in (6, 7):
            copy(k).start()

    def four():
        copy(4).wait_recv()
        copy(8).start()
        copy(6).wait_recv()
        copy(9).start()

    def five():
        for k in (5, 7, 8, 9):
            copy(k).wait_recv()
        for k in range(3, 10):
            copy(k).wait_send()

        def sent():
            for k in range(3):
                copy(k).wait_send()

        sent() if plane is None else pl.when(z == plane)(sent)

    return [one, two, three, four, five]


def gather_stages_x(at, shard, whole, sems, local, base):
    z, y, c, x = at.z, at.y, at.c, at.x
    own = whole.at[z, y, c, x]
    keep = pltpu.make_async_copy(shard, own, local)

    def copy(k):
        if k == 0:
            return remote(shard, own, sems, base, at.along_x())
        view, device = {
            1: (whole.at[z, y, c], at.along_z(1)),
            2: (whole.at[z, y, c], at.along_z(2)),
            3: (whole.at[z, y, c], at.along_z(3)),
            4: (whole.at[:, y, c], at.along_y()),
            5: (whole.at[:, y, c], at.core()),
            6: (whole.at[:, 1 - y, c], at.core()),
        }[k]
        return remote(view, view, sems, base + k, device)

    def step(arrivals, starts):
        def run():
            for k in arrivals:
                copy(k).wait_recv()
            for k in starts:
                copy(k).start()

        return run

    def one():
        keep.start()
        copy(0).start()

    def two():
        keep.wait()
        step((0,), (1, 2, 3))()

    def five():
        step((5, 6), ())()
        for k in range(7):
            copy(k).wait_send()

    return [one, two, step((1, 2, 3), (4, 5)), step((4,), (6,)), five]


def small_stages(at, part, total, held, got, sems, base):
    def copy(k):
        device = [at.core, at.along_y, at.along_x][k]() if k < 3 else at.along_z(k - 2)
        return remote(held.at[min(k, 3)], got.at[k], sems, base + k, device)

    def one():
        held[0] = part[...]
        copy(0).start()

    def add(k):
        def run():
            copy(k).wait_recv()
            held[k + 1] = held[k] + got[k]
            for following in (k + 1,) if k < 2 else (3, 4, 5):
                copy(following).start()

        return run

    def five():
        parts = [held[3]]
        for d in (1, 2, 3):
            copy(2 + d).wait_recv()
            parts.append(got[2 + d])
        out = jnp.zeros_like(parts[0])
        for spot in range(4):
            for d in range(4):
                out = out + jnp.where((at.z - d + 4) % 4 == spot, parts[d], 0.0)
        total[...] = out
        for k in range(6):
            copy(k).wait_send()

    return [one, add(0), add(1), add(2), five]


def norm_rows(x):
    return lax.rsqrt(jnp.mean(x * x, axis=1, keepdims=True) + EPSILON)


def dot_nt(a, b):
    return lax.dot_general(a, b, (((1,), (1,)), ((), ())), preferred_element_type=F32)


def flipped(a):
    return jnp.transpose(a.astype(F32)).astype(BF)


TICKS = 6


def feed_forward_plan(sums):
    events = []
    for i, (stages, j) in enumerate(sums):
        for s, lag in enumerate(FF_SUM_LAG):
            events.append((TICKS * (j + 1) + FF_SUM[i % 2] + lag, stages[s]))
    plan = {}
    for when, stage in sorted(events, key=lambda e: e[0]):
        plan.setdefault(when, []).append(stage)
    return plan


def feed_forward(R, blocks, *refs):
    flag, att_, tok_, up_, wo_, grow = refs[:6]
    given = refs[6:8]
    refs = list(refs[8:])
    take = lambda k: [refs.pop(0) for _ in range(k)]
    mixed, dres, datt, dwo = take(4)
    last = FF_SUMS
    handed = [take(2) for _ in range(last, blocks)]
    (dgain,) = take(1)
    totals_in = take(last)
    (total_out,) = take(1)
    att, tok, up, wo, wbi, wbt, n2, n2t, resid, acc, dn2, act_t, dpre_s, parts_in, parts_out = take(15)
    sum_scratch = [take(5) for _ in range(2 * last)]
    send, recv, local = take(3)
    rows, width = att.shape
    block = wbi.shape[2]
    piece = rows // 4
    pieces = [pl.ds(i, piece) for i in range(0, rows, piece)]
    step = pl.program_id(0)
    slot = lax.rem(step, 2)
    at = Place()
    sems = (send, recv)

    sums = []
    for j in range(last):
        for which, (part, total) in enumerate([(parts_in.at[j], totals_in[j]), (parts_out.at[j], total_out)]):
            i = len(sums)
            chain = Sum(at, part, total, sum_scratch[i], sems, None, Sum.COPIES * i, None, j if which else None)
            sums.append((chain.stages, j))
    plan = feed_forward_plan(sums)

    def local_copy(a, b, k):
        return pltpu.make_async_copy(a, b, local.at[k])

    def weights(j):
        hidden = pl.ds(j * block, block)
        return [local_copy(given[0].at[:, hidden], wbi.at[j % 2], 4), local_copy(given[1].at[hidden], wbt.at[j % 2], 5)]

    def tick(t):
        for when in plan:
            if when < TICKS * blocks and when % TICKS == t:

                @pl.when(step == when // TICKS)
                def _(when=when):
                    for stage in plan[when]:
                        stage()

    @pl.when(step == 0)
    def _():
        loads = [local_copy(a, b, i) for i, (a, b) in enumerate([(tok_, tok), (att_, att), (wo_, wo), (up_, up)])]
        for load in loads + weights(0):
            load.start()
        at.greet()
        for load in loads:
            load.wait()
        for a in (tok, up):
            a[:R], a[R:] = swapped(flag, a[:R], a[R:])
        for b in pieces:
            x = tok[b].astype(F32) + dot(att[b], wo[...])
            resid[b] = x
            normed = (x * norm_rows(x) * grow[1:2]).astype(BF)
            n2[b] = normed
            n2t[:, b] = flipped(normed)
            acc[b] = x
            dn2[b] = jnp.zeros_like(x)

    for j in range(blocks):

        @pl.when(step == j)
        def _(j=j):
            for load in weights(j):
                load.wait()
            if j + 1 < blocks:
                for load in weights(j + 1):
                    load.start()

    for i, b in enumerate(pieces):
        tick(i)
        pre = dot(n2[b], wbi[slot])
        dact = dot_nt(up[b], wbt[slot])
        half = 0.5 + 0.5 * lax.erf(pre * 0.7071067811865476)
        act = (pre * half).astype(BF)
        dpre = (dact * (half + pre * (jnp.exp(-0.5 * pre * pre) * 0.3989422804014327))).astype(BF)
        acc[b] += dot(act, wbt[slot])
        dn2[b] += dot_nt(dpre, wbi[slot])
        act_t[:, b] = flipped(act)
        dpre_s[b] = dpre
    tick(4)
    grad_in = dot(n2t[...], dpre_s[...])
    tick(5)
    grad_out = dot(act_t[...], up[...])

    into_slabs(grad_in, parts_in.at[step])
    count = parts_out.shape[5]
    for i in range(8):
        parts_out[step, 0, i // 4, i // 2 % 2, i % 2] = grad_out[count * i : count * (i + 1)].astype(BF)
    hand = [
        [local_copy(parts_in.at[j], handed[j - last][0], 6 + 2 * j), local_copy(parts_out.at[j], handed[j - last][1], 7 + 2 * j)]
        for j in range(last, blocks)
    ]
    for j in range(last, blocks):

        @pl.when(step == j)
        def _(j=j):
            for copy in hand[j - last]:
                copy.start()

    @pl.when(step == blocks - 1)
    def _():
        rest = [stage for t in sorted(plan) if t >= TICKS * blocks for stage in plan[t]]

        def some(count):
            for _ in range(min(count, len(rest))):
                rest.pop(0)()

        ends = []
        some(2)
        for i, b in enumerate(pieces):
            n2[b] = acc[b].astype(BF)
        n2[:R], n2[R:] = swapped(flag, n2[:R], n2[R:])
        ends.append(local_copy(n2, mixed, 2))
        ends[-1].start()
        total = None
        for b in pieces:
            x, d = resid[b], dn2[b]
            back = norm_rows(x)
            a = grow[1:2] * d
            part = jnp.sum(d * x * back, axis=0, keepdims=True)
            total = part if total is None else total + part
            g = up[b].astype(F32) + back * a - x * (back * back * back) * jnp.mean(a * x, axis=1, keepdims=True)
            dn2[b] = g
            g = g.astype(BF)
            up[b] = g
            tok[b] = dot_nt(g, wo[...]).astype(BF)
            act_t[:width, b] = flipped(att[b])
            some(1)
        dgain[...] = total
        ends += [local_copy(dn2, dres, 3), local_copy(tok, datt, 4)]
        ends[-1].start()
        ends[-2].start()
        dpre_s[:width, :width] = dot(act_t[:width], up[...]).astype(BF)
        ends.append(local_copy(dpre_s.at[pl.ds(0, width), pl.ds(0, width)], dwo, 5))
        ends[-1].start()
        some(100)
        for end in ends + sum(hand, []):
            end.wait()


def feed_forward_call(flag, att, tokens, up, wo, grow, wi, wt):
    rows, D = tokens.shape
    R = rows // 2
    blocks = 4
    last = FF_SUMS
    block = wi.shape[1] // blocks
    share_in, share_out = (D // 32, block), (wt.shape[0] // 32, D)
    anywhere = pl.BlockSpec(memory_space=pl.ANY)
    whole = lambda shape: pl.BlockSpec(shape, lambda j: (0,) * len(shape))
    vmem = lambda *s: pltpu.VMEM(s, BF)
    wide = lambda *s: pltpu.VMEM(s, F32)
    slab_in, slab_out = (4, 2, 2, 2) + share_in, (1, 2, 2, 2) + share_out
    outs = [((rows, D), BF), ((rows, D), F32), ((rows, D), BF), ((D, D), BF)] + [(slab_in, BF), (slab_out, BF)] * (blocks - last)
    small = [((1, D), F32)] + [(share_in, F32)] * last + [(share_out, F32)]
    copies = max(Sum.COPIES * 2 * last, 1)
    scratch = [vmem(rows, D)] * 3 + [vmem(D, D), vmem(2, D, block), vmem(2, block, D), vmem(rows, D), vmem(D, rows)]
    scratch += [wide(rows, D)] * 3 + [vmem(block, rows), vmem(rows, block), vmem(blocks, *slab_in), vmem(blocks, *slab_out)]
    scratch += (Sum.scratch(4, *share_in, 0) + Sum.scratch(1, *share_out, 0)) * last
    scratch += [pltpu.SemaphoreType.DMA((copies,))] * 2 + [pltpu.SemaphoreType.DMA((6 + 2 * blocks,))]
    return pl.pallas_call(
        functools.partial(feed_forward, R, blocks),
        grid=(blocks,),
        in_specs=[pl.BlockSpec(memory_space=pltpu.SMEM)] + [anywhere] * 4 + [whole(grow.shape)] + [anywhere] * 2,
        out_specs=[anywhere] * len(outs) + [whole(s) for s, _ in small],
        out_shape=[jax.ShapeDtypeStruct(*s) for s in outs + small],
        scratch_shapes=scratch,
        compiler_params=pltpu.CompilerParams(
            vmem_limit_bytes=60 * 2**20, dimension_semantics=("arbitrary",), collective_id=2, has_side_effects=True
        ),
        name="feed_forward",
    )(flag, att, tokens, up, wo, grow, wi, wt)


def turn_plan(chains, places):
    plan = {}
    for chain, at in zip(chains, places):
        for place, stage in zip(at, chain):
            plan.setdefault(place, []).insert(0, stage)
    return plan


def together(*chains):
    def stage(s):
        def run():
            for chain in chains:
                chain[s]()

        return run

    return [stage(s) for s in range(len(chains[0]))]


def unslab(slabs, flat):
    rows = slabs.shape[4]
    for i in range(16):
        pair = [slabs[i // 4, i // 2 % 2, i % 2, x] for x in range(2)]
        flat[2 * rows * i : 2 * rows * (i + 1)] = jnp.concatenate(pair, axis=0)


def normed_rows(x, gain):
    x = x.astype(F32)
    return (x * norm_rows(x) * gain).astype(BF)


def block_chain(ats, shard_in, shard_out, j, whole_in, whole_out, sems, local, k):
    width = whole_in.shape[5]
    return [
        gather_stages(ats[0], shard_in, whole_in, sems, local.at[k], GATHER_COPIES * k, pl.ds(j * width, width)),
        gather_stages(ats[1], shard_out, whole_out, sems, local.at[k + 1], GATHER_COPIES * (k + 1), None, j),
    ]


def swapped(lengths, a, b):
    turn = lengths[0] < lengths[1]
    return jnp.where(turn, b, a), jnp.where(turn, a, b)


def coordinates(at, lengths, layout, R, S):
    long, short = swapped(lengths, layout[0:1], layout[1:2])
    keys = jnp.where(at.x == 0, long, jnp.concatenate([long[:, R:], long[:, :R]], axis=1))
    return keys, short[:, :S], keys[:, :R], jnp.where(at.x == 0, short[:, :R], short[:, R:])


def forward_kernel(R, L, S, E, pairs, *refs):
    flag, tokens, layout, table, basis = refs[:5]
    shards = refs[5:12]
    refs = list(refs[12:])
    take = lambda k: [refs.pop(0) for _ in range(k)]
    o, pa, pb, cs, grow = take(5)
    kept = take(7)
    wholes = take(6)
    kcat, qcat, vt, s_ref, ohq, xfar, xshort, flat, normed, tok, held, stats, u = take(13)
    q, kf, vf, ks, vs, nkt, nst = inner = take(7)
    slabs = take(4)
    send, recv, local = take(3)
    W = 2 * E
    D = tok.shape[2]
    at = Place()
    sems = (send, recv)
    ways = [(at, Place(True))[i] for i in FORWARD_WAYS]
    targets = slabs + wholes[3:]
    chains = []
    for i, cols in [(i, None) for i in range(5)] + [(i, cols) for i in (5, 6) for cols in pieces_of(shards[i].shape[1])]:
        k = len(chains)
        view = targets[i] if cols is None else targets[i].at[:, :, :, :, :, cols]
        chains.append(gather_stages(ways[k], shards[i], view, sems, local.at[k], GATHER_COPIES * k, cols))
    count = len(chains)
    chains = [together(chains[0], chains[1])] + chains[2:]
    plan = turn_plan(chains, FORWARD_AT)
    spare = GATHER_COPIES * count
    long = remote(tok.at[0], xfar, sems, spare, at.along_x())
    short = remote(tok.at[1, pl.ds(0, S)], xshort, sems, spare + 1, at.along_x())
    out = lambda i, a, b: pltpu.make_async_copy(a, b, local.at[count + i])
    weights_out = [out(i, slabs[1 + i], wholes[i]) for i in range(3)]
    kept_out = [out(3 + i, a, b) for i, (a, b) in enumerate(zip(inner, kept))]

    def send_tokens():
        long.start()
        pl.when(at.x == 0)(short.start)

    def turn(t):
        for stage in plan.get(t, []):
            stage()

    step = pl.program_id(0)
    pair = lax.rem(step, pairs)

    @pl.when(step == 0)
    def _():
        at.greet()
        turn(-9)
        tok[0], tok[1] = swapped(flag, tokens[0], tokens[1])
        send_tokens()
        long_keys, short_keys, *queries = coordinates(at, flag, layout, R, S)
        for i, (base, row) in enumerate([(0, long_keys), (L, short_keys)]):
            kcat[base : base + row.shape[1], W:] = jnp.transpose(eye_of(row, SPAN, False).astype(F32)).astype(BF)
            ohq[i] = eye_of(queries[i], SPAN, False)
        rows = lax.dot_general(table[...], basis[...], (((0,), (0,)), ((), ())), preferred_element_type=F32)
        for h in range(2 * pairs):
            u[h] = rows[h : h + 1]
        vt[:, E:] = jnp.ones((2, vt.shape[1] - E, vt.shape[2]), BF)
        for t in range(-8, -4):
            turn(t)
        gslab = slabs[0]
        columns = jnp.concatenate(
            [gslab[i // 8, i // 4 % 2, i // 2 % 2, i % 2].astype(F32) for i in range(32)], axis=0
        )
        grow[...] = jnp.transpose(columns)[:8]
        gain = grow[0:1]
        weights_out[0].start()
        unslab(slabs[1], flat.at[0])
        for i in range(2):
            normed[i] = normed_rows(tok[i], gain)
            q[i] = (dot(normed[i], flat[0]).astype(BF).astype(F32) * 0.125).astype(BF)
        turn(-4)
        weights_out[1].start()
        unslab(slabs[2], flat.at[0])
        kf[:R] = dot(normed[0], flat[0]).astype(BF)
        turn(-3)
        weights_out[2].start()
        unslab(slabs[3], flat.at[1])
        vf[:R] = dot(normed[0], flat[1]).astype(BF)
        kept_out[0].start()
        turn(-2)

    @pl.when(step == pairs)
    def _():
        nkt[:, :R] = flipped(normed[0])
        nst[...] = flipped(normed[1])
        long.wait()

        @pl.when(at.x == 0)
        def _():
            short.wait_send()

        @pl.when(at.x == 1)
        def _():
            short.wait_recv()

        @pl.when(at.x == 0)
        def _():
            xshort[...] = tok[1, :S]

        gain = grow[0:1]
        normed[0] = normed_rows(xfar[...], gain)
        normed[1, :S] = normed_rows(xshort[...], gain)
        kf[R:] = dot(normed[0], flat[0]).astype(BF)
        vf[R:] = dot(normed[0], flat[1]).astype(BF)
        ks[...] = dot(normed[1, :S], flat[0]).astype(BF)
        vs[...] = dot(normed[1, :S], flat[1]).astype(BF)
        nkt[:, R:L] = flipped(normed[0])
        nkt[:, L:] = flipped(normed[1, :S])
        for copy in kept_out[1:]:
            copy.start()

    steps = 2 * pairs

    def tick(spot):
        for t in sorted(plan):
            if t >= 2 * steps and spot == 2 or 0 <= t < 2 * steps and t % 2 == spot:

                @pl.when(step == min(t // 2, steps - 1))
                def _(t=t):
                    turn(t)

    here = pl.ds(pl.multiple_of(pair * W, W), W)

    def attend_to(i, base, m, keys, values, into, ticking):
        ch = min(CH, m)
        kcat[base : base + m, :W] = keys
        vt[0, :E, :m], vt[1, :E, :m] = jnp.split(flipped(values), 2, axis=0)
        qt = flipped(q[i, :, here])
        found = []
        for h in range(2):
            if ticking:
                tick(h)
            toep = pltpu.roll(jnp.broadcast_to(u[2 * pair + h], (SPAN, 2 * SPAN)), 0, 1, stride=1, stride_axis=0)
            qcat[h * E : (h + 1) * E] = qt[h * E : (h + 1) * E]
            qcat[(1 - h) * E : (2 - h) * E] = jnp.zeros((E, R), BF)
            qcat[W:] = dot(toep[:, :SPAN].astype(BF), ohq[i]).astype(BF)
            top = jnp.full((8, R), -jnp.inf, F32)
            for c in range(0, m, ch):
                s = dot(kcat[base + c : base + c + ch], qcat[...])
                s_ref[c : c + ch] = s
                top = jnp.maximum(top, jnp.max(s.reshape(ch // 8, 8, R), axis=0))
            top = jnp.max(top, axis=0, keepdims=True)
            for c in range(0, m, ch):
                into[h, c : c + ch] = jnp.exp(s_ref[c : c + ch] - top).astype(BF)
            full = dot(vt[h, :, :m], into[h, :m])
            found.append((top, full[E : E + 1], full[:E]))
        return found

    def heads(parts):
        return jnp.transpose(jnp.concatenate(parts, axis=0)).astype(BF)

    @pl.when(step < pairs)
    def _():
        found = attend_to(0, 0, R, kf[:R, here], vf[:R, here], pa.at[0], True)
        for h, (top, total, full) in enumerate(found):
            stats[pair, 2 * h : 2 * h + 1] = top
            stats[pair, 2 * h + 1 : 2 * h + 2] = total
            held[pair, h * E : (h + 1) * E] = full

    @pl.when(step >= pairs)
    def _():
        m = L - R
        found = attend_to(0, R, m, kf[R:, here], vf[R:, here], pb.at[0, :, pl.ds(0, m)], True)
        parts = []
        for h, (top, total, full) in enumerate(found):
            first, first_total = stats[pair, 2 * h : 2 * h + 1], stats[pair, 2 * h + 1 : 2 * h + 2]
            most = jnp.maximum(first, top)
            a, b = jnp.exp(first - most), jnp.exp(top - most)
            back = 1.0 / (a * first_total + b * total)
            cs[0, 0, h : h + 1] = a * back
            cs[1, 0, h : h + 1] = b * back
            parts.append(held[pair, h * E : (h + 1) * E] * (a * back) + full * (b * back))
        o[0] = heads(parts)
        found = attend_to(1, L, S, ks[:, here], vs[:, here], pb.at[0, :, pl.ds(m, S)], False)
        for h, (top, total, full) in enumerate(found):
            cs[2, 0, h : h + 1] = 1.0 / total
        o[1] = heads([full / total for _, total, full in found])

    tick(2)

    @pl.when(step == steps - 1)
    def _():
        for copy in weights_out + kept_out:
            copy.wait()


def pieces_of(width):
    return [pl.ds(i * width // FORWARD_PIECES, width // FORWARD_PIECES) for i in range(FORWARD_PIECES)]


def forward_call(flag, tokens, layout, table, basis, shards, S):
    n, R, D = tokens.shape
    L = layout.shape[1]
    pairs = table.shape[1] // 2
    E = D // (2 * pairs)
    W = 2 * E
    KT = L + S
    whole = lambda shape: pl.BlockSpec(shape, lambda j: (0,) * len(shape))
    anywhere = pl.BlockSpec(memory_space=pl.ANY)
    vmem = lambda *s: pltpu.VMEM(s, BF)
    wide = lambda *s: pltpu.VMEM(s, F32)
    early = lambda j: jnp.minimum(j, pairs - 1)
    late = lambda j: jnp.maximum(j - pairs, 0)
    kept = [(n, R, D), (L, D), (L, D), (S, D), (S, D), (D, KT), (D, R)]
    chains = 5 + 2 * FORWARD_PIECES
    copies = GATHER_COPIES * chains + 2
    gathered = [(4, 2, 2, 2) + s.shape for s in shards]
    filled = gathered[1:]
    blocked = [
        ((n, R, D), BF, pl.BlockSpec((n, R, W), lambda j: (0, 0, late(j)))),
        ((pairs, 2, R, R), BF, pl.BlockSpec((1, 2, R, R), lambda j: (early(j), 0, 0, 0))),
        ((pairs, 2, KT - R, R), BF, pl.BlockSpec((1, 2, KT - R, R), lambda j: (late(j), 0, 0, 0))),
        ((3, pairs, 2, R), F32, pl.BlockSpec((3, 1, 2, R), lambda j: (0, late(j), 0, 0))),
        ((8, D), F32, whole((8, D))),
    ]
    return pl.pallas_call(
        functools.partial(forward_kernel, R, L, S, E, pairs),
        grid=(2 * pairs,),
        in_specs=[pl.BlockSpec(memory_space=pltpu.SMEM)]
        + [whole(a.shape) for a in (tokens, layout, table, basis)]
        + [anywhere] * 7,
        out_specs=[b[2] for b in blocked] + [anywhere] * (len(kept) + len(filled)),
        out_shape=[jax.ShapeDtypeStruct(*b[:2]) for b in blocked] + [jax.ShapeDtypeStruct(s, BF) for s in kept + filled],
        scratch_shapes=[vmem(KT, W + SPAN), vmem(W + SPAN, R), vmem(2, E + 16, R), wide(R, R), vmem(n, SPAN, R)]
        + [vmem(R, D), vmem(S, D), vmem(2, D, D), vmem(n, R, D), vmem(n, R, D), wide(pairs, W, R), wide(pairs, 8, R), wide(2 * pairs, 1, 2 * SPAN)]
        + [vmem(*s) for s in kept]
        + [vmem(*s) for s in gathered[:4]]
        + [pltpu.SemaphoreType.DMA((copies,))] * 2
        + [pltpu.SemaphoreType.DMA((chains + 10,))],
        compiler_params=pltpu.CompilerParams(
            vmem_limit_bytes=60 * 2**20, dimension_semantics=("arbitrary",), collective_id=0, has_side_effects=True
        ),
        name="forward",
    )(flag, tokens, layout, table, basis, *shards)


class Sum:
    COPIES = 7

    def __init__(self, at, part, total, scratch, sems, local, base, cols=None, plane=None):
        self.at, self.part, self.total, self.sems, self.base, self.plane = at, part, total, sems, base, plane
        self.cols = pl.ds(0, total.shape[1]) if cols is None else cols
        self.acc, self.got_diag, self.got_one, self.got_two, self.got_z = scratch[:5]
        self.held = scratch[5] if len(scratch) > 5 else None
        if self.held is not None:
            self.keep = pltpu.make_async_copy(part.at[:, :, at.c, :, :, self.cols], self.held, local)
        self.stages = [self.one, self.two, self.three, self.four, self.five]

    @staticmethod
    def scratch(depth, rows, columns, held):
        slab = (rows, columns)
        shapes = [(depth, 2, 2) + slab] + [(depth,) + slab] * 3 + [(3,) + slab] + [(depth, 2, 2) + slab] * held
        return [pltpu.VMEM(s, BF) for s in shapes]

    def send(self, k):
        at, acc = self.at, self.acc
        if k > 3:
            d = k - 3
            src, dst, device = acc.at[(at.z + d) % 4, at.y, at.x], self.got_z.at[d - 1], at.along_z(d)
        else:
            src, dst, device = [
                (self.part.at[:, :, 1 - at.c, :, :, self.cols], acc, at.core()),
                (acc.at[:, 1 - at.y, 1 - at.x], self.got_diag, at.second()),
                (acc.at[:, at.y2, at.x2], self.got_two, at.second()),
                (acc.at[:, at.y1, at.x1], self.got_one, at.first()),
            ][k]
        return remote(src, dst, self.sems, self.base + k, device)

    def to_plane(self):
        at = self.at
        d = (self.plane - at.z + 4) % 4
        k = self.base + 3 + d
        return pltpu.make_async_remote_copy(
            src_ref=self.acc.at[0, at.y, at.x],
            dst_ref=self.got_z.at[d - 1],
            send_sem=self.sems[0].at[k],
            recv_sem=self.sems[1].at[k],
            device_id=at.device(self.plane, at.y, at.c, at.x),
            device_id_type=MESH,
        )

    def one(self):
        self.send(0).start()
        if self.held is not None:
            self.keep.start()

    def two(self):
        at, acc = self.at, self.acc
        if self.held is not None:
            self.keep.wait()
        self.send(0).wait_recv()

        def add(i, _):
            for yy in range(2):
                own = self.held[i, yy] if self.held is not None else self.part[i, yy, at.c, :, :, self.cols]
                acc[i, yy] = (acc[i, yy].astype(F32) + own.astype(F32)).astype(BF)
            return 0

        lax.fori_loop(0, acc.shape[0], add, 0)
        self.send(1).start()
        self.send(2).start()

    def three(self):
        at, acc = self.at, self.acc
        self.send(1).wait_recv()
        acc[:, at.y1, at.x1] = (acc[:, at.y1, at.x1].astype(F32) + self.got_diag[...].astype(F32)).astype(BF)
        self.send(3).start()

    def four(self):
        at, acc = self.at, self.acc
        self.send(2).wait_recv()
        self.send(3).wait_recv()
        mine = acc[:, at.y, at.x].astype(F32) + self.got_one[...].astype(F32) + self.got_two[...].astype(F32)
        acc[:, at.y, at.x] = mine.astype(BF)
        if self.plane is None:
            for k in (4, 5, 6):
                self.send(k).start()
        else:

            @pl.when(at.z != self.plane)
            def _():
                self.to_plane().start()

    def five(self):
        at = self.at

        def collect():
            out = self.acc[at.z if self.plane is None else 0, at.y, at.x].astype(F32)
            for d in (1, 2, 3):
                arrival = remote(self.got_z.at[d - 1], self.got_z.at[d - 1], self.sems, self.base + 3 + d, at.along_z(d))
                arrival.wait_recv()
                out = out + self.got_z[d - 1].astype(F32)
            self.total[:, self.cols] = out

        for k in range(4):
            self.send(k).wait_send()
        if self.plane is None:
            collect()
            for k in (4, 5, 6):
                self.send(k).wait_send()
        else:
            pl.when(at.z == self.plane)(collect)

            @pl.when(at.z != self.plane)
            def _():
                self.to_plane().wait_send()


def into_slabs(flat, slabs):
    rows = slabs.shape[4]
    for i in range(32):
        slabs[i // 8, i // 4 % 2, i // 2 % 2, i % 2] = flat[rows * i : rows * (i + 1)].astype(BF)


def backward_kernel(R, L, S, E, pairs, planes, *refs):
    flag, q, kf, vf, ks, vs, o, do, pa, pb, cs, layout = refs[:12]
    refs = list(refs[12:])
    take = lambda k: [refs.pop(0) for _ in range(k)]
    parts = take(len(planes))
    nkt_, nst_, wq, wk, wv, tok, dres, grow, dg2 = take(9)
    gtok, small_total = take(2)
    totals = take(3 + len(planes))
    kq, vaug, rhs, ds, ohq, nacc, qm, dm, held = take(9)
    dq, dk, dv, nkt, nst, ws, toks, dress = take(8)
    far, fars, gfar, gshort, ends = take(5)
    tsum, small, small_held, small_got = take(4)
    send, recv, local = take(3)
    W = 2 * E
    D = ws.shape[1]
    at = Place()
    sems = (send, recv)
    sums = []

    def summed(part, total, held, plane=None):
        i = len(sums)
        sums.append(Sum(at, part, total, take(5 + held), sems, local.at[i], Sum.COPIES * i, None, plane))

    for part, total, plane in zip(parts, totals, planes):
        summed(part, total, 1, plane)
    early = len(sums)
    mats = take(3)
    for part, total in zip(mats, totals[early:]):
        summed(part, total, 0)
    base = Sum.COPIES * len(sums)
    small_chain = small_stages(at, small, small_total, small_held, small_got, sems, base)
    long = remote(far, gfar, sems, base + 6, at.along_x())
    short = remote(fars, gshort, sems, base + 7, at.along_x())
    loads = [(w, ws.at[i]) for i, w in enumerate((wq, wk, wv))] + [(nkt_, nkt), (nst_, nst), (tok, toks), (dres, dress)]
    loads = [pltpu.make_async_copy(a, b, local.at[len(sums) + i]) for i, (a, b) in enumerate(loads)]

    step = pl.program_id(0)
    pair = lax.rem(step, pairs)
    steps = 2 * pairs
    plan = {}
    for i in range(early):
        for s in range(5):
            when = 0 if s == 0 else int(BACK_SUM[0] + BACK_SUM[1] * i + BACK_SUM[2] * (s - 1))
            plan.setdefault(when, []).insert(0, sums[i].stages[s])

    def tick(spot):
        for t in plan:
            if t < 2 * steps and t % 2 == spot:

                @pl.when(step == t // 2)
                def _(t=t):
                    for stage in plan[t]:
                        stage()

    @pl.when(step == 0)
    def _():
        at.greet()
        for load in loads:
            load.start()
        long_keys, short_keys, *queries = coordinates(at, flag, layout, R, S)
        for i, (base, row) in enumerate([(0, long_keys), (L, short_keys)]):
            kq[:SPAN, base : base + row.shape[1]] = eye_of(row, SPAN, True)
            ohq[i] = jnp.transpose(eye_of(queries[i], SPAN, False).astype(F32)).astype(BF)
        vaug[:, W:] = (lax.broadcasted_iota(jnp.int32, (R, W), 1) < 2).astype(F32).astype(BF)
        rhs[...] = jnp.zeros_like(rhs)

    @pl.when(step == pairs)
    def _():
        for load in loads[:3]:
            load.wait()
        far[...] = (dot_nt(dk[R:L], ws[1]) + dot_nt(dv[R:L], ws[2])).astype(BF)
        long.start()
        ends[...] = dot_nt(dk[L:], ws[1]) + dot_nt(dv[L:], ws[2])
        fars[...] = ends[...].astype(BF)
        pl.when(at.x == 1)(short.start)

    nacc[...] = jnp.zeros_like(nacc)
    lane = lax.broadcasted_iota(jnp.int32, (R, W), 1)
    spot = lax.broadcasted_iota(jnp.int32, (16, R), 0)
    here = pl.ds(pl.multiple_of(pair * W, W), W)

    def attend_to(i, base, m, keys, values, p, scale, ticking):
        ch = min(CH, m)
        vaug[:m, :W] = values
        kt = flipped(keys)
        dot_, ot = jnp.transpose(do[i].astype(F32)), jnp.transpose(o[i].astype(F32))
        scaled = [(dot_[h * E : (h + 1) * E] * cs[scale, 0, h : h + 1]).astype(BF) for h in range(2)]
        don = flipped(jnp.concatenate(scaled, axis=0))
        qq = q[i]
        zero = jnp.zeros((R, W), BF)
        for h in range(2):
            mine = (lane < E) if h == 0 else (lane >= E)
            qm[h * R : (h + 1) * R] = jnp.where(mine, qq, zero)
            dm[h * R : (h + 1) * R] = jnp.where(mine, don, zero)
        dqs = []
        for h in range(2):
            if ticking:
                tick(h)
            rhs[h * E : (h + 1) * E] = scaled[h]
            rhs[(1 - h) * E : (2 - h) * E] = jnp.zeros((E, R), BF)
            delta = jnp.sum(scaled[h].astype(F32) * ot[h * E : (h + 1) * E], axis=0, keepdims=True)
            hi = delta.astype(BF).astype(F32)
            rhs[W : W + 16] = jnp.where(spot == 0, -hi, jnp.where(spot == 1, hi - delta, 0.0)).astype(BF)
            for c in range(0, m, ch):
                g = dot(vaug[c : c + ch], rhs[...])
                ds[c : c + ch, h * R : (h + 1) * R] = (p[h, c : c + ch].astype(F32) * g).astype(BF)
            kq[SPAN:, base : base + m] = kt[h * E : (h + 1) * E]
            both = dot(kq[:, base : base + m], ds[:m, h * R : (h + 1) * R])
            dqs.append(both[SPAN:] * 0.125)
            nacc[h] += dot(both[:SPAN].astype(BF), ohq[i])
        for c in range(0, m, ch):
            dk[base + c : base + c + ch, here] = dot(ds[c : c + ch], qm[...]).astype(BF)
            both = dot(p[0, c : c + ch], dm[:R]) + dot(p[1, c : c + ch], dm[R:])
            dv[base + c : base + c + ch, here] = both.astype(BF)
        return jnp.concatenate(dqs, axis=0)

    def diagonals(h):
        wide = jnp.concatenate([nacc[h], jnp.zeros((SPAN, SPAN), F32)], axis=1)
        return jnp.sum(pltpu.roll(wide, 0, 1, stride=1, stride_axis=0), axis=0, keepdims=True)

    @pl.when(step < pairs)
    def _():
        m = L - R
        held[pair] = attend_to(0, R, m, kf[R:], vf[R:], pb.at[0, :, pl.ds(0, m)], 1, True)
        dq[1, :, here] = flipped(attend_to(1, L, S, ks[...], vs[...], pb.at[0, :, pl.ds(m, S)], 2, False))
        for h in range(2):
            tsum[2 * pair + h] = diagonals(h)

    @pl.when(step >= pairs)
    def _():
        dq[0, :, here] = flipped(held[pair] + attend_to(0, 0, R, kf[:R], vf[:R], pa.at[0], 0, True))
        for h in range(2):
            tsum[2 * pair + h] = tsum[2 * pair + h] + diagonals(h)

    @pl.when(step == steps - 1)
    def _():
        rest = [stage for t in sorted(plan) if t >= 2 * steps for stage in plan[t]]

        def some(count):
            for _ in range(min(count, len(rest))):
                rest.pop(0)()

        for load in loads[3:]:
            load.wait()
        later = sums[early:]
        into_slabs(dot(nkt[...], dv[...]), mats[2])
        later[2].one()
        some(2)
        into_slabs(dot(nkt[...], dk[...]), mats[1])
        later[1].one()
        some(2)
        into_slabs(dot(nkt[:, :R], dq[0]) + dot(nst[...], dq[1]), mats[0])
        later[0].one()
        some(100)
        later[2].two()
        toks[0], toks[1] = swapped(flag, toks[0], toks[1])
        own = [dot_nt(dq[0], ws[0]) + dot_nt(dk[:R], ws[1]) + dot_nt(dv[:R], ws[2]), dot_nt(dq[1], ws[0])]
        later[1].two()
        later[2].three()
        long.wait()
        pl.when(at.x == 1)(short.wait_send)
        pl.when(at.x == 0)(short.wait_recv)
        gain = grow[0:1]
        keys = jnp.where(at.x == 0, ends[...] + gshort[...].astype(F32), 0.0)
        total = jnp.zeros((1, D), F32)
        for i in range(2):
            d = own[i] + (gfar[...].astype(F32) if i == 0 else jnp.concatenate([keys, jnp.zeros((R - S, D), F32)], axis=0))
            x = toks[i].astype(F32)
            back = norm_rows(x)
            a = gain * d
            total = total + jnp.sum(d * x * back, axis=0, keepdims=True)
            part = back * a - x * (back * back * back) * jnp.mean(a * x, axis=1, keepdims=True)
            toks[i] = (dress[i * R : (i + 1) * R] + part).astype(BF)
        toks[0], toks[1] = swapped(flag, toks[0], toks[1])
        finish = pltpu.make_async_copy(toks, gtok, local.at[len(sums) + len(loads)])
        finish.start()
        small[...] = jnp.zeros_like(small)
        lines = D // 128
        for i in range(lines):
            small[i : i + 1] = total[:, 128 * i : 128 * (i + 1)]
            small[lines + i : lines + i + 1] = dg2[:, 128 * i : 128 * (i + 1)]
        for h in range(2 * pairs):
            for i in range(4):
                spots = 2 * lines + 4 * h + i
                small[spots : spots + 1] = tsum[h, :, 128 * i : 128 * (i + 1)]
        small_chain[0]()
        later[0].two()
        later[1].three()
        small_chain[1]()
        later[2].four()
        later[0].three()
        small_chain[2]()
        later[1].four()
        small_chain[3]()
        later[0].four()
        for s in later[::-1]:
            s.five()
        small_chain[4]()
        finish.wait()


def backward_call(flag, q, kf, vf, ks, vs, o, do, pa, pb, cs, layout, parts, planes, nkt, nst, wq, wk, wv, tok, dres, grow, dg2):
    n, R, D = q.shape
    L, S = kf.shape[0], ks.shape[0]
    pairs = pa.shape[0]
    E = D // (2 * pairs)
    W = 2 * E
    KT = L + S
    whole = lambda a: pl.BlockSpec(a.shape, lambda j: (0,) * len(a.shape))
    anywhere = pl.BlockSpec(memory_space=pl.ANY)
    early = lambda j: jnp.minimum(j, pairs - 1)
    late = lambda j: jnp.maximum(j - pairs, 0)
    rows = pl.BlockSpec((n, R, W), lambda j: (0, 0, lax.rem(j, pairs)))
    keys = lambda a: pl.BlockSpec((a.shape[0], W), lambda j: (0, lax.rem(j, pairs)))
    shares = [p_.shape[4:] for p_ in parts] + [(D // 32, D)] * 3
    lines = -(-(2 * D // 128 + 8 * pairs) // 8) * 8
    outs = [jax.ShapeDtypeStruct((n, R, D), BF), jax.ShapeDtypeStruct((lines, 128), F32)]
    outs += [jax.ShapeDtypeStruct(s, F32) for s in shares]
    vmem = lambda *s: pltpu.VMEM(s, BF)
    wide = lambda *s: pltpu.VMEM(s, F32)
    scratch = [vmem(SPAN + E, KT), vmem(R, 2 * W), vmem(2 * W, R), vmem(R, 2 * R), vmem(n, R, SPAN)]
    scratch += [wide(2, SPAN, SPAN), vmem(2 * R, W), vmem(2 * R, W), wide(pairs, W, R)]
    scratch += [vmem(n, R, D), vmem(KT, D), vmem(KT, D), vmem(D, KT), vmem(D, R)]
    scratch += [vmem(3, D, D), vmem(n, R, D), wide(n * R, D)]
    scratch += [vmem(R, D), vmem(S, D), vmem(R, D), vmem(S, D), wide(S, D)]
    scratch += [wide(2 * pairs, 1, 2 * SPAN), wide(lines, 128), wide(4, lines, 128), wide(6, lines, 128)]
    chunks = [(p_.shape[0],) + p_.shape[4:] for p_ in parts]
    copies = Sum.COPIES * (len(chunks) + 3) + 8
    scratch += [pltpu.SemaphoreType.DMA((copies,)), pltpu.SemaphoreType.DMA((copies,)), pltpu.SemaphoreType.DMA((len(chunks) + 12,))]
    scratch += sum([Sum.scratch(*s, 1) for s in chunks], [])
    scratch += [vmem(4, 2, 2, 2, D // 32, D)] * 3
    scratch += sum([Sum.scratch(4, *s, 0) for s in shares[len(parts):]], [])
    return pl.pallas_call(
        functools.partial(backward_kernel, R, L, S, E, pairs, planes),
        grid=(2 * pairs,),
        in_specs=[pl.BlockSpec(memory_space=pltpu.SMEM), rows, keys(kf), keys(vf), keys(ks), keys(vs), rows, rows]
        + [pl.BlockSpec((1, 2, R, R), lambda j: (late(j), 0, 0, 0)), pl.BlockSpec((1, 2, KT - R, R), lambda j: (early(j), 0, 0, 0))]
        + [pl.BlockSpec((3, 1, 2, R), lambda j: (0, lax.rem(j, pairs), 0, 0)), whole(layout)]
        + [anywhere] * (len(parts) + 7)
        + [whole(grow), whole(dg2)],
        out_specs=[anywhere] + [whole(s) for s in outs[1:]],
        out_shape=outs,
        scratch_shapes=scratch,
        compiler_params=pltpu.CompilerParams(
            vmem_limit_bytes=60 * 2**20, dimension_semantics=("arbitrary",), collective_id=1, has_side_effects=True
        ),
        name="backward",
    )(flag, q, kf, vf, ks, vs, o, do, pa, pb, cs, layout, *parts, nkt, nst, wq, wk, wv, tok, dres, grow, dg2)


EPSILON = 1e-06
THRESHOLDS = (12, 16, 23, 32, 46, 64, 91)
BOTH = ("dp", "blk")


def bucket_np(relative):
    magnitude = np.abs(relative)
    larger = 8 + sum((magnitude >= limit).astype(np.int64) for limit in THRESHOLDS)
    return np.where(magnitude < 8, magnitude, larger) + 16 * (relative > 0)


def bucket_rows(distance, buckets):
    return (bucket_np(distance)[:, None] == np.arange(buckets)[None, :]).astype(np.float32)


def norm_parts(x, gain):
    back = lax.rsqrt(jnp.mean(x * x, axis=-1, keepdims=True) + EPSILON)
    return (x * back * gain).astype(BF), back


def norm_back(d, x, back, gain):
    a = gain * d
    grad_gain = jnp.sum(d * x * back, axis=0)
    return back * a - x * back**3 * jnp.mean(a * x, axis=-1, keepdims=True), grad_gain


def mm(a, b, dims):
    return lax.dot_general(a, b, (dims, ((), ())), preferred_element_type=F32)


def gather_weights(gain_one, wq, wk, wv, wo, gain_two, wi, wt):
    full = lambda a: lax.all_gather(a, BOTH, axis=0, tiled=True)
    packed = full(jnp.concatenate([wq, wk, wv, wo, wi], axis=1))
    width = wq.shape[1]
    gains = full(jnp.stack([gain_one, gain_two], axis=1))
    return packed[:, : 3 * width], packed[:, 3 * width : 4 * width], packed[:, 4 * width :], full(wt), gains[:, 0], gains[:, 1]


def scatter_sums(dqkv, dwo, dwi, dwt, dg1, dg2):
    take = lambda a: lax.psum_scatter(a, BOTH, scatter_dimension=0, tiled=True)
    width = dwo.shape[1]
    packed = take(jnp.concatenate([dqkv, dwo, dwi], axis=1).astype(BF)).astype(F32)
    gains = take(jnp.stack([dg1, dg2], axis=1))
    parts = [packed[:, i * width : (i + 1) * width] for i in range(4)]
    return parts, packed[:, 4 * width :], take(dwt.astype(BF)).astype(F32), gains[:, 0], gains[:, 1]


def on_any_device(tokens, layout, lengths, gain_one, wq, wk, wv, wo, gain_two, wi, wt, table, grad_out):
    n, R, D = tokens.shape
    H = table.shape[1]
    G = lax.axis_size("blk")
    me = lax.axis_index("blk")
    L = layout.shape[1]
    S = L // 8
    order = jnp.argsort(-lengths, stable=True)
    place = jnp.argsort(order)
    tok = tokens[order]
    gout = grad_out[order]
    lay = layout[order]
    lens = lengths[order]

    def from_step(x, s):
        return lax.ppermute(x, "blk", [(i, (i - s) % G) for i in range(G)])

    pieces = [tok[:-1]] + [from_step(tok[:-1], s) for s in range(1, G)]
    xf = jnp.concatenate(pieces, axis=1)
    first = tok[-1, :S]
    xs = jnp.where(me == 0, first, sum(lax.ppermute(first, "blk", [(0, i)]) for i in range(1, G)))
    lay_turned = jnp.roll(lay, -me * R, axis=1)
    layq = lay_turned[:, None, :R]
    layf = lay_turned[:-1, None, :]
    lays = lay[-1:, :S]
    spots = (jnp.arange(L) + me * R) % L
    mask = jnp.where(spots[None, :, None] < lens[:-1, None, None], 0.0, -1e30).astype(F32)

    wqkv, wo_all, wi_all, wt_all, g1, g2 = gather_weights(gain_one, wq, wk, wv, wo, gain_two, wi, wt)
    g1 = g1.astype(F32)
    g2 = g2.astype(F32)
    hidden = tok.reshape(n * R, D).astype(F32)
    normed, r1 = norm_parts(hidden, g1)
    xkeys = jnp.concatenate([xf.reshape((n - 1) * L, D), xs], axis=0)
    nkeys, _ = norm_parts(xkeys.astype(F32), g1)
    q = (mm(normed, wqkv[:, :D], ((1,), (0,))).astype(BF) * jnp.asarray(0.125, BF)).reshape(n, R, D)
    k = mm(nkeys, wqkv[:, D : 2 * D], ((1,), (0,))).astype(BF)
    v = mm(nkeys, wqkv[:, 2 * D :], ((1,), (0,))).astype(BF)
    cut = (n - 1) * L
    kf, ks = k[:cut].reshape(n - 1, L, D), k[cut:]
    vf, vs = v[:cut].reshape(n - 1, L, D), v[cut:]
    lane = np.arange(2 * SPAN)
    turned = np.where(lane >= SPAN, lane - 2 * SPAN, lane)
    urow = mm(table, bucket_rows(-turned, table.shape[0]).astype(BF), ((0,), (1,))).reshape(H // 2, 2, 2 * SPAN)
    o, p, l = attend_call(q, kf, vf, ks, vs, layq, layf, lays, mask, urow)

    attended = o.reshape(n * R, D)
    resid = hidden + mm(attended, wo_all, ((1,), (0,)))
    normed_two, r2 = norm_parts(resid, g2)
    pre = mm(normed_two, wi_all, ((1,), (0,)))
    act, act_back = jax.vjp(lambda x: jax.nn.gelu(x, approximate=False), pre)
    act = act.astype(BF)
    mixed = (resid + mm(act, wt_all, ((1,), (0,)))).astype(BF)
    up = gout.reshape(n * R, D)
    dwt = mm(act, up, ((0,), (0,)))
    (dpre,) = act_back(mm(up, wt_all, ((1,), (1,))))
    dpre = dpre.astype(BF)
    dwi = mm(normed_two, dpre, ((0,), (0,)))
    dn2 = mm(dpre, wi_all, ((1,), (1,)))
    dresid, dg2 = norm_back(dn2, resid, r2, g2)
    dresid = dresid + up.astype(F32)
    low = dresid.astype(BF)
    dwo = mm(attended, low, ((0,), (0,)))
    datt = mm(low, wo_all, ((1,), (1,))).astype(BF).reshape(n, R, D)

    dq, dkf, dvf, dks, dvs, t = attend_back_call(q, kf, vf, ks, vs, layq, layf, lays, o, datt, p, l)
    dtable = jnp.einsum(
        "hj,jb->bh", t.reshape(H, 2 * SPAN), bucket_rows(SPAN - 1 - lane, table.shape[0]), precision=lax.Precision.HIGHEST
    )
    dq = dq.reshape(n * R, D)
    dk = jnp.concatenate([dkf.reshape(cut, D), dks], axis=0)
    dv = jnp.concatenate([dvf.reshape(cut, D), dvs], axis=0)
    dnk = mm(dk, wqkv[:, D : 2 * D], ((1,), (1,))) + mm(dv, wqkv[:, 2 * D :], ((1,), (1,)))
    dnf = dnk[:cut].reshape(n - 1, L, D)
    dns = dnk[cut:].astype(BF)
    far = sum(
        lax.ppermute(dnf[:, s * R : (s + 1) * R].astype(BF), "blk", [(i, (i + s) % G) for i in range(G)]).astype(F32)
        for s in range(1, G)
    )
    near = jnp.where(
        me == 0, dnk[cut:] + sum(lax.ppermute(dns, "blk", [(i, 0)]).astype(F32) for i in range(1, G)), 0.0
    )
    extra = jnp.concatenate([dnf[:, :R] + far, jnp.pad(near, ((0, R - S), (0, 0)))[None]], axis=0).reshape(n * R, D)
    dn1 = mm(dq, wqkv[:, :D], ((1,), (1,))) + extra
    dwq = mm(normed, dq, ((0,), (0,)))
    dwk = mm(nkeys, dk, ((0,), (0,)))
    dwv = mm(nkeys, dv, ((0,), (0,)))
    dx, dg1 = norm_back(dn1, hidden, r1, g1)
    gtok = (dresid + dx).astype(BF)
    parts, gwi, gwt, gg1, gg2 = scatter_sums(jnp.concatenate([dwq, dwk, dwv], axis=1), dwo, dwi, dwt, dg1, dg2)
    dtable = lax.psum(dtable, BOTH)
    return (
        mixed.reshape(n, R, D)[place],
        gtok.reshape(n, R, D)[place],
        gg1,
        parts[0],
        parts[1],
        parts[2],
        parts[3],
        gg2,
        gwi,
        gwt,
        dtable,
    )


def on_device(tokens, layout, lengths, gain_one, wq, wk, wv, wo, gain_two, wi, wt, table, grad_out):
    n, R, D = tokens.shape
    H = table.shape[1]
    G = lax.axis_size("blk")
    me = lax.axis_index("blk")
    L = layout.shape[1]
    S = L // 8
    lane = np.arange(2 * SPAN)
    turned = np.where(lane >= SPAN, lane - 2 * SPAN, lane)
    basis = jnp.asarray(bucket_rows(-turned, table.shape[0]).T, BF)
    gains = jnp.pad(jnp.stack([gain_one, gain_two], axis=1), ((0, 0), (0, 126)))
    o, pa, pb, cs, grow, q, kf, vf, ks, vs, nkt, nst, *wholes = forward_call(
        lengths, tokens, layout, table, basis, [gains, wq, wk, wv, wo, wi, wt], S
    )
    flat = lambda a: a.reshape(-1, a.shape[-1])
    wq_all, wk_all, wv_all, wo_all, wi_all, wt_all = [flat(a) for a in wholes]
    rows = lambda a: a.reshape(n * R, D)
    mixed, dresid, datt, dwo, *handed = feed_forward_call(
        lengths, rows(o), rows(tokens), rows(grad_out), wo_all, grow, wi_all, wt_all
    )
    count = 2 * (4 - FF_SUMS)
    dg2, done = handed[count], handed[count + 1 :]
    planes = sum([(None, j) for j in range(FF_SUMS, 4)], ()) + (None,)
    gtok, small, *sums = backward_call(
        lengths, q, kf, vf, ks, vs, o, datt.reshape(n, R, D), pa, pb, cs, layout,
        handed[:count] + [dwo.reshape(4, 2, 2, 2, -1, D)], planes,
        nkt, nst, wq_all, wk_all, wv_all, tokens, dresid, grow, dg2,
    )
    gwo, gwq, gwk, gwv = sums[count:]
    gwi = jnp.concatenate(done[:FF_SUMS] + sums[0:count:2], axis=1)
    gwt = done[FF_SUMS]
    for j in range(FF_SUMS, 4):
        gwt = jnp.where(lax.axis_index("dp") // 4 == j, sums[2 * (j - FF_SUMS) + 1], gwt)
    small = small.reshape(-1)
    mine = (lax.axis_index("dp") * G + me) * (D // 32)
    gg1, gg2 = [lax.dynamic_slice_in_dim(small, mine + i * D, D // 32) for i in range(2)]
    t = small[2 * D : 2 * D + H * 2 * SPAN].reshape(H, 2 * SPAN)
    dtable = jnp.einsum(
        "hj,jb->bh", t, bucket_rows(SPAN - 1 - lane, table.shape[0]), precision=lax.Precision.HIGHEST
    )
    return mixed.reshape(n, R, D), gtok, gg1, gwq, gwk, gwv, gwo, gg2, gwi, gwt, dtable


def solution(mesh):
    rows = P(BOTH, None)
    items = P("dp", "blk", None)
    known = dict(mesh.shape) == {"dp": 16, "blk": 2}

    def body(tokens, *rest):
        return (on_device if known and tokens.shape[0] == 2 else on_any_device)(tokens, *rest)

    return jax.shard_map(
        body,
        mesh=mesh,
        in_specs=(items, P("dp", None), P("dp"), P(BOTH), rows, rows, rows, rows, P(BOTH), rows, rows, P(), items),
        out_specs=(items, items, P(BOTH), rows, rows, rows, rows, P(BOTH), rows, rows, P()),
        check_vma=False,
    )
```

```python
import functools
import math

import jax
import jax.numpy as jnp
import numpy as np
from jax import lax
from jax.experimental import pallas as pl
from jax.experimental.pallas import tpu as pltpu
from jax.sharding import PartitionSpec as P

F32=jnp.float32; BF=jnp.bfloat16
SPAN=256
CH=256
def dot(a,b): return lax.dot_general(a,b,(((1,),(0,)),((),())),preferred_element_type=F32)
def eye_of(row, width, reverse):
    spots=lax.broadcasted_iota(jnp.int32,(width,row.shape[1]),0)
    if reverse: spots=width-1-spots
    return (spots==row).astype(F32).astype(BF)

def attend(n,L,S,R,E, q,kf,vf,ks,vs,layq,layf,lays,mask,u,o,p,l, kcat,qcat,vt,s_ref,ohq):
    W=2*E
    spans=[L]*(n-1)+[S]
    @pl.when(pl.program_id(0)==0)
    def _():
        base=0
        for i,m in enumerate(spans):
            row=layf[i] if i<n-1 else lays[...]
            kcat[base:base+m,W:]=jnp.transpose(eye_of(row,SPAN,False).astype(F32)).astype(BF)
            ohq[i]=eye_of(layq[i],SPAN,False)
            base+=m
        vt[:,E:]=jnp.ones((2,vt.shape[1]-E,vt.shape[2]),BF)
    pair=pl.program_id(0)
    base=0
    for i,m in enumerate(spans):
        ch=min(CH,m)
        kcat[base:base+m,:W]=kf[i] if i<n-1 else ks[...]
        v=vf[i] if i<n-1 else vs[...]
        vtr=jnp.transpose(v.astype(F32)).astype(BF)
        vt[0,:E,:m]=vtr[:E]
        vt[1,:E,:m]=vtr[E:]
        qt=jnp.transpose(q[i].astype(F32)).astype(BF)
        outs=[]
        for h in range(2):
            urow=u[pl.ds(0,1),h,:] if False else u[0,h:h+1,:]
            toep=pltpu.roll(jnp.broadcast_to(urow,(SPAN,2*SPAN)),0,1,stride=1,stride_axis=0)[:,:SPAN].astype(BF)
            qcat[h*E:(h+1)*E]=qt[h*E:(h+1)*E]
            qcat[(1-h)*E:(2-h)*E]=jnp.zeros((E,R),BF)
            qcat[W:]=dot(toep,ohq[i]).astype(BF)
            m8=jnp.full((8,R),-jnp.inf,F32)
            for c in range(0,m,ch):
                s=dot(kcat[base+c:base+c+ch],qcat[...])
                if 0<i<n-1: s=s+mask[i,c:c+ch,:]
                s_ref[c:c+ch]=s
                m8=jnp.maximum(m8,jnp.max(s.reshape(ch//8,8,R),axis=0))
            top=jnp.max(m8,axis=0,keepdims=True)
            for c in range(0,m,ch):
                p[0,h,base+c:base+c+ch]=jnp.exp(s_ref[c:c+ch]-top).astype(BF)
            full=dot(vt[h,:,:m],p[0,h,base:base+m])
            total=full[E:E+1]
            l[i,0,h:h+1]=total
            outs.append(full[:E]/total)
        o[i]=jnp.transpose(jnp.concatenate(outs,axis=0)).astype(BF)
        base+=m

def attend_call(q,kf,vf,ks,vs,layq,layf,lays,mask,u):
    n,R,D=q.shape; L=kf.shape[1]; S=ks.shape[0]; H=u.shape[0]*2; E=D//H; W=2*E
    KT=(n-1)*L+S
    full=lambda a: pl.BlockSpec(a.shape,lambda j:(0,)*a.ndim)
    return pl.pallas_call(functools.partial(attend,n,L,S,R,E),
      grid=(H//2,),
      in_specs=[pl.BlockSpec((n,R,W),lambda j:(0,0,j)),
        pl.BlockSpec((n-1,L,W),lambda j:(0,0,j)),pl.BlockSpec((n-1,L,W),lambda j:(0,0,j)),
        pl.BlockSpec((S,W),lambda j:(0,j)),pl.BlockSpec((S,W),lambda j:(0,j)),
        full(layq),full(layf),full(lays),full(mask),pl.BlockSpec((1,2,2*SPAN),lambda j:(j,0,0))],
      out_specs=[pl.BlockSpec((n,R,W),lambda j:(0,0,j)),
        pl.BlockSpec((1,2,KT,R),lambda j:(j,0,0,0)),
        pl.BlockSpec((n,1,2,R),lambda j:(0,j,0,0))],
      out_shape=[jax.ShapeDtypeStruct((n,R,D),BF),jax.ShapeDtypeStruct((H//2,2,KT,R),BF),jax.ShapeDtypeStruct((n,H//2,2,R),F32)],
      scratch_shapes=[pltpu.VMEM((KT,W+SPAN),BF),pltpu.VMEM((W+SPAN,R),BF),pltpu.VMEM((2,E+16,L),BF),pltpu.VMEM((L,R),F32),pltpu.VMEM((n,SPAN,R),BF)],
      compiler_params=pltpu.CompilerParams(vmem_limit_bytes=56*2**20,dimension_semantics=("arbitrary",)),
      name="attend",
    )(q,kf,vf,ks,vs,layq,layf,lays,mask,u)

def attend_back(n,L,S,R,E, q,kf,vf,ks,vs,layq,layf,lays,o,do,p,l, dq,dkf,dvf,dks,dvs,t, kq,vaug,rhs,ds,ohq,nacc,qm,dm):
    W=2*E
    spans=[L]*(n-1)+[S]
    @pl.when(pl.program_id(0)==0)
    def _():
        base=0
        for i,m in enumerate(spans):
            row=layf[i] if i<n-1 else lays[...]
            kq[:SPAN,base:base+m]=eye_of(row,SPAN,True)
            ohq[i]=jnp.transpose(eye_of(layq[i],SPAN,False).astype(F32)).astype(BF)
            base+=m
        vaug[:,W:]=(lax.broadcasted_iota(jnp.int32,(vaug.shape[0],W),1)<2).astype(F32).astype(BF)
        rhs[...]=jnp.zeros_like(rhs)
    nacc[...]=jnp.zeros_like(nacc)
    base=0
    lane=lax.broadcasted_iota(jnp.int32,(R,W),1)
    for i,m in enumerate(spans):
        ch=min(CH,m)
        kk=kf[i] if i<n-1 else ks[...]
        vaug[:m,:W]=vf[i] if i<n-1 else vs[...]
        kt=jnp.transpose(kk.astype(F32)).astype(BF)
        dot_=jnp.transpose(do[i].astype(F32))
        ot=jnp.transpose(o[i].astype(F32))
        scaled=[];
        for h in range(2):
            inv=1.0/l[i,0,h:h+1]
            scaled.append((dot_[h*E:(h+1)*E]*inv).astype(BF))
        sc=jnp.concatenate(scaled,axis=0)
        don=jnp.transpose(sc.astype(F32)).astype(BF)
        qq=q[i]
        zero=jnp.zeros((R,W),BF)
        for h in range(2):
            mine=(lane<E) if h==0 else (lane>=E)
            qm[h*R:(h+1)*R]=jnp.where(mine,qq,zero)
            dm[h*R:(h+1)*R]=jnp.where(mine,don,zero)
        dqs=[]
        for h in range(2):
            rhs[h*E:(h+1)*E]=scaled[h]
            rhs[(1-h)*E:(2-h)*E]=jnp.zeros((E,R),BF)
            delta=jnp.sum(scaled[h].astype(F32)*ot[h*E:(h+1)*E],axis=0,keepdims=True)
            hi=delta.astype(BF).astype(F32)
            lo=delta-hi
            spot=lax.broadcasted_iota(jnp.int32,(16,R),0)
            rhs[W:W+16]=jnp.where(spot==0,-hi,jnp.where(spot==1,-lo,0.0)).astype(BF)
            for c in range(0,m,ch):
                g=dot(vaug[c:c+ch],rhs[...])
                ds[c:c+ch,h*R:(h+1)*R]=(p[0,h,base+c:base+c+ch].astype(F32)*g).astype(BF)
            kq[SPAN:,base:base+m]=kt[h*E:(h+1)*E]
            both=dot(kq[:,base:base+m],ds[:m,h*R:(h+1)*R])
            dqs.append(both[SPAN:]*0.125)
            nacc[h]+=dot(both[:SPAN].astype(BF),ohq[i])
        dq[i]=jnp.transpose(jnp.concatenate(dqs,axis=0)).astype(BF)
        for c in range(0,m,ch):
            dk=dot(ds[c:c+ch],qm[...])
            dv=dot(p[0,0,base+c:base+c+ch],dm[:R])+dot(p[0,1,base+c:base+c+ch],dm[R:])
            if i<n-1:
                dkf[i,c:c+ch]=dk.astype(BF); dvf[i,c:c+ch]=dv.astype(BF)
            else:
                dks[c:c+ch]=dk.astype(BF); dvs[c:c+ch]=dv.astype(BF)
        base+=m
    for h in range(2):
        wide=jnp.concatenate([nacc[h],jnp.zeros((SPAN,SPAN),F32)],axis=1)
        rolled=pltpu.roll(wide,0,1,stride=1,stride_axis=0)
        t[0,h:h+1]=jnp.sum(rolled,axis=0,keepdims=True)

def attend_back_call(q,kf,vf,ks,vs,layq,layf,lays,o,do,p,l):
    n,R,D=q.shape; L=kf.shape[1]; S=ks.shape[0]; H=p.shape[0]*2; E=D//H; W=2*E
    KT=(n-1)*L+S
    full=lambda a: pl.BlockSpec(a.shape,lambda j:(0,)*a.ndim)
    rows=lambda: pl.BlockSpec((n,R,W),lambda j:(0,0,j))
    kb=lambda: pl.BlockSpec((n-1,L,W),lambda j:(0,0,j))
    sb=lambda: pl.BlockSpec((S,W),lambda j:(0,j))
    return pl.pallas_call(functools.partial(attend_back,n,L,S,R,E),
      grid=(H//2,),
      in_specs=[rows(),kb(),kb(),sb(),sb(),full(layq),full(layf),full(lays),rows(),rows(),
        pl.BlockSpec((1,2,KT,R),lambda j:(j,0,0,0)),pl.BlockSpec((n,1,2,R),lambda j:(0,j,0,0))],
      out_specs=[rows(),kb(),kb(),sb(),sb(),pl.BlockSpec((1,2,2*SPAN),lambda j:(j,0,0))],
      out_shape=[jax.ShapeDtypeStruct((n,R,D),BF),jax.ShapeDtypeStruct(kf.shape,BF),jax.ShapeDtypeStruct(kf.shape,BF),
        jax.ShapeDtypeStruct(ks.shape,BF),jax.ShapeDtypeStruct(ks.shape,BF),jax.ShapeDtypeStruct((H//2,2,2*SPAN),F32)],
      scratch_shapes=[pltpu.VMEM((SPAN+E,KT),BF),pltpu.VMEM((L,2*W),BF),pltpu.VMEM((2*W,R),BF),pltpu.VMEM((L,2*R),BF),
        pltpu.VMEM((n,R,SPAN),BF),pltpu.VMEM((2,SPAN,SPAN),F32),pltpu.VMEM((2*R,W),BF),pltpu.VMEM((2*R,W),BF)],
      compiler_params=pltpu.CompilerParams(vmem_limit_bytes=56*2**20,dimension_semantics=("arbitrary",)),
      name="attend_back",
    )(q,kf,vf,ks,vs,layq,layf,lays,o,do,p,l)


EPSILON = 1e-06
FORWARD_TOKENS = (-8.5, -8, -7, -6, -5, -4, -3, -2)
FORWARD_PIECES = 3
FORWARD_WAYS = (0,) * 5 + (1,) * 4 + (0,) * 2
FORWARD_AT = (
    (-9, -8, -7, -6, -5),
    (-8, -7, -6, -5, -4),
    (-7, -6, -5, -4, -3),
    (-6, -5, -4, -3, -2),
    (-5, -4, -3, -2, 4),
    (-4, -3, -2, 4, 8),
    (-3, -2, 4, 8, 12),
    (-2, 4, 8, 12, 16),
    (4, 8, 12, 16, 20),
    (8, 12, 16, 20, 24),
)
FF_SUMS = 3
FF_SUM = (0, 2)
FF_SUM_LAG = (0, 3, 7, 11, 16)
BACK_SUM = (2, 2, 4)


MESH = pl.DeviceIdType.MESH


class Place:
    def __init__(self, mostly_y=False):
        dp = lax.axis_index("dp")
        self.x = lax.axis_index("blk")
        self.z, self.y, self.c = dp // 4, (dp // 2) % 2, dp % 2
        c = 1 if mostly_y else self.c
        self.y1, self.x1 = (self.y + 1 - c) % 2, (self.x + c) % 2
        self.y2, self.x2 = (self.y + c) % 2, (self.x + 1 - c) % 2

    def device(self, z, y, c, x):
        return ((z * 2 + y) * 2 + c, x)

    def along_z(self, d):
        return self.device((self.z + d) % 4, self.y, self.c, self.x)

    def along_x(self):
        return self.device(self.z, self.y, self.c, 1 - self.x)

    def along_y(self):
        return self.device(self.z, 1 - self.y, self.c, self.x)

    def first(self):
        return self.device(self.z, self.y1, self.c, self.x1)

    def second(self):
        return self.device(self.z, self.y2, self.c, self.x2)

    def core(self):
        return self.device(self.z, self.y, 1 - self.c, self.x)

    def greet(self):
        barrier = pltpu.get_barrier_semaphore()
        partners = [self.along_z(d) for d in (1, 2, 3)] + [self.first(), self.second(), self.core()]
        for partner in partners:
            pl.semaphore_signal(barrier, inc=1, device_id=partner, device_id_type=MESH)
        pl.semaphore_wait(barrier, len(partners))


def remote(src, dst, sems, k, device):
    return pltpu.make_async_remote_copy(
        src_ref=src, dst_ref=dst, send_sem=sems[0].at[k], recv_sem=sems[1].at[k], device_id=device, device_id_type=MESH
    )


GATHER_COPIES = 10


def gather_stages(at, shard, whole, sems, local, base, cols=None, plane=None):
    z, y, c, x = at.z, at.y, at.c, at.x
    cols = pl.ds(0, shard.shape[1]) if cols is None else cols
    shard = shard.at[:, cols]
    own = whole.at[z if plane is None else 0, y, c, x]
    keep = pltpu.make_async_copy(shard, own, local)

    def group(yy, xx):
        return whole.at[:, yy, c, xx]

    def copy(k):
        if k < 3:
            return remote(shard, own, sems, base + k, at.along_z(k + 1))
        view, device = {
            3: (group(y, x), at.first()),
            4: (group(y, x), at.second()),
            5: (group(y, x), at.core()),
            6: (group(at.y1, at.x1), at.second()),
            7: (group(at.y1, at.x1), at.core()),
            8: (group(at.y2, at.x2), at.core()),
            9: (group(1 - y, 1 - x), at.core()),
        }[k]
        return remote(view, view, sems, base + k, device)

    def one():
        def start():
            keep.start()
            for k in range(3):
                copy(k).start()

        start() if plane is None else pl.when(z == plane)(start)

    def two():
        if plane is None:
            keep.wait()
            for k in range(3):
                copy(k).wait_recv()
        else:
            pl.when(z == plane)(keep.wait)
            d = (z - plane + 4) % 4
            arrival = remote(shard, own, sems, base + d - 1, at.along_z(1))
            pl.when(z != plane)(arrival.wait_recv)
        for k in (3, 4, 5):
            copy(k).start()

    def three():
        copy(3).wait_recv()
        for k in (6, 7):
            copy(k).start()

    def four():
        copy(4).wait_recv()
        copy(8).start()
        copy(6).wait_recv()
        copy(9).start()

    def five():
        for k in (5, 7, 8, 9):
            copy(k).wait_recv()
        for k in range(3, 10):
            copy(k).wait_send()

        def sent():
            for k in range(3):
                copy(k).wait_send()

        sent() if plane is None else pl.when(z == plane)(sent)

    return [one, two, three, four, five]


def gather_stages_x(at, shard, whole, sems, local, base):
    z, y, c, x = at.z, at.y, at.c, at.x
    own = whole.at[z, y, c, x]
    keep = pltpu.make_async_copy(shard, own, local)

    def copy(k):
        if k == 0:
            return remote(shard, own, sems, base, at.along_x())
        view, device = {
            1: (whole.at[z, y, c], at.along_z(1)),
            2: (whole.at[z, y, c], at.along_z(2)),
            3: (whole.at[z, y, c], at.along_z(3)),
            4: (whole.at[:, y, c], at.along_y()),
            5: (whole.at[:, y, c], at.core()),
            6: (whole.at[:, 1 - y, c], at.core()),
        }[k]
        return remote(view, view, sems, base + k, device)

    def step(arrivals, starts):
        def run():
            for k in arrivals:
                copy(k).wait_recv()
            for k in starts:
                copy(k).start()

        return run

    def one():
        keep.start()
        copy(0).start()

    def two():
        keep.wait()
        step((0,), (1, 2, 3))()

    def five():
        step((5, 6), ())()
        for k in range(7):
            copy(k).wait_send()

    return [one, two, step((1, 2, 3), (4, 5)), step((4,), (6,)), five]


def small_stages(at, part, total, held, got, sems, base):
    def copy(k):
        device = [at.core, at.along_y, at.along_x][k]() if k < 3 else at.along_z(k - 2)
        return remote(held.at[min(k, 3)], got.at[k], sems, base + k, device)

    def one():
        held[0] = part[...]
        copy(0).start()

    def add(k):
        def run():
            copy(k).wait_recv()
            held[k + 1] = held[k] + got[k]
            for following in (k + 1,) if k < 2 else (3, 4, 5):
                copy(following).start()

        return run

    def five():
        parts = [held[3]]
        for d in (1, 2, 3):
            copy(2 + d).wait_recv()
            parts.append(got[2 + d])
        out = jnp.zeros_like(parts[0])
        for spot in range(4):
            for d in range(4):
                out = out + jnp.where((at.z - d + 4) % 4 == spot, parts[d], 0.0)
        total[...] = out
        for k in range(6):
            copy(k).wait_send()

    return [one, add(0), add(1), add(2), five]


def norm_rows(x):
    return lax.rsqrt(jnp.mean(x * x, axis=1, keepdims=True) + EPSILON)


def dot_nt(a, b):
    return lax.dot_general(a, b, (((1,), (1,)), ((), ())), preferred_element_type=F32)


def flipped(a):
    return jnp.transpose(a.astype(F32)).astype(BF)


TICKS = 6


def feed_forward_plan(sums):
    events = []
    for i, (stages, j) in enumerate(sums):
        for s, lag in enumerate(FF_SUM_LAG):
            events.append((TICKS * (j + 1) + FF_SUM[i % 2] + lag, stages[s]))
    plan = {}
    for when, stage in sorted(events, key=lambda e: e[0]):
        plan.setdefault(when, []).append(stage)
    return plan


def feed_forward(R, blocks, *refs):
    flag, att_, tok_, up_, wo_, grow = refs[:6]
    given = refs[6:8]
    refs = list(refs[8:])
    take = lambda k: [refs.pop(0) for _ in range(k)]
    mixed, dres, datt, dwo = take(4)
    last = FF_SUMS
    handed = [take(2) for _ in range(last, blocks)]
    (dgain,) = take(1)
    totals_in = take(last)
    (total_out,) = take(1)
    att, tok, up, wo, wbi, wbt, n2, n2t, resid, acc, dn2, act_t, dpre_s, parts_in, parts_out = take(15)
    sum_scratch = [take(5) for _ in range(2 * last)]
    send, recv, local = take(3)
    rows, width = att.shape
    block = wbi.shape[2]
    piece = rows // 4
    pieces = [pl.ds(i, piece) for i in range(0, rows, piece)]
    step = pl.program_id(0)
    slot = lax.rem(step, 2)
    at = Place()
    sems = (send, recv)

    sums = []
    for j in range(last):
        for which, (part, total) in enumerate([(parts_in.at[j], totals_in[j]), (parts_out.at[j], total_out)]):
            i = len(sums)
            chain = Sum(at, part, total, sum_scratch[i], sems, None, Sum.COPIES * i, None, j if which else None)
            sums.append((chain.stages, j))
    plan = feed_forward_plan(sums)

    def local_copy(a, b, k):
        return pltpu.make_async_copy(a, b, local.at[k])

    def weights(j):
        hidden = pl.ds(j * block, block)
        return [local_copy(given[0].at[:, hidden], wbi.at[j % 2], 4), local_copy(given[1].at[hidden], wbt.at[j % 2], 5)]

    def tick(t):
        for when in plan:
            if when < TICKS * blocks and when % TICKS == t:

                @pl.when(step == when // TICKS)
                def _(when=when):
                    for stage in plan[when]:
                        stage()

    @pl.when(step == 0)
    def _():
        loads = [local_copy(a, b, i) for i, (a, b) in enumerate([(tok_, tok), (att_, att), (wo_, wo), (up_, up)])]
        for load in loads + weights(0):
            load.start()
        at.greet()
        for load in loads:
            load.wait()
        for a in (tok, up):
            a[:R], a[R:] = swapped(flag, a[:R], a[R:])
        for b in pieces:
            x = tok[b].astype(F32) + dot(att[b], wo[...])
            resid[b] = x
            normed = (x * norm_rows(x) * grow[1:2]).astype(BF)
            n2[b] = normed
            n2t[:, b] = flipped(normed)
            acc[b] = x
            dn2[b] = jnp.zeros_like(x)

    for j in range(blocks):

        @pl.when(step == j)
        def _(j=j):
            for load in weights(j):
                load.wait()
            if j + 1 < blocks:
                for load in weights(j + 1):
                    load.start()

    for i, b in enumerate(pieces):
        tick(i)
        pre = dot(n2[b], wbi[slot])
        dact = dot_nt(up[b], wbt[slot])
        half = 0.5 + 0.5 * lax.erf(pre * 0.7071067811865476)
        act = (pre * half).astype(BF)
        dpre = (dact * (half + pre * (jnp.exp(-0.5 * pre * pre) * 0.3989422804014327))).astype(BF)
        acc[b] += dot(act, wbt[slot])
        dn2[b] += dot_nt(dpre, wbi[slot])
        act_t[:, b] = flipped(act)
        dpre_s[b] = dpre
    tick(4)
    grad_in = dot(n2t[...], dpre_s[...])
    tick(5)
    grad_out = dot(act_t[...], up[...])

    into_slabs(grad_in, parts_in.at[step])
    count = parts_out.shape[5]
    for i in range(8):
        parts_out[step, 0, i // 4, i // 2 % 2, i % 2] = grad_out[count * i : count * (i + 1)].astype(BF)
    hand = [
        [local_copy(parts_in.at[j], handed[j - last][0], 6 + 2 * j), local_copy(parts_out.at[j], handed[j - last][1], 7 + 2 * j)]
        for j in range(last, blocks)
    ]
    for j in range(last, blocks):

        @pl.when(step == j)
        def _(j=j):
            for copy in hand[j - last]:
                copy.start()

    @pl.when(step == blocks - 1)
    def _():
        rest = [stage for t in sorted(plan) if t >= TICKS * blocks for stage in plan[t]]

        def some(count):
            for _ in range(min(count, len(rest))):
                rest.pop(0)()

        ends = []
        some(2)
        for i, b in enumerate(pieces):
            n2[b] = acc[b].astype(BF)
        n2[:R], n2[R:] = swapped(flag, n2[:R], n2[R:])
        ends.append(local_copy(n2, mixed, 2))
        ends[-1].start()
        total = None
        for b in pieces:
            x, d = resid[b], dn2[b]
            back = norm_rows(x)
            a = grow[1:2] * d
            part = jnp.sum(d * x * back, axis=0, keepdims=True)
            total = part if total is None else total + part
            g = up[b].astype(F32) + back * a - x * (back * back * back) * jnp.mean(a * x, axis=1, keepdims=True)
            dn2[b] = g
            g = g.astype(BF)
            up[b] = g
            tok[b] = dot_nt(g, wo[...]).astype(BF)
            act_t[:width, b] = flipped(att[b])
            some(1)
        dgain[...] = total
        ends += [local_copy(dn2, dres, 3), local_copy(tok, datt, 4)]
        ends[-1].start()
        ends[-2].start()
        dpre_s[:width, :width] = dot(act_t[:width], up[...]).astype(BF)
        ends.append(local_copy(dpre_s.at[pl.ds(0, width), pl.ds(0, width)], dwo, 5))
        ends[-1].start()
        some(100)
        for end in ends + sum(hand, []):
            end.wait()


def feed_forward_call(flag, att, tokens, up, wo, grow, wi, wt):
    rows, D = tokens.shape
    R = rows // 2
    blocks = 4
    last = FF_SUMS
    block = wi.shape[1] // blocks
    share_in, share_out = (D // 32, block), (wt.shape[0] // 32, D)
    anywhere = pl.BlockSpec(memory_space=pl.ANY)
    whole = lambda shape: pl.BlockSpec(shape, lambda j: (0,) * len(shape))
    vmem = lambda *s: pltpu.VMEM(s, BF)
    wide = lambda *s: pltpu.VMEM(s, F32)
    slab_in, slab_out = (4, 2, 2, 2) + share_in, (1, 2, 2, 2) + share_out
    outs = [((rows, D), BF), ((rows, D), F32), ((rows, D), BF), ((D, D), BF)] + [(slab_in, BF), (slab_out, BF)] * (blocks - last)
    small = [((1, D), F32)] + [(share_in, F32)] * last + [(share_out, F32)]
    copies = max(Sum.COPIES * 2 * last, 1)
    scratch = [vmem(rows, D)] * 3 + [vmem(D, D), vmem(2, D, block), vmem(2, block, D), vmem(rows, D), vmem(D, rows)]
    scratch += [wide(rows, D)] * 3 + [vmem(block, rows), vmem(rows, block), vmem(blocks, *slab_in), vmem(blocks, *slab_out)]
    scratch += (Sum.scratch(4, *share_in, 0) + Sum.scratch(1, *share_out, 0)) * last
    scratch += [pltpu.SemaphoreType.DMA((copies,))] * 2 + [pltpu.SemaphoreType.DMA((6 + 2 * blocks,))]
    return pl.pallas_call(
        functools.partial(feed_forward, R, blocks),
        grid=(blocks,),
        in_specs=[pl.BlockSpec(memory_space=pltpu.SMEM)] + [anywhere] * 4 + [whole(grow.shape)] + [anywhere] * 2,
        out_specs=[anywhere] * len(outs) + [whole(s) for s, _ in small],
        out_shape=[jax.ShapeDtypeStruct(*s) for s in outs + small],
        scratch_shapes=scratch,
        compiler_params=pltpu.CompilerParams(
            vmem_limit_bytes=60 * 2**20, dimension_semantics=("arbitrary",), collective_id=2, has_side_effects=True
        ),
        name="feed_forward",
    )(flag, att, tokens, up, wo, grow, wi, wt)


def turn_plan(chains, places):
    plan = {}
    for chain, at in zip(chains, places):
        for place, stage in zip(at, chain):
            plan.setdefault(place, []).insert(0, stage)
    return plan


def together(*chains):
    def stage(s):
        def run():
            for chain in chains:
                chain[s]()

        return run

    return [stage(s) for s in range(len(chains[0]))]


def unslab(slabs, flat):
    rows = slabs.shape[4]
    for i in range(16):
        pair = [slabs[i // 4, i // 2 % 2, i % 2, x] for x in range(2)]
        flat[2 * rows * i : 2 * rows * (i + 1)] = jnp.concatenate(pair, axis=0)


def normed_rows(x, gain):
    x = x.astype(F32)
    return (x * norm_rows(x) * gain).astype(BF)


def block_chain(ats, shard_in, shard_out, j, whole_in, whole_out, sems, local, k):
    width = whole_in.shape[5]
    return [
        gather_stages(ats[0], shard_in, whole_in, sems, local.at[k], GATHER_COPIES * k, pl.ds(j * width, width)),
        gather_stages(ats[1], shard_out, whole_out, sems, local.at[k + 1], GATHER_COPIES * (k + 1), None, j),
    ]


def swapped(lengths, a, b):
    turn = lengths[0] < lengths[1]
    return jnp.where(turn, b, a), jnp.where(turn, a, b)


def coordinates(at, lengths, layout, R, S):
    long, short = swapped(lengths, layout[0:1], layout[1:2])
    keys = jnp.where(at.x == 0, long, jnp.concatenate([long[:, R:], long[:, :R]], axis=1))
    return keys, short[:, :S], keys[:, :R], jnp.where(at.x == 0, short[:, :R], short[:, R:])


def forward_kernel(R, L, S, E, pairs, *refs):
    flag, tokens, layout, table, basis = refs[:5]
    shards = refs[5:12]
    refs = list(refs[12:])
    take = lambda k: [refs.pop(0) for _ in range(k)]
    o, pa, pb, cs, grow = take(5)
    kept = take(7)
    wholes = take(6)
    kcat, qcat, vt, s_ref, ohq, xfar, xshort, flat, normed, tok, held, stats, u = take(13)
    q, kf, vf, ks, vs, nkt, nst = inner = take(7)
    slabs = take(4)
    send, recv, local = take(3)
    W = 2 * E
    D = tok.shape[2]
    at = Place()
    sems = (send, recv)
    ways = [(at, Place(True))[i] for i in FORWARD_WAYS]
    targets = slabs + wholes[3:]
    chains = []
    for i, cols in [(i, None) for i in range(5)] + [(i, cols) for i in (5, 6) for cols in pieces_of(shards[i].shape[1])]:
        k = len(chains)
        view = targets[i] if cols is None else targets[i].at[:, :, :, :, :, cols]
        chains.append(gather_stages(ways[k], shards[i], view, sems, local.at[k], GATHER_COPIES * k, cols))
    count = len(chains)
    chains = [together(chains[0], chains[1])] + chains[2:]
    plan = turn_plan(chains, FORWARD_AT)
    spare = GATHER_COPIES * count
    short = remote(tok.at[1, pl.ds(0, S)], xshort, sems, spare, at.along_x())
    long = []
    for i in range(len(FORWARD_TOKENS)):
        some = pl.ds(i * R // len(FORWARD_TOKENS), R // len(FORWARD_TOKENS))
        long.append(remote(tok.at[0, some], xfar.at[some], sems, spare + 1 + i, at.along_x()))
    out = lambda i, a, b: pltpu.make_async_copy(a, b, local.at[count + i])
    weights_out = [out(i, slabs[1 + i], wholes[i]) for i in range(3)]
    kept_out = [out(3 + i, a, b) for i, (a, b) in enumerate(zip(inner, kept))]

    for place, copy in zip(FORWARD_TOKENS, long):
        plan.setdefault(place, []).append(copy.start)
    plan[FORWARD_TOKENS[-1]].append(lambda: pl.when(at.x == 0)(short.start))

    def turn(t):
        for stage in plan.get(t, []):
            stage()

    step = pl.program_id(0)
    pair = lax.rem(step, pairs)

    @pl.when(step == 0)
    def _():
        at.greet()
        turn(-9)
        tok[0], tok[1] = swapped(flag, tokens[0], tokens[1])
        turn(-8.5)
        long_keys, short_keys, *queries = coordinates(at, flag, layout, R, S)
        for i, (base, row) in enumerate([(0, long_keys), (L, short_keys)]):
            kcat[base : base + row.shape[1], W:] = jnp.transpose(eye_of(row, SPAN, False).astype(F32)).astype(BF)
            ohq[i] = eye_of(queries[i], SPAN, False)
        rows = lax.dot_general(table[...].astype(BF), basis[...], (((0,), (0,)), ((), ())), preferred_element_type=F32)
        for h in range(2 * pairs):
            u[h] = rows[h : h + 1]
        vt[:, E:] = jnp.ones((2, vt.shape[1] - E, vt.shape[2]), BF)
        for t in range(-8, -4):
            turn(t)
        gslab = slabs[0]
        columns = jnp.concatenate(
            [gslab[i // 8, i // 4 % 2, i // 2 % 2, i % 2].astype(F32) for i in range(32)], axis=0
        )
        grow[...] = jnp.transpose(columns)[:8]
        gain = grow[0:1]
        weights_out[0].start()
        unslab(slabs[1], flat.at[0])
        for i in range(2):
            normed[i] = normed_rows(tok[i], gain)
            q[i] = (dot(normed[i], flat[0]).astype(BF).astype(F32) * 0.125).astype(BF)
        turn(-4)
        weights_out[1].start()
        unslab(slabs[2], flat.at[0])
        kf[:R] = dot(normed[0], flat[0]).astype(BF)
        turn(-3)
        weights_out[2].start()
        unslab(slabs[3], flat.at[1])
        vf[:R] = dot(normed[0], flat[1]).astype(BF)
        kept_out[0].start()
        turn(-2)

    @pl.when(step == pairs)
    def _():
        nkt[:, :R] = flipped(normed[0])
        nst[...] = flipped(normed[1])
        for copy in long:
            copy.wait()

        @pl.when(at.x == 0)
        def _():
            short.wait_send()

        @pl.when(at.x == 1)
        def _():
            short.wait_recv()

        @pl.when(at.x == 0)
        def _():
            xshort[...] = tok[1, :S]

        gain = grow[0:1]
        normed[0] = normed_rows(xfar[...], gain)
        normed[1, :S] = normed_rows(xshort[...], gain)
        kf[R:] = dot(normed[0], flat[0]).astype(BF)
        vf[R:] = dot(normed[0], flat[1]).astype(BF)
        ks[...] = dot(normed[1, :S], flat[0]).astype(BF)
        vs[...] = dot(normed[1, :S], flat[1]).astype(BF)
        nkt[:, R:L] = flipped(normed[0])
        nkt[:, L:] = flipped(normed[1, :S])
        for copy in kept_out[1:]:
            copy.start()

    steps = 2 * pairs

    def tick(spot):
        for t in sorted(plan):
            if t >= 2 * steps and spot == 2 or 0 <= t < 2 * steps and t % 2 == spot:

                @pl.when(step == min(t // 2, steps - 1))
                def _(t=t):
                    turn(t)

    here = pl.ds(pl.multiple_of(pair * W, W), W)

    def attend_to(i, base, m, keys, values, into, ticking):
        ch = min(CH, m)
        kcat[base : base + m, :W] = keys
        vt[0, :E, :m], vt[1, :E, :m] = jnp.split(flipped(values), 2, axis=0)
        qt = flipped(q[i, :, here])
        found = []
        for h in range(2):
            if ticking:
                tick(h)
            toep = pltpu.roll(jnp.broadcast_to(u[2 * pair + h], (SPAN, 2 * SPAN)), 0, 1, stride=1, stride_axis=0)
            qcat[h * E : (h + 1) * E] = qt[h * E : (h + 1) * E]
            qcat[(1 - h) * E : (2 - h) * E] = jnp.zeros((E, R), BF)
            qcat[W:] = dot(toep[:, :SPAN].astype(BF), ohq[i]).astype(BF)
            top = jnp.full((8, R), -jnp.inf, F32)
            for c in range(0, m, ch):
                s = dot(kcat[base + c : base + c + ch], qcat[...])
                s_ref[c : c + ch] = s
                top = jnp.maximum(top, jnp.max(s.reshape(ch // 8, 8, R), axis=0))
            top = jnp.max(top, axis=0, keepdims=True)
            for c in range(0, m, ch):
                into[h, c : c + ch] = jnp.exp(s_ref[c : c + ch] - top).astype(BF)
            full = dot(vt[h, :, :m], into[h, :m])
            found.append((top, full[E : E + 1], full[:E]))
        return found

    def heads(parts):
        return jnp.transpose(jnp.concatenate(parts, axis=0)).astype(BF)

    @pl.when(step < pairs)
    def _():
        found = attend_to(0, 0, R, kf[:R, here], vf[:R, here], pa.at[0], True)
        for h, (top, total, full) in enumerate(found):
            stats[pair, 2 * h : 2 * h + 1] = top
            stats[pair, 2 * h + 1 : 2 * h + 2] = total
            held[pair, h * E : (h + 1) * E] = full

    @pl.when(step >= pairs)
    def _():
        m = L - R
        found = attend_to(0, R, m, kf[R:, here], vf[R:, here], pb.at[0, :, pl.ds(0, m)], True)
        parts = []
        for h, (top, total, full) in enumerate(found):
            first, first_total = stats[pair, 2 * h : 2 * h + 1], stats[pair, 2 * h + 1 : 2 * h + 2]
            most = jnp.maximum(first, top)
            a, b = jnp.exp(first - most), jnp.exp(top - most)
            back = 1.0 / (a * first_total + b * total)
            cs[0, 0, h : h + 1] = a * back
            cs[1, 0, h : h + 1] = b * back
            parts.append(held[pair, h * E : (h + 1) * E] * (a * back) + full * (b * back))
        o[0] = heads(parts)
        found = attend_to(1, L, S, ks[:, here], vs[:, here], pb.at[0, :, pl.ds(m, S)], False)
        for h, (top, total, full) in enumerate(found):
            cs[2, 0, h : h + 1] = 1.0 / total
        o[1] = heads([full / total for _, total, full in found])

    tick(2)

    @pl.when(step == steps - 1)
    def _():
        for copy in weights_out + kept_out:
            copy.wait()


def pieces_of(width):
    return [pl.ds(i * width // FORWARD_PIECES, width // FORWARD_PIECES) for i in range(FORWARD_PIECES)]


def forward_call(flag, tokens, layout, table, basis, shards, S):
    n, R, D = tokens.shape
    L = layout.shape[1]
    pairs = table.shape[1] // 2
    E = D // (2 * pairs)
    W = 2 * E
    KT = L + S
    whole = lambda shape: pl.BlockSpec(shape, lambda j: (0,) * len(shape))
    anywhere = pl.BlockSpec(memory_space=pl.ANY)
    vmem = lambda *s: pltpu.VMEM(s, BF)
    wide = lambda *s: pltpu.VMEM(s, F32)
    early = lambda j: jnp.minimum(j, pairs - 1)
    late = lambda j: jnp.maximum(j - pairs, 0)
    kept = [(n, R, D), (L, D), (L, D), (S, D), (S, D), (D, KT), (D, R)]
    chains = 5 + 2 * FORWARD_PIECES
    copies = GATHER_COPIES * chains + 1 + len(FORWARD_TOKENS)
    gathered = [(4, 2, 2, 2) + s.shape for s in shards]
    filled = gathered[1:]
    blocked = [
        ((n, R, D), BF, pl.BlockSpec((n, R, W), lambda j: (0, 0, late(j)))),
        ((pairs, 2, R, R), BF, pl.BlockSpec((1, 2, R, R), lambda j: (early(j), 0, 0, 0))),
        ((pairs, 2, KT - R, R), BF, pl.BlockSpec((1, 2, KT - R, R), lambda j: (late(j), 0, 0, 0))),
        ((3, pairs, 2, R), F32, pl.BlockSpec((3, 1, 2, R), lambda j: (0, late(j), 0, 0))),
        ((8, D), F32, whole((8, D))),
    ]
    return pl.pallas_call(
        functools.partial(forward_kernel, R, L, S, E, pairs),
        grid=(2 * pairs,),
        in_specs=[pl.BlockSpec(memory_space=pltpu.SMEM)]
        + [whole(a.shape) for a in (tokens, layout, table, basis)]
        + [anywhere] * 7,
        out_specs=[b[2] for b in blocked] + [anywhere] * (len(kept) + len(filled)),
        out_shape=[jax.ShapeDtypeStruct(*b[:2]) for b in blocked] + [jax.ShapeDtypeStruct(s, BF) for s in kept + filled],
        scratch_shapes=[vmem(KT, W + SPAN), vmem(W + SPAN, R), vmem(2, E + 16, R), wide(R, R), vmem(n, SPAN, R)]
        + [vmem(R, D), vmem(S, D), vmem(2, D, D), vmem(n, R, D), vmem(n, R, D), wide(pairs, W, R), wide(pairs, 8, R), wide(2 * pairs, 1, 2 * SPAN)]
        + [vmem(*s) for s in kept]
        + [vmem(*s) for s in gathered[:4]]
        + [pltpu.SemaphoreType.DMA((copies,))] * 2
        + [pltpu.SemaphoreType.DMA((chains + 10,))],
        compiler_params=pltpu.CompilerParams(
            vmem_limit_bytes=60 * 2**20, dimension_semantics=("arbitrary",), collective_id=0, has_side_effects=True
        ),
        name="forward",
    )(flag, tokens, layout, table, basis, *shards)


class Sum:
    COPIES = 7

    def __init__(self, at, part, total, scratch, sems, local, base, cols=None, plane=None):
        self.at, self.part, self.total, self.sems, self.base, self.plane = at, part, total, sems, base, plane
        self.cols = pl.ds(0, total.shape[1]) if cols is None else cols
        self.acc, self.got_diag, self.got_one, self.got_two, self.got_z = scratch[:5]
        self.held = scratch[5] if len(scratch) > 5 else None
        if self.held is not None:
            self.keep = pltpu.make_async_copy(part.at[:, :, at.c, :, :, self.cols], self.held, local)
        self.stages = [self.one, self.two, self.three, self.four, self.five]

    @staticmethod
    def scratch(depth, rows, columns, held):
        slab = (rows, columns)
        shapes = [(depth, 2, 2) + slab] + [(depth,) + slab] * 3 + [(3,) + slab] + [(depth, 2, 2) + slab] * held
        return [pltpu.VMEM(s, BF) for s in shapes]

    def send(self, k):
        at, acc = self.at, self.acc
        if k > 3:
            d = k - 3
            src, dst, device = acc.at[(at.z + d) % 4, at.y, at.x], self.got_z.at[d - 1], at.along_z(d)
        else:
            src, dst, device = [
                (self.part.at[:, :, 1 - at.c, :, :, self.cols], acc, at.core()),
                (acc.at[:, 1 - at.y, 1 - at.x], self.got_diag, at.second()),
                (acc.at[:, at.y2, at.x2], self.got_two, at.second()),
                (acc.at[:, at.y1, at.x1], self.got_one, at.first()),
            ][k]
        return remote(src, dst, self.sems, self.base + k, device)

    def to_plane(self):
        at = self.at
        d = (self.plane - at.z + 4) % 4
        k = self.base + 3 + d
        return pltpu.make_async_remote_copy(
            src_ref=self.acc.at[0, at.y, at.x],
            dst_ref=self.got_z.at[d - 1],
            send_sem=self.sems[0].at[k],
            recv_sem=self.sems[1].at[k],
            device_id=at.device(self.plane, at.y, at.c, at.x),
            device_id_type=MESH,
        )

    def one(self):
        self.send(0).start()
        if self.held is not None:
            self.keep.start()

    def two(self):
        at, acc = self.at, self.acc
        if self.held is not None:
            self.keep.wait()
        self.send(0).wait_recv()

        def add(i, _):
            for yy in range(2):
                own = self.held[i, yy] if self.held is not None else self.part[i, yy, at.c, :, :, self.cols]
                acc[i, yy] = (acc[i, yy].astype(F32) + own.astype(F32)).astype(BF)
            return 0

        lax.fori_loop(0, acc.shape[0], add, 0)
        self.send(1).start()
        self.send(2).start()

    def three(self):
        at, acc = self.at, self.acc
        self.send(1).wait_recv()
        acc[:, at.y1, at.x1] = (acc[:, at.y1, at.x1].astype(F32) + self.got_diag[...].astype(F32)).astype(BF)
        self.send(3).start()

    def four(self):
        at, acc = self.at, self.acc
        self.send(2).wait_recv()
        self.send(3).wait_recv()
        mine = acc[:, at.y, at.x].astype(F32) + self.got_one[...].astype(F32) + self.got_two[...].astype(F32)
        acc[:, at.y, at.x] = mine.astype(BF)
        if self.plane is None:
            for k in (4, 5, 6):
                self.send(k).start()
        else:

            @pl.when(at.z != self.plane)
            def _():
                self.to_plane().start()

    def five(self):
        at = self.at

        def collect():
            out = self.acc[at.z if self.plane is None else 0, at.y, at.x].astype(F32)
            for d in (1, 2, 3):
                arrival = remote(self.got_z.at[d - 1], self.got_z.at[d - 1], self.sems, self.base + 3 + d, at.along_z(d))
                arrival.wait_recv()
                out = out + self.got_z[d - 1].astype(F32)
            self.total[:, self.cols] = out

        for k in range(4):
            self.send(k).wait_send()
        if self.plane is None:
            collect()
            for k in (4, 5, 6):
                self.send(k).wait_send()
        else:
            pl.when(at.z == self.plane)(collect)

            @pl.when(at.z != self.plane)
            def _():
                self.to_plane().wait_send()


def into_slabs(flat, slabs):
    rows = slabs.shape[4]
    for i in range(32):
        slabs[i // 8, i // 4 % 2, i // 2 % 2, i % 2] = flat[rows * i : rows * (i + 1)].astype(BF)


def backward_kernel(R, L, S, E, pairs, planes, *refs):
    flag, q, kf, vf, ks, vs, o, do, pa, pb, cs, layout = refs[:12]
    refs = list(refs[12:])
    take = lambda k: [refs.pop(0) for _ in range(k)]
    parts = take(len(planes))
    nkt_, nst_, wq, wk, wv, tok, dres, grow, dg2 = take(9)
    gtok, small_total = take(2)
    totals = take(3 + len(planes))
    kq, vaug, rhs, ds, ohq, nacc, qm, dm, held = take(9)
    dq, dk, dv, nkt, nst, ws, toks, dress = take(8)
    far, fars, gfar, gshort, ends = take(5)
    tsum, small, small_held, small_got = take(4)
    send, recv, local = take(3)
    W = 2 * E
    D = ws.shape[1]
    at = Place()
    sems = (send, recv)
    sums = []

    def summed(part, total, held, plane=None):
        i = len(sums)
        sums.append(Sum(at, part, total, take(5 + held), sems, local.at[i], Sum.COPIES * i, None, plane))

    for part, total, plane in zip(parts, totals, planes):
        summed(part, total, 1, plane)
    early = len(sums)
    mats = take(3)
    for part, total in zip(mats, totals[early:]):
        summed(part, total, 0)
    base = Sum.COPIES * len(sums)
    small_chain = small_stages(at, small, small_total, small_held, small_got, sems, base)
    long = remote(far, gfar, sems, base + 6, at.along_x())
    short = remote(fars, gshort, sems, base + 7, at.along_x())
    loads = [(w, ws.at[i]) for i, w in enumerate((wq, wk, wv))] + [(nkt_, nkt), (nst_, nst), (tok, toks), (dres, dress)]
    loads = [pltpu.make_async_copy(a, b, local.at[len(sums) + i]) for i, (a, b) in enumerate(loads)]

    step = pl.program_id(0)
    pair = lax.rem(step, pairs)
    steps = 2 * pairs
    plan = {}
    for i in range(early):
        for s in range(5):
            when = 0 if s == 0 else int(BACK_SUM[0] + BACK_SUM[1] * i + BACK_SUM[2] * (s - 1))
            plan.setdefault(when, []).insert(0, sums[i].stages[s])

    def tick(spot):
        for t in plan:
            if t < 2 * steps and t % 2 == spot:

                @pl.when(step == t // 2)
                def _(t=t):
                    for stage in plan[t]:
                        stage()

    @pl.when(step == 0)
    def _():
        at.greet()
        for load in loads:
            load.start()
        long_keys, short_keys, *queries = coordinates(at, flag, layout, R, S)
        for i, (base, row) in enumerate([(0, long_keys), (L, short_keys)]):
            kq[:SPAN, base : base + row.shape[1]] = eye_of(row, SPAN, True)
            ohq[i] = jnp.transpose(eye_of(queries[i], SPAN, False).astype(F32)).astype(BF)
        vaug[:, W:] = (lax.broadcasted_iota(jnp.int32, (R, W), 1) < 2).astype(F32).astype(BF)
        rhs[...] = jnp.zeros_like(rhs)

    @pl.when(step == pairs)
    def _():
        for load in loads[:3]:
            load.wait()
        far[...] = (dot_nt(dk[R:L], ws[1]) + dot_nt(dv[R:L], ws[2])).astype(BF)
        long.start()
        ends[...] = dot_nt(dk[L:], ws[1]) + dot_nt(dv[L:], ws[2])
        fars[...] = ends[...].astype(BF)
        pl.when(at.x == 1)(short.start)

    nacc[...] = jnp.zeros_like(nacc)
    lane = lax.broadcasted_iota(jnp.int32, (R, W), 1)
    spot = lax.broadcasted_iota(jnp.int32, (16, R), 0)
    here = pl.ds(pl.multiple_of(pair * W, W), W)

    def attend_to(i, base, m, keys, values, p, scale, ticking):
        ch = min(CH, m)
        vaug[:m, :W] = values
        kt = flipped(keys)
        dot_, ot = jnp.transpose(do[i].astype(F32)), jnp.transpose(o[i].astype(F32))
        scaled = [(dot_[h * E : (h + 1) * E] * cs[scale, 0, h : h + 1]).astype(BF) for h in range(2)]
        don = flipped(jnp.concatenate(scaled, axis=0))
        qq = q[i]
        zero = jnp.zeros((R, W), BF)
        for h in range(2):
            mine = (lane < E) if h == 0 else (lane >= E)
            qm[h * R : (h + 1) * R] = jnp.where(mine, qq, zero)
            dm[h * R : (h + 1) * R] = jnp.where(mine, don, zero)
        dqs = []
        for h in range(2):
            if ticking:
                tick(h)
            rhs[h * E : (h + 1) * E] = scaled[h]
            rhs[(1 - h) * E : (2 - h) * E] = jnp.zeros((E, R), BF)
            delta = jnp.sum(scaled[h].astype(F32) * ot[h * E : (h + 1) * E], axis=0, keepdims=True)
            hi = delta.astype(BF).astype(F32)
            rhs[W : W + 16] = jnp.where(spot == 0, -hi, jnp.where(spot == 1, hi - delta, 0.0)).astype(BF)
            for c in range(0, m, ch):
                g = dot(vaug[c : c + ch], rhs[...])
                ds[c : c + ch, h * R : (h + 1) * R] = (p[h, c : c + ch].astype(F32) * g).astype(BF)
            kq[SPAN:, base : base + m] = kt[h * E : (h + 1) * E]
            both = dot(kq[:, base : base + m], ds[:m, h * R : (h + 1) * R])
            dqs.append(both[SPAN:] * 0.125)
            nacc[h] += dot(both[:SPAN].astype(BF), ohq[i])
        for c in range(0, m, ch):
            dk[base + c : base + c + ch, here] = dot(ds[c : c + ch], qm[...]).astype(BF)
            both = dot(p[0, c : c + ch], dm[:R]) + dot(p[1, c : c + ch], dm[R:])
            dv[base + c : base + c + ch, here] = both.astype(BF)
        return jnp.concatenate(dqs, axis=0)

    def diagonals(h):
        wide = jnp.concatenate([nacc[h], jnp.zeros((SPAN, SPAN), F32)], axis=1)
        return jnp.sum(pltpu.roll(wide, 0, 1, stride=1, stride_axis=0), axis=0, keepdims=True)

    @pl.when(step < pairs)
    def _():
        m = L - R
        held[pair] = attend_to(0, R, m, kf[R:], vf[R:], pb.at[0, :, pl.ds(0, m)], 1, True)
        dq[1, :, here] = flipped(attend_to(1, L, S, ks[...], vs[...], pb.at[0, :, pl.ds(m, S)], 2, False))
        for h in range(2):
            tsum[2 * pair + h] = diagonals(h)

    @pl.when(step >= pairs)
    def _():
        dq[0, :, here] = flipped(held[pair] + attend_to(0, 0, R, kf[:R], vf[:R], pa.at[0], 0, True))
        for h in range(2):
            tsum[2 * pair + h] = tsum[2 * pair + h] + diagonals(h)

    @pl.when(step == steps - 1)
    def _():
        rest = [stage for t in sorted(plan) if t >= 2 * steps for stage in plan[t]]

        def some(count):
            for _ in range(min(count, len(rest))):
                rest.pop(0)()

        for load in loads[3:]:
            load.wait()
        later = sums[early:]
        into_slabs(dot(nkt[...], dv[...]), mats[2])
        later[2].one()
        some(2)
        into_slabs(dot(nkt[...], dk[...]), mats[1])
        later[1].one()
        some(2)
        into_slabs(dot(nkt[:, :R], dq[0]) + dot(nst[...], dq[1]), mats[0])
        later[0].one()
        some(100)
        later[2].two()
        toks[0], toks[1] = swapped(flag, toks[0], toks[1])
        own = [dot_nt(dq[0], ws[0]) + dot_nt(dk[:R], ws[1]) + dot_nt(dv[:R], ws[2]), dot_nt(dq[1], ws[0])]
        later[1].two()
        later[2].three()
        long.wait()
        pl.when(at.x == 1)(short.wait_send)
        pl.when(at.x == 0)(short.wait_recv)
        gain = grow[0:1]
        keys = jnp.where(at.x == 0, ends[...] + gshort[...].astype(F32), 0.0)
        total = jnp.zeros((1, D), F32)
        for i in range(2):
            d = own[i] + (gfar[...].astype(F32) if i == 0 else jnp.concatenate([keys, jnp.zeros((R - S, D), F32)], axis=0))
            x = toks[i].astype(F32)
            back = norm_rows(x)
            a = gain * d
            total = total + jnp.sum(d * x * back, axis=0, keepdims=True)
            part = back * a - x * (back * back * back) * jnp.mean(a * x, axis=1, keepdims=True)
            toks[i] = (dress[i * R : (i + 1) * R] + part).astype(BF)
        toks[0], toks[1] = swapped(flag, toks[0], toks[1])
        finish = pltpu.make_async_copy(toks, gtok, local.at[len(sums) + len(loads)])
        finish.start()
        small[...] = jnp.zeros_like(small)
        lines = D // 128
        for i in range(lines):
            small[i : i + 1] = total[:, 128 * i : 128 * (i + 1)]
            small[lines + i : lines + i + 1] = dg2[:, 128 * i : 128 * (i + 1)]
        for h in range(2 * pairs):
            for i in range(4):
                spots = 2 * lines + 4 * h + i
                small[spots : spots + 1] = tsum[h, :, 128 * i : 128 * (i + 1)]
        small_chain[0]()
        later[0].two()
        later[1].three()
        small_chain[1]()
        later[2].four()
        later[0].three()
        small_chain[2]()
        later[1].four()
        small_chain[3]()
        later[0].four()
        for s in later[::-1]:
            s.five()
        small_chain[4]()
        finish.wait()


def backward_call(flag, q, kf, vf, ks, vs, o, do, pa, pb, cs, layout, parts, planes, nkt, nst, wq, wk, wv, tok, dres, grow, dg2):
    n, R, D = q.shape
    L, S = kf.shape[0], ks.shape[0]
    pairs = pa.shape[0]
    E = D // (2 * pairs)
    W = 2 * E
    KT = L + S
    whole = lambda a: pl.BlockSpec(a.shape, lambda j: (0,) * len(a.shape))
    anywhere = pl.BlockSpec(memory_space=pl.ANY)
    early = lambda j: jnp.minimum(j, pairs - 1)
    late = lambda j: jnp.maximum(j - pairs, 0)
    rows = pl.BlockSpec((n, R, W), lambda j: (0, 0, lax.rem(j, pairs)))
    keys = lambda a: pl.BlockSpec((a.shape[0], W), lambda j: (0, lax.rem(j, pairs)))
    shares = [p_.shape[4:] for p_ in parts] + [(D // 32, D)] * 3
    lines = -(-(2 * D // 128 + 8 * pairs) // 8) * 8
    outs = [jax.ShapeDtypeStruct((n, R, D), BF), jax.ShapeDtypeStruct((lines, 128), F32)]
    outs += [jax.ShapeDtypeStruct(s, F32) for s in shares]
    vmem = lambda *s: pltpu.VMEM(s, BF)
    wide = lambda *s: pltpu.VMEM(s, F32)
    scratch = [vmem(SPAN + E, KT), vmem(R, 2 * W), vmem(2 * W, R), vmem(R, 2 * R), vmem(n, R, SPAN)]
    scratch += [wide(2, SPAN, SPAN), vmem(2 * R, W), vmem(2 * R, W), wide(pairs, W, R)]
    scratch += [vmem(n, R, D), vmem(KT, D), vmem(KT, D), vmem(D, KT), vmem(D, R)]
    scratch += [vmem(3, D, D), vmem(n, R, D), wide(n * R, D)]
    scratch += [vmem(R, D), vmem(S, D), vmem(R, D), vmem(S, D), wide(S, D)]
    scratch += [wide(2 * pairs, 1, 2 * SPAN), wide(lines, 128), wide(4, lines, 128), wide(6, lines, 128)]
    chunks = [(p_.shape[0],) + p_.shape[4:] for p_ in parts]
    copies = Sum.COPIES * (len(chunks) + 3) + 8
    scratch += [pltpu.SemaphoreType.DMA((copies,)), pltpu.SemaphoreType.DMA((copies,)), pltpu.SemaphoreType.DMA((len(chunks) + 12,))]
    scratch += sum([Sum.scratch(*s, 1) for s in chunks], [])
    scratch += [vmem(4, 2, 2, 2, D // 32, D)] * 3
    scratch += sum([Sum.scratch(4, *s, 0) for s in shares[len(parts):]], [])
    return pl.pallas_call(
        functools.partial(backward_kernel, R, L, S, E, pairs, planes),
        grid=(2 * pairs,),
        in_specs=[pl.BlockSpec(memory_space=pltpu.SMEM), rows, keys(kf), keys(vf), keys(ks), keys(vs), rows, rows]
        + [pl.BlockSpec((1, 2, R, R), lambda j: (late(j), 0, 0, 0)), pl.BlockSpec((1, 2, KT - R, R), lambda j: (early(j), 0, 0, 0))]
        + [pl.BlockSpec((3, 1, 2, R), lambda j: (0, lax.rem(j, pairs), 0, 0)), whole(layout)]
        + [anywhere] * (len(parts) + 7)
        + [whole(grow), whole(dg2)],
        out_specs=[anywhere] + [whole(s) for s in outs[1:]],
        out_shape=outs,
        scratch_shapes=scratch,
        compiler_params=pltpu.CompilerParams(
            vmem_limit_bytes=60 * 2**20, dimension_semantics=("arbitrary",), collective_id=1, has_side_effects=True
        ),
        name="backward",
    )(flag, q, kf, vf, ks, vs, o, do, pa, pb, cs, layout, *parts, nkt, nst, wq, wk, wv, tok, dres, grow, dg2)


EPSILON = 1e-06
THRESHOLDS = (12, 16, 23, 32, 46, 64, 91)
BOTH = ("dp", "blk")


def bucket_np(relative):
    magnitude = np.abs(relative)
    larger = 8 + sum((magnitude >= limit).astype(np.int64) for limit in THRESHOLDS)
    return np.where(magnitude < 8, magnitude, larger) + 16 * (relative > 0)


def bucket_rows(distance, buckets):
    return (bucket_np(distance)[:, None] == np.arange(buckets)[None, :]).astype(np.float32)


def norm_parts(x, gain):
    back = lax.rsqrt(jnp.mean(x * x, axis=-1, keepdims=True) + EPSILON)
    return (x * back * gain).astype(BF), back


def norm_back(d, x, back, gain):
    a = gain * d
    grad_gain = jnp.sum(d * x * back, axis=0)
    return back * a - x * back**3 * jnp.mean(a * x, axis=-1, keepdims=True), grad_gain


def mm(a, b, dims):
    return lax.dot_general(a, b, (dims, ((), ())), preferred_element_type=F32)


def gather_weights(gain_one, wq, wk, wv, wo, gain_two, wi, wt):
    full = lambda a: lax.all_gather(a, BOTH, axis=0, tiled=True)
    packed = full(jnp.concatenate([wq, wk, wv, wo, wi], axis=1))
    width = wq.shape[1]
    gains = full(jnp.stack([gain_one, gain_two], axis=1))
    return packed[:, : 3 * width], packed[:, 3 * width : 4 * width], packed[:, 4 * width :], full(wt), gains[:, 0], gains[:, 1]


def scatter_sums(dqkv, dwo, dwi, dwt, dg1, dg2):
    take = lambda a: lax.psum_scatter(a, BOTH, scatter_dimension=0, tiled=True)
    width = dwo.shape[1]
    packed = take(jnp.concatenate([dqkv, dwo, dwi], axis=1).astype(BF)).astype(F32)
    gains = take(jnp.stack([dg1, dg2], axis=1))
    parts = [packed[:, i * width : (i + 1) * width] for i in range(4)]
    return parts, packed[:, 4 * width :], take(dwt.astype(BF)).astype(F32), gains[:, 0], gains[:, 1]


def on_any_device(tokens, layout, lengths, gain_one, wq, wk, wv, wo, gain_two, wi, wt, table, grad_out):
    n, R, D = tokens.shape
    H = table.shape[1]
    G = lax.axis_size("blk")
    me = lax.axis_index("blk")
    L = layout.shape[1]
    S = L // 8
    order = jnp.argsort(-lengths, stable=True)
    place = jnp.argsort(order)
    tok = tokens[order]
    gout = grad_out[order]
    lay = layout[order]
    lens = lengths[order]

    def from_step(x, s):
        return lax.ppermute(x, "blk", [(i, (i - s) % G) for i in range(G)])

    pieces = [tok[:-1]] + [from_step(tok[:-1], s) for s in range(1, G)]
    xf = jnp.concatenate(pieces, axis=1)
    first = tok[-1, :S]
    xs = jnp.where(me == 0, first, sum(lax.ppermute(first, "blk", [(0, i)]) for i in range(1, G)))
    lay_turned = jnp.roll(lay, -me * R, axis=1)
    layq = lay_turned[:, None, :R]
    layf = lay_turned[:-1, None, :]
    lays = lay[-1:, :S]
    spots = (jnp.arange(L) + me * R) % L
    mask = jnp.where(spots[None, :, None] < lens[:-1, None, None], 0.0, -1e30).astype(F32)

    wqkv, wo_all, wi_all, wt_all, g1, g2 = gather_weights(gain_one, wq, wk, wv, wo, gain_two, wi, wt)
    g1 = g1.astype(F32)
    g2 = g2.astype(F32)
    hidden = tok.reshape(n * R, D).astype(F32)
    normed, r1 = norm_parts(hidden, g1)
    xkeys = jnp.concatenate([xf.reshape((n - 1) * L, D), xs], axis=0)
    nkeys, _ = norm_parts(xkeys.astype(F32), g1)
    q = (mm(normed, wqkv[:, :D], ((1,), (0,))).astype(BF) * jnp.asarray(0.125, BF)).reshape(n, R, D)
    k = mm(nkeys, wqkv[:, D : 2 * D], ((1,), (0,))).astype(BF)
    v = mm(nkeys, wqkv[:, 2 * D :], ((1,), (0,))).astype(BF)
    cut = (n - 1) * L
    kf, ks = k[:cut].reshape(n - 1, L, D), k[cut:]
    vf, vs = v[:cut].reshape(n - 1, L, D), v[cut:]
    lane = np.arange(2 * SPAN)
    turned = np.where(lane >= SPAN, lane - 2 * SPAN, lane)
    urow = mm(table, bucket_rows(-turned, table.shape[0]).astype(BF), ((0,), (1,))).reshape(H // 2, 2, 2 * SPAN)
    o, p, l = attend_call(q, kf, vf, ks, vs, layq, layf, lays, mask, urow)

    attended = o.reshape(n * R, D)
    resid = hidden + mm(attended, wo_all, ((1,), (0,)))
    normed_two, r2 = norm_parts(resid, g2)
    pre = mm(normed_two, wi_all, ((1,), (0,)))
    act, act_back = jax.vjp(lambda x: jax.nn.gelu(x, approximate=False), pre)
    act = act.astype(BF)
    mixed = (resid + mm(act, wt_all, ((1,), (0,)))).astype(BF)
    up = gout.reshape(n * R, D)
    dwt = mm(act, up, ((0,), (0,)))
    (dpre,) = act_back(mm(up, wt_all, ((1,), (1,))))
    dpre = dpre.astype(BF)
    dwi = mm(normed_two, dpre, ((0,), (0,)))
    dn2 = mm(dpre, wi_all, ((1,), (1,)))
    dresid, dg2 = norm_back(dn2, resid, r2, g2)
    dresid = dresid + up.astype(F32)
    low = dresid.astype(BF)
    dwo = mm(attended, low, ((0,), (0,)))
    datt = mm(low, wo_all, ((1,), (1,))).astype(BF).reshape(n, R, D)

    dq, dkf, dvf, dks, dvs, t = attend_back_call(q, kf, vf, ks, vs, layq, layf, lays, o, datt, p, l)
    dtable = jnp.einsum(
        "hj,jb->bh", t.reshape(H, 2 * SPAN), bucket_rows(SPAN - 1 - lane, table.shape[0]), precision=lax.Precision.HIGHEST
    )
    dq = dq.reshape(n * R, D)
    dk = jnp.concatenate([dkf.reshape(cut, D), dks], axis=0)
    dv = jnp.concatenate([dvf.reshape(cut, D), dvs], axis=0)
    dnk = mm(dk, wqkv[:, D : 2 * D], ((1,), (1,))) + mm(dv, wqkv[:, 2 * D :], ((1,), (1,)))
    dnf = dnk[:cut].reshape(n - 1, L, D)
    dns = dnk[cut:].astype(BF)
    far = sum(
        lax.ppermute(dnf[:, s * R : (s + 1) * R].astype(BF), "blk", [(i, (i + s) % G) for i in range(G)]).astype(F32)
        for s in range(1, G)
    )
    near = jnp.where(
        me == 0, dnk[cut:] + sum(lax.ppermute(dns, "blk", [(i, 0)]).astype(F32) for i in range(1, G)), 0.0
    )
    extra = jnp.concatenate([dnf[:, :R] + far, jnp.pad(near, ((0, R - S), (0, 0)))[None]], axis=0).reshape(n * R, D)
    dn1 = mm(dq, wqkv[:, :D], ((1,), (1,))) + extra
    dwq = mm(normed, dq, ((0,), (0,)))
    dwk = mm(nkeys, dk, ((0,), (0,)))
    dwv = mm(nkeys, dv, ((0,), (0,)))
    dx, dg1 = norm_back(dn1, hidden, r1, g1)
    gtok = (dresid + dx).astype(BF)
    parts, gwi, gwt, gg1, gg2 = scatter_sums(jnp.concatenate([dwq, dwk, dwv], axis=1), dwo, dwi, dwt, dg1, dg2)
    dtable = lax.psum(dtable, BOTH)
    return (
        mixed.reshape(n, R, D)[place],
        gtok.reshape(n, R, D)[place],
        gg1,
        parts[0],
        parts[1],
        parts[2],
        parts[3],
        gg2,
        gwi,
        gwt,
        dtable,
    )


def on_device(tokens, layout, lengths, gain_one, wq, wk, wv, wo, gain_two, wi, wt, table, grad_out):
    n, R, D = tokens.shape
    H = table.shape[1]
    G = lax.axis_size("blk")
    me = lax.axis_index("blk")
    L = layout.shape[1]
    S = L // 8
    lane = np.arange(2 * SPAN)
    turned = np.where(lane >= SPAN, lane - 2 * SPAN, lane)
    basis = jnp.asarray(bucket_rows(-turned, table.shape[0]).T, BF)
    column = jnp.arange(128)[None, :]
    gains = jnp.where(column == 0, gain_one[:, None], jnp.where(column == 1, gain_two[:, None], 0)).astype(BF)
    o, pa, pb, cs, grow, q, kf, vf, ks, vs, nkt, nst, *wholes = forward_call(
        lengths, tokens, layout, table.astype(F32), basis, [gains, wq, wk, wv, wo, wi, wt], S
    )
    flat = lambda a: a.reshape(-1, a.shape[-1])
    wq_all, wk_all, wv_all, wo_all, wi_all, wt_all = [flat(a) for a in wholes]
    rows = lambda a: a.reshape(n * R, D)
    mixed, dresid, datt, dwo, *handed = feed_forward_call(
        lengths, rows(o), rows(tokens), rows(grad_out), wo_all, grow, wi_all, wt_all
    )
    count = 2 * (4 - FF_SUMS)
    dg2, done = handed[count], handed[count + 1 :]
    planes = sum([(None, j) for j in range(FF_SUMS, 4)], ()) + (None,)
    gtok, small, *sums = backward_call(
        lengths, q, kf, vf, ks, vs, o, datt.reshape(n, R, D), pa, pb, cs, layout,
        handed[:count] + [dwo.reshape(4, 2, 2, 2, -1, D)], planes,
        nkt, nst, wq_all, wk_all, wv_all, tokens, dresid, grow, dg2,
    )
    gwo, gwq, gwk, gwv = sums[count:]
    gwi = jnp.concatenate(done[:FF_SUMS] + sums[0:count:2], axis=1)
    gwt = done[FF_SUMS]
    for j in range(FF_SUMS, 4):
        gwt = jnp.where(lax.axis_index("dp") // 4 == j, sums[2 * (j - FF_SUMS) + 1], gwt)
    small = small.reshape(-1)
    mine = (lax.axis_index("dp") * G + me) * (D // 32)
    gg1, gg2 = [lax.dynamic_slice_in_dim(small, mine + i * D, D // 32) for i in range(2)]
    t = small[2 * D : 2 * D + H * 2 * SPAN].reshape(H, 2 * SPAN)
    dtable = jnp.einsum(
        "hj,jb->bh", t, bucket_rows(SPAN - 1 - lane, table.shape[0]), precision=lax.Precision.HIGHEST
    )
    return mixed.reshape(n, R, D), gtok, gg1, gwq, gwk, gwv, gwo, gg2, gwi, gwt, dtable


def solution(mesh):
    rows = P(BOTH, None)
    items = P("dp", "blk", None)
    known = dict(mesh.shape) == {"dp": 16, "blk": 2}

    def body(tokens, *rest):
        return (on_device if known and tokens.shape[0] == 2 else on_any_device)(tokens, *rest)

    return jax.shard_map(
        body,
        mesh=mesh,
        in_specs=(items, P("dp", None), P("dp"), P(BOTH), rows, rows, rows, rows, P(BOTH), rows, rows, P(), items),
        out_specs=(items, items, P(BOTH), rows, rows, rows, rows, P(BOTH), rows, rows, P()),
        check_vma=False,
    )
```

```python
import functools
import math

import jax
import jax.numpy as jnp
import numpy as np
from jax import lax
from jax.experimental import pallas as pl
from jax.experimental.pallas import tpu as pltpu
from jax.sharding import PartitionSpec as P

F32=jnp.float32; BF=jnp.bfloat16
SPAN=256
CH=256
def dot(a,b): return lax.dot_general(a,b,(((1,),(0,)),((),())),preferred_element_type=F32)
def eye_of(row, width, reverse):
    spots=lax.broadcasted_iota(jnp.int32,(width,row.shape[1]),0)
    if reverse: spots=width-1-spots
    return (spots==row).astype(F32).astype(BF)

def attend(n,L,S,R,E, q,kf,vf,ks,vs,layq,layf,lays,mask,u,o,p,l, kcat,qcat,vt,s_ref,ohq):
    W=2*E
    spans=[L]*(n-1)+[S]
    @pl.when(pl.program_id(0)==0)
    def _():
        base=0
        for i,m in enumerate(spans):
            row=layf[i] if i<n-1 else lays[...]
            kcat[base:base+m,W:]=jnp.transpose(eye_of(row,SPAN,False).astype(F32)).astype(BF)
            ohq[i]=eye_of(layq[i],SPAN,False)
            base+=m
        vt[:,E:]=jnp.ones((2,vt.shape[1]-E,vt.shape[2]),BF)
    pair=pl.program_id(0)
    base=0
    for i,m in enumerate(spans):
        ch=min(CH,m)
        kcat[base:base+m,:W]=kf[i] if i<n-1 else ks[...]
        v=vf[i] if i<n-1 else vs[...]
        vtr=jnp.transpose(v.astype(F32)).astype(BF)
        vt[0,:E,:m]=vtr[:E]
        vt[1,:E,:m]=vtr[E:]
        qt=jnp.transpose(q[i].astype(F32)).astype(BF)
        outs=[]
        for h in range(2):
            urow=u[pl.ds(0,1),h,:] if False else u[0,h:h+1,:]
            toep=pltpu.roll(jnp.broadcast_to(urow,(SPAN,2*SPAN)),0,1,stride=1,stride_axis=0)[:,:SPAN].astype(BF)
            qcat[h*E:(h+1)*E]=qt[h*E:(h+1)*E]
            qcat[(1-h)*E:(2-h)*E]=jnp.zeros((E,R),BF)
            qcat[W:]=dot(toep,ohq[i]).astype(BF)
            m8=jnp.full((8,R),-jnp.inf,F32)
            for c in range(0,m,ch):
                s=dot(kcat[base+c:base+c+ch],qcat[...])
                if 0<i<n-1: s=s+mask[i,c:c+ch,:]
                s_ref[c:c+ch]=s
                m8=jnp.maximum(m8,jnp.max(s.reshape(ch//8,8,R),axis=0))
            top=jnp.max(m8,axis=0,keepdims=True)
            for c in range(0,m,ch):
                p[0,h,base+c:base+c+ch]=jnp.exp(s_ref[c:c+ch]-top).astype(BF)
            full=dot(vt[h,:,:m],p[0,h,base:base+m])
            total=full[E:E+1]
            l[i,0,h:h+1]=total
            outs.append(full[:E]/total)
        o[i]=jnp.transpose(jnp.concatenate(outs,axis=0)).astype(BF)
        base+=m

def attend_call(q,kf,vf,ks,vs,layq,layf,lays,mask,u):
    n,R,D=q.shape; L=kf.shape[1]; S=ks.shape[0]; H=u.shape[0]*2; E=D//H; W=2*E
    KT=(n-1)*L+S
    full=lambda a: pl.BlockSpec(a.shape,lambda j:(0,)*a.ndim)
    return pl.pallas_call(functools.partial(attend,n,L,S,R,E),
      grid=(H//2,),
      in_specs=[pl.BlockSpec((n,R,W),lambda j:(0,0,j)),
        pl.BlockSpec((n-1,L,W),lambda j:(0,0,j)),pl.BlockSpec((n-1,L,W),lambda j:(0,0,j)),
        pl.BlockSpec((S,W),lambda j:(0,j)),pl.BlockSpec((S,W),lambda j:(0,j)),
        full(layq),full(layf),full(lays),full(mask),pl.BlockSpec((1,2,2*SPAN),lambda j:(j,0,0))],
      out_specs=[pl.BlockSpec((n,R,W),lambda j:(0,0,j)),
        pl.BlockSpec((1,2,KT,R),lambda j:(j,0,0,0)),
        pl.BlockSpec((n,1,2,R),lambda j:(0,j,0,0))],
      out_shape=[jax.ShapeDtypeStruct((n,R,D),BF),jax.ShapeDtypeStruct((H//2,2,KT,R),BF),jax.ShapeDtypeStruct((n,H//2,2,R),F32)],
      scratch_shapes=[pltpu.VMEM((KT,W+SPAN),BF),pltpu.VMEM((W+SPAN,R),BF),pltpu.VMEM((2,E+16,L),BF),pltpu.VMEM((L,R),F32),pltpu.VMEM((n,SPAN,R),BF)],
      compiler_params=pltpu.CompilerParams(vmem_limit_bytes=56*2**20,dimension_semantics=("arbitrary",)),
      name="attend",
    )(q,kf,vf,ks,vs,layq,layf,lays,mask,u)

def attend_back(n,L,S,R,E, q,kf,vf,ks,vs,layq,layf,lays,o,do,p,l, dq,dkf,dvf,dks,dvs,t, kq,vaug,rhs,ds,ohq,nacc,qm,dm):
    W=2*E
    spans=[L]*(n-1)+[S]
    @pl.when(pl.program_id(0)==0)
    def _():
        base=0
        for i,m in enumerate(spans):
            row=layf[i] if i<n-1 else lays[...]
            kq[:SPAN,base:base+m]=eye_of(row,SPAN,True)
            ohq[i]=jnp.transpose(eye_of(layq[i],SPAN,False).astype(F32)).astype(BF)
            base+=m
        vaug[:,W:]=(lax.broadcasted_iota(jnp.int32,(vaug.shape[0],W),1)<2).astype(F32).astype(BF)
        rhs[...]=jnp.zeros_like(rhs)
    nacc[...]=jnp.zeros_like(nacc)
    base=0
    lane=lax.broadcasted_iota(jnp.int32,(R,W),1)
    for i,m in enumerate(spans):
        ch=min(CH,m)
        kk=kf[i] if i<n-1 else ks[...]
        vaug[:m,:W]=vf[i] if i<n-1 else vs[...]
        kt=jnp.transpose(kk.astype(F32)).astype(BF)
        dot_=jnp.transpose(do[i].astype(F32))
        ot=jnp.transpose(o[i].astype(F32))
        scaled=[];
        for h in range(2):
            inv=1.0/l[i,0,h:h+1]
            scaled.append((dot_[h*E:(h+1)*E]*inv).astype(BF))
        sc=jnp.concatenate(scaled,axis=0)
        don=jnp.transpose(sc.astype(F32)).astype(BF)
        qq=q[i]
        zero=jnp.zeros((R,W),BF)
        for h in range(2):
            mine=(lane<E) if h==0 else (lane>=E)
            qm[h*R:(h+1)*R]=jnp.where(mine,qq,zero)
            dm[h*R:(h+1)*R]=jnp.where(mine,don,zero)
        dqs=[]
        for h in range(2):
            rhs[h*E:(h+1)*E]=scaled[h]
            rhs[(1-h)*E:(2-h)*E]=jnp.zeros((E,R),BF)
            delta=jnp.sum(scaled[h].astype(F32)*ot[h*E:(h+1)*E],axis=0,keepdims=True)
            hi=delta.astype(BF).astype(F32)
            lo=delta-hi
            spot=lax.broadcasted_iota(jnp.int32,(16,R),0)
            rhs[W:W+16]=jnp.where(spot==0,-hi,jnp.where(spot==1,-lo,0.0)).astype(BF)
            for c in range(0,m,ch):
                g=dot(vaug[c:c+ch],rhs[...])
                ds[c:c+ch,h*R:(h+1)*R]=(p[0,h,base+c:base+c+ch].astype(F32)*g).astype(BF)
            kq[SPAN:,base:base+m]=kt[h*E:(h+1)*E]
            both=dot(kq[:,base:base+m],ds[:m,h*R:(h+1)*R])
            dqs.append(both[SPAN:]*0.125)
            nacc[h]+=dot(both[:SPAN].astype(BF),ohq[i])
        dq[i]=jnp.transpose(jnp.concatenate(dqs,axis=0)).astype(BF)
        for c in range(0,m,ch):
            dk=dot(ds[c:c+ch],qm[...])
            dv=dot(p[0,0,base+c:base+c+ch],dm[:R])+dot(p[0,1,base+c:base+c+ch],dm[R:])
            if i<n-1:
                dkf[i,c:c+ch]=dk.astype(BF); dvf[i,c:c+ch]=dv.astype(BF)
            else:
                dks[c:c+ch]=dk.astype(BF); dvs[c:c+ch]=dv.astype(BF)
        base+=m
    for h in range(2):
        wide=jnp.concatenate([nacc[h],jnp.zeros((SPAN,SPAN),F32)],axis=1)
        rolled=pltpu.roll(wide,0,1,stride=1,stride_axis=0)
        t[0,h:h+1]=jnp.sum(rolled,axis=0,keepdims=True)

def attend_back_call(q,kf,vf,ks,vs,layq,layf,lays,o,do,p,l):
    n,R,D=q.shape; L=kf.shape[1]; S=ks.shape[0]; H=p.shape[0]*2; E=D//H; W=2*E
    KT=(n-1)*L+S
    full=lambda a: pl.BlockSpec(a.shape,lambda j:(0,)*a.ndim)
    rows=lambda: pl.BlockSpec((n,R,W),lambda j:(0,0,j))
    kb=lambda: pl.BlockSpec((n-1,L,W),lambda j:(0,0,j))
    sb=lambda: pl.BlockSpec((S,W),lambda j:(0,j))
    return pl.pallas_call(functools.partial(attend_back,n,L,S,R,E),
      grid=(H//2,),
      in_specs=[rows(),kb(),kb(),sb(),sb(),full(layq),full(layf),full(lays),rows(),rows(),
        pl.BlockSpec((1,2,KT,R),lambda j:(j,0,0,0)),pl.BlockSpec((n,1,2,R),lambda j:(0,j,0,0))],
      out_specs=[rows(),kb(),kb(),sb(),sb(),pl.BlockSpec((1,2,2*SPAN),lambda j:(j,0,0))],
      out_shape=[jax.ShapeDtypeStruct((n,R,D),BF),jax.ShapeDtypeStruct(kf.shape,BF),jax.ShapeDtypeStruct(kf.shape,BF),
        jax.ShapeDtypeStruct(ks.shape,BF),jax.ShapeDtypeStruct(ks.shape,BF),jax.ShapeDtypeStruct((H//2,2,2*SPAN),F32)],
      scratch_shapes=[pltpu.VMEM((SPAN+E,KT),BF),pltpu.VMEM((L,2*W),BF),pltpu.VMEM((2*W,R),BF),pltpu.VMEM((L,2*R),BF),
        pltpu.VMEM((n,R,SPAN),BF),pltpu.VMEM((2,SPAN,SPAN),F32),pltpu.VMEM((2*R,W),BF),pltpu.VMEM((2*R,W),BF)],
      compiler_params=pltpu.CompilerParams(vmem_limit_bytes=56*2**20,dimension_semantics=("arbitrary",)),
      name="attend_back",
    )(q,kf,vf,ks,vs,layq,layf,lays,o,do,p,l)


EPSILON = 1e-06
FORWARD_TOKENS = (-8.5, -8, -7, -6, -5, -4, -3, -2)
FORWARD_PIECES = 3
FORWARD_WAYS = (0,) * 5 + (1,) * 5 + (0,) * 1
FORWARD_AT = (
    (-9, -8, -7, -6, -5),
    (-8, -7, -6, -5, -4),
    (-7, -6, -5, -4, -3),
    (-6, -5, -4, -3, -2),
    (-5, -4, -3, -2, 4),
    (-4, -3, -2, 4, 8),
    (-3, -2, 4, 8, 12),
    (-2, 4, 8, 12, 16),
    (4, 8, 12, 16, 20),
    (8, 12, 16, 20, 24),
)
FF_SUMS = 3
FF_SUM = (0, 2)
FF_SUM_LAG = (0, 3, 7, 11, 16)
BACK_SUM = (2, 2, 4)


MESH = pl.DeviceIdType.MESH


class Place:
    def __init__(self, mostly_y=False):
        dp = lax.axis_index("dp")
        self.x = lax.axis_index("blk")
        self.z, self.y, self.c = dp // 4, (dp // 2) % 2, dp % 2
        c = 1 if mostly_y else self.c
        self.y1, self.x1 = (self.y + 1 - c) % 2, (self.x + c) % 2
        self.y2, self.x2 = (self.y + c) % 2, (self.x + 1 - c) % 2

    def device(self, z, y, c, x):
        return ((z * 2 + y) * 2 + c, x)

    def along_z(self, d):
        return self.device((self.z + d) % 4, self.y, self.c, self.x)

    def along_x(self):
        return self.device(self.z, self.y, self.c, 1 - self.x)

    def along_y(self):
        return self.device(self.z, 1 - self.y, self.c, self.x)

    def first(self):
        return self.device(self.z, self.y1, self.c, self.x1)

    def second(self):
        return self.device(self.z, self.y2, self.c, self.x2)

    def core(self):
        return self.device(self.z, self.y, 1 - self.c, self.x)

    def greet(self):
        barrier = pltpu.get_barrier_semaphore()
        partners = [self.along_z(d) for d in (1, 2, 3)] + [self.first(), self.second(), self.core()]
        for partner in partners:
            pl.semaphore_signal(barrier, inc=1, device_id=partner, device_id_type=MESH)
        pl.semaphore_wait(barrier, len(partners))


def remote(src, dst, sems, k, device):
    return pltpu.make_async_remote_copy(
        src_ref=src, dst_ref=dst, send_sem=sems[0].at[k], recv_sem=sems[1].at[k], device_id=device, device_id_type=MESH
    )


GATHER_COPIES = 10


def gather_stages(at, shard, whole, sems, local, base, cols=None, plane=None):
    z, y, c, x = at.z, at.y, at.c, at.x
    cols = pl.ds(0, shard.shape[1]) if cols is None else cols
    shard = shard.at[:, cols]
    own = whole.at[z if plane is None else 0, y, c, x]
    keep = pltpu.make_async_copy(shard, own, local)

    def group(yy, xx):
        return whole.at[:, yy, c, xx]

    def copy(k):
        if k < 3:
            return remote(shard, own, sems, base + k, at.along_z(k + 1))
        view, device = {
            3: (group(y, x), at.first()),
            4: (group(y, x), at.second()),
            5: (group(y, x), at.core()),
            6: (group(at.y1, at.x1), at.second()),
            7: (group(at.y1, at.x1), at.core()),
            8: (group(at.y2, at.x2), at.core()),
            9: (group(1 - y, 1 - x), at.core()),
        }[k]
        return remote(view, view, sems, base + k, device)

    def one():
        def start():
            keep.start()
            for k in range(3):
                copy(k).start()

        start() if plane is None else pl.when(z == plane)(start)

    def two():
        if plane is None:
            keep.wait()
            for k in range(3):
                copy(k).wait_recv()
        else:
            pl.when(z == plane)(keep.wait)
            d = (z - plane + 4) % 4
            arrival = remote(shard, own, sems, base + d - 1, at.along_z(1))
            pl.when(z != plane)(arrival.wait_recv)
        for k in (3, 4, 5):
            copy(k).start()

    def three():
        copy(3).wait_recv()
        for k in (6, 7):
            copy(k).start()

    def four():
        copy(4).wait_recv()
        copy(8).start()
        copy(6).wait_recv()
        copy(9).start()

    def five():
        for k in (5, 7, 8, 9):
            copy(k).wait_recv()
        for k in range(3, 10):
            copy(k).wait_send()

        def sent():
            for k in range(3):
                copy(k).wait_send()

        sent() if plane is None else pl.when(z == plane)(sent)

    return [one, two, three, four, five]


def gather_stages_x(at, shard, whole, sems, local, base):
    z, y, c, x = at.z, at.y, at.c, at.x
    own = whole.at[z, y, c, x]
    keep = pltpu.make_async_copy(shard, own, local)

    def copy(k):
        if k == 0:
            return remote(shard, own, sems, base, at.along_x())
        view, device = {
            1: (whole.at[z, y, c], at.along_z(1)),
            2: (whole.at[z, y, c], at.along_z(2)),
            3: (whole.at[z, y, c], at.along_z(3)),
            4: (whole.at[:, y, c], at.along_y()),
            5: (whole.at[:, y, c], at.core()),
            6: (whole.at[:, 1 - y, c], at.core()),
        }[k]
        return remote(view, view, sems, base + k, device)

    def step(arrivals, starts):
        def run():
            for k in arrivals:
                copy(k).wait_recv()
            for k in starts:
                copy(k).start()

        return run

    def one():
        keep.start()
        copy(0).start()

    def two():
        keep.wait()
        step((0,), (1, 2, 3))()

    def five():
        step((5, 6), ())()
        for k in range(7):
            copy(k).wait_send()

    return [one, two, step((1, 2, 3), (4, 5)), step((4,), (6,)), five]


def small_stages(at, part, total, held, got, sems, base):
    def copy(k):
        device = [at.core, at.along_y, at.along_x][k]() if k < 3 else at.along_z(k - 2)
        return remote(held.at[min(k, 3)], got.at[k], sems, base + k, device)

    def one():
        held[0] = part[...]
        copy(0).start()

    def add(k):
        def run():
            copy(k).wait_recv()
            held[k + 1] = held[k] + got[k]
            for following in (k + 1,) if k < 2 else (3, 4, 5):
                copy(following).start()

        return run

    def five():
        parts = [held[3]]
        for d in (1, 2, 3):
            copy(2 + d).wait_recv()
            parts.append(got[2 + d])
        out = jnp.zeros_like(parts[0])
        for spot in range(4):
            for d in range(4):
                out = out + jnp.where((at.z - d + 4) % 4 == spot, parts[d], 0.0)
        total[...] = out
        for k in range(6):
            copy(k).wait_send()

    return [one, add(0), add(1), add(2), five]


def norm_rows(x):
    return lax.rsqrt(jnp.mean(x * x, axis=1, keepdims=True) + EPSILON)


def dot_nt(a, b):
    return lax.dot_general(a, b, (((1,), (1,)), ((), ())), preferred_element_type=F32)


def flipped(a):
    return jnp.transpose(a.astype(F32)).astype(BF)


TICKS = 6


def feed_forward_plan(sums):
    events = []
    for i, (stages, j) in enumerate(sums):
        for s, lag in enumerate(FF_SUM_LAG):
            events.append((TICKS * (j + 1) + FF_SUM[i % 2] + lag, stages[s]))
    plan = {}
    for when, stage in sorted(events, key=lambda e: e[0]):
        plan.setdefault(when, []).append(stage)
    return plan


def feed_forward(R, blocks, *refs):
    flag, att_, tok_, up_, wo_, grow = refs[:6]
    given = refs[6:8]
    refs = list(refs[8:])
    take = lambda k: [refs.pop(0) for _ in range(k)]
    mixed, dres, datt, dwo = take(4)
    last = FF_SUMS
    handed = [take(2) for _ in range(last, blocks)]
    (dgain,) = take(1)
    totals_in = take(last)
    (total_out,) = take(1)
    att, tok, up, wo, wbi, wbt, n2, n2t, resid, acc, dn2, act_t, dpre_s, parts_in, parts_out = take(15)
    sum_scratch = [take(5) for _ in range(2 * last)]
    send, recv, local = take(3)
    rows, width = att.shape
    block = wbi.shape[2]
    piece = rows // 4
    pieces = [pl.ds(i, piece) for i in range(0, rows, piece)]
    step = pl.program_id(0)
    slot = lax.rem(step, 2)
    at = Place()
    sems = (send, recv)

    sums = []
    for j in range(last):
        for which, (part, total) in enumerate([(parts_in.at[j], totals_in[j]), (parts_out.at[j], total_out)]):
            i = len(sums)
            chain = Sum(at, part, total, sum_scratch[i], sems, None, Sum.COPIES * i, None, j if which else None)
            sums.append((chain.stages, j))
    plan = feed_forward_plan(sums)

    def local_copy(a, b, k):
        return pltpu.make_async_copy(a, b, local.at[k])

    def weights(j):
        hidden = pl.ds(j * block, block)
        return [local_copy(given[0].at[:, hidden], wbi.at[j % 2], 4), local_copy(given[1].at[hidden], wbt.at[j % 2], 5)]

    def tick(t):
        for when in plan:
            if when < TICKS * blocks and when % TICKS == t:

                @pl.when(step == when // TICKS)
                def _(when=when):
                    for stage in plan[when]:
                        stage()

    @pl.when(step == 0)
    def _():
        loads = [local_copy(a, b, i) for i, (a, b) in enumerate([(tok_, tok), (att_, att), (wo_, wo), (up_, up)])]
        for load in loads + weights(0):
            load.start()
        at.greet()
        for load in loads:
            load.wait()
        for a in (tok, up):
            a[:R], a[R:] = swapped(flag, a[:R], a[R:])
        for b in pieces:
            x = tok[b].astype(F32) + dot(att[b], wo[...])
            resid[b] = x
            normed = (x * norm_rows(x) * grow[1:2]).astype(BF)
            n2[b] = normed
            n2t[:, b] = flipped(normed)
            acc[b] = x
            dn2[b] = jnp.zeros_like(x)

    for j in range(blocks):

        @pl.when(step == j)
        def _(j=j):
            for load in weights(j):
                load.wait()
            if j + 1 < blocks:
                for load in weights(j + 1):
                    load.start()

    for i, b in enumerate(pieces):
        tick(i)
        pre = dot(n2[b], wbi[slot])
        dact = dot_nt(up[b], wbt[slot])
        half = 0.5 + 0.5 * lax.erf(pre * 0.7071067811865476)
        act = (pre * half).astype(BF)
        dpre = (dact * (half + pre * (jnp.exp(-0.5 * pre * pre) * 0.3989422804014327))).astype(BF)
        acc[b] += dot(act, wbt[slot])
        dn2[b] += dot_nt(dpre, wbi[slot])
        act_t[:, b] = flipped(act)
        dpre_s[b] = dpre
    tick(4)
    grad_in = dot(n2t[...], dpre_s[...])
    tick(5)
    grad_out = dot(act_t[...], up[...])

    into_slabs(grad_in, parts_in.at[step])
    count = parts_out.shape[5]
    for i in range(8):
        parts_out[step, 0, i // 4, i // 2 % 2, i % 2] = grad_out[count * i : count * (i + 1)].astype(BF)
    hand = [
        [local_copy(parts_in.at[j], handed[j - last][0], 6 + 2 * j), local_copy(parts_out.at[j], handed[j - last][1], 7 + 2 * j)]
        for j in range(last, blocks)
    ]
    for j in range(last, blocks):

        @pl.when(step == j)
        def _(j=j):
            for copy in hand[j - last]:
                copy.start()

    @pl.when(step == blocks - 1)
    def _():
        rest = [stage for t in sorted(plan) if t >= TICKS * blocks for stage in plan[t]]

        def some(count):
            for _ in range(min(count, len(rest))):
                rest.pop(0)()

        ends = []
        some(2)
        for i, b in enumerate(pieces):
            n2[b] = acc[b].astype(BF)
        n2[:R], n2[R:] = swapped(flag, n2[:R], n2[R:])
        ends.append(local_copy(n2, mixed, 2))
        ends[-1].start()
        total = None
        for b in pieces:
            x, d = resid[b], dn2[b]
            back = norm_rows(x)
            a = grow[1:2] * d
            part = jnp.sum(d * x * back, axis=0, keepdims=True)
            total = part if total is None else total + part
            g = up[b].astype(F32) + back * a - x * (back * back * back) * jnp.mean(a * x, axis=1, keepdims=True)
            dn2[b] = g
            g = g.astype(BF)
            up[b] = g
            tok[b] = dot_nt(g, wo[...]).astype(BF)
            act_t[:width, b] = flipped(att[b])
            some(1)
        dgain[...] = total
        ends += [local_copy(dn2, dres, 3), local_copy(tok, datt, 4)]
        ends[-1].start()
        ends[-2].start()
        dpre_s[:width, :width] = dot(act_t[:width], up[...]).astype(BF)
        ends.append(local_copy(dpre_s.at[pl.ds(0, width), pl.ds(0, width)], dwo, 5))
        ends[-1].start()
        some(100)
        for end in ends + sum(hand, []):
            end.wait()


def feed_forward_call(flag, att, tokens, up, wo, grow, wi, wt):
    rows, D = tokens.shape
    R = rows // 2
    blocks = 4
    last = FF_SUMS
    block = wi.shape[1] // blocks
    share_in, share_out = (D // 32, block), (wt.shape[0] // 32, D)
    anywhere = pl.BlockSpec(memory_space=pl.ANY)
    whole = lambda shape: pl.BlockSpec(shape, lambda j: (0,) * len(shape))
    vmem = lambda *s: pltpu.VMEM(s, BF)
    wide = lambda *s: pltpu.VMEM(s, F32)
    slab_in, slab_out = (4, 2, 2, 2) + share_in, (1, 2, 2, 2) + share_out
    outs = [((rows, D), BF), ((rows, D), F32), ((rows, D), BF), ((D, D), BF)] + [(slab_in, BF), (slab_out, BF)] * (blocks - last)
    small = [((1, D), F32)] + [(share_in, F32)] * last + [(share_out, F32)]
    copies = max(Sum.COPIES * 2 * last, 1)
    scratch = [vmem(rows, D)] * 3 + [vmem(D, D), vmem(2, D, block), vmem(2, block, D), vmem(rows, D), vmem(D, rows)]
    scratch += [wide(rows, D)] * 3 + [vmem(block, rows), vmem(rows, block), vmem(blocks, *slab_in), vmem(blocks, *slab_out)]
    scratch += (Sum.scratch(4, *share_in, 0) + Sum.scratch(1, *share_out, 0)) * last
    scratch += [pltpu.SemaphoreType.DMA((copies,))] * 2 + [pltpu.SemaphoreType.DMA((6 + 2 * blocks,))]
    return pl.pallas_call(
        functools.partial(feed_forward, R, blocks),
        grid=(blocks,),
        in_specs=[pl.BlockSpec(memory_space=pltpu.SMEM)] + [anywhere] * 4 + [whole(grow.shape)] + [anywhere] * 2,
        out_specs=[anywhere] * len(outs) + [whole(s) for s, _ in small],
        out_shape=[jax.ShapeDtypeStruct(*s) for s in outs + small],
        scratch_shapes=scratch,
        compiler_params=pltpu.CompilerParams(
            vmem_limit_bytes=60 * 2**20, dimension_semantics=("arbitrary",), collective_id=2, has_side_effects=True
        ),
        name="feed_forward",
    )(flag, att, tokens, up, wo, grow, wi, wt)


def turn_plan(chains, places):
    plan = {}
    for chain, at in zip(chains, places):
        for place, stage in zip(at, chain):
            plan.setdefault(place, []).insert(0, stage)
    return plan


def together(*chains):
    def stage(s):
        def run():
            for chain in chains:
                chain[s]()

        return run

    return [stage(s) for s in range(len(chains[0]))]


def unslab(slabs, flat):
    rows = slabs.shape[4]
    for i in range(16):
        pair = [slabs[i // 4, i // 2 % 2, i % 2, x] for x in range(2)]
        flat[2 * rows * i : 2 * rows * (i + 1)] = jnp.concatenate(pair, axis=0)


def normed_rows(x, gain):
    x = x.astype(F32)
    return (x * norm_rows(x) * gain).astype(BF)


def block_chain(ats, shard_in, shard_out, j, whole_in, whole_out, sems, local, k):
    width = whole_in.shape[5]
    return [
        gather_stages(ats[0], shard_in, whole_in, sems, local.at[k], GATHER_COPIES * k, pl.ds(j * width, width)),
        gather_stages(ats[1], shard_out, whole_out, sems, local.at[k + 1], GATHER_COPIES * (k + 1), None, j),
    ]


def swapped(lengths, a, b):
    turn = lengths[0] < lengths[1]
    return jnp.where(turn, b, a), jnp.where(turn, a, b)


def coordinates(at, lengths, layout, R, S):
    long, short = swapped(lengths, layout[0:1], layout[1:2])
    keys = jnp.where(at.x == 0, long, jnp.concatenate([long[:, R:], long[:, :R]], axis=1))
    return keys, short[:, :S], keys[:, :R], jnp.where(at.x == 0, short[:, :R], short[:, R:])


def forward_kernel(R, L, S, E, pairs, *refs):
    flag, tokens, layout, table, basis = refs[:5]
    shards = refs[5:12]
    refs = list(refs[12:])
    take = lambda k: [refs.pop(0) for _ in range(k)]
    o, pa, pb, cs, grow = take(5)
    kept = take(7)
    wholes = take(6)
    kcat, qcat, vt, s_ref, ohq, xfar, xshort, flat, normed, tok, held, stats, u = take(13)
    q, kf, vf, ks, vs, nkt, nst = inner = take(7)
    slabs = take(4)
    send, recv, local = take(3)
    W = 2 * E
    D = tok.shape[2]
    at = Place()
    sems = (send, recv)
    ways = [(at, Place(True))[i] for i in FORWARD_WAYS]
    targets = slabs + wholes[3:]
    chains = []
    for i, cols in [(i, None) for i in range(5)] + [(i, cols) for i in (5, 6) for cols in pieces_of(shards[i].shape[1])]:
        k = len(chains)
        view = targets[i] if cols is None else targets[i].at[:, :, :, :, :, cols]
        chains.append(gather_stages(ways[k], shards[i], view, sems, local.at[k], GATHER_COPIES * k, cols))
    count = len(chains)
    chains = [together(chains[0], chains[1])] + chains[2:]
    plan = turn_plan(chains, FORWARD_AT)
    spare = GATHER_COPIES * count
    short = remote(tok.at[1, pl.ds(0, S)], xshort, sems, spare, at.along_x())
    long = []
    for i in range(len(FORWARD_TOKENS)):
        some = pl.ds(i * R // len(FORWARD_TOKENS), R // len(FORWARD_TOKENS))
        long.append(remote(tok.at[0, some], xfar.at[some], sems, spare + 1 + i, at.along_x()))
    out = lambda i, a, b: pltpu.make_async_copy(a, b, local.at[count + i])
    weights_out = [out(i, slabs[1 + i], wholes[i]) for i in range(3)]
    kept_out = [out(3 + i, a, b) for i, (a, b) in enumerate(zip(inner, kept))]

    for place, copy in zip(FORWARD_TOKENS, long):
        plan.setdefault(place, []).append(copy.start)
    plan[FORWARD_TOKENS[-1]].append(lambda: pl.when(at.x == 0)(short.start))

    def turn(t):
        for stage in plan.get(t, []):
            stage()

    step = pl.program_id(0)
    pair = lax.rem(step, pairs)

    @pl.when(step == 0)
    def _():
        at.greet()
        turn(-9)
        tok[0], tok[1] = swapped(flag, tokens[0], tokens[1])
        turn(-8.5)
        long_keys, short_keys, *queries = coordinates(at, flag, layout, R, S)
        for i, (base, row) in enumerate([(0, long_keys), (L, short_keys)]):
            kcat[base : base + row.shape[1], W:] = jnp.transpose(eye_of(row, SPAN, False).astype(F32)).astype(BF)
            ohq[i] = eye_of(queries[i], SPAN, False)
        rows = lax.dot_general(table[...].astype(BF), basis[...], (((0,), (0,)), ((), ())), preferred_element_type=F32)
        for h in range(2 * pairs):
            u[h] = rows[h : h + 1]
        vt[:, E:] = jnp.ones((2, vt.shape[1] - E, vt.shape[2]), BF)
        for t in range(-8, -4):
            turn(t)
        gslab = slabs[0]
        columns = jnp.concatenate(
            [gslab[i // 8, i // 4 % 2, i // 2 % 2, i % 2].astype(F32) for i in range(32)], axis=0
        )
        grow[...] = jnp.transpose(columns)[:8]
        gain = grow[0:1]
        weights_out[0].start()
        unslab(slabs[1], flat.at[0])
        for i in range(2):
            normed[i] = normed_rows(tok[i], gain)
            q[i] = (dot(normed[i], flat[0]).astype(BF).astype(F32) * 0.125).astype(BF)
        turn(-4)
        weights_out[1].start()
        unslab(slabs[2], flat.at[0])
        kf[:R] = dot(normed[0], flat[0]).astype(BF)
        turn(-3)
        weights_out[2].start()
        unslab(slabs[3], flat.at[1])
        vf[:R] = dot(normed[0], flat[1]).astype(BF)
        kept_out[0].start()
        turn(-2)

    @pl.when(step == pairs)
    def _():
        nkt[:, :R] = flipped(normed[0])
        nst[...] = flipped(normed[1])
        for copy in long:
            copy.wait()

        @pl.when(at.x == 0)
        def _():
            short.wait_send()

        @pl.when(at.x == 1)
        def _():
            short.wait_recv()

        @pl.when(at.x == 0)
        def _():
            xshort[...] = tok[1, :S]

        gain = grow[0:1]
        normed[0] = normed_rows(xfar[...], gain)
        normed[1, :S] = normed_rows(xshort[...], gain)
        kf[R:] = dot(normed[0], flat[0]).astype(BF)
        vf[R:] = dot(normed[0], flat[1]).astype(BF)
        ks[...] = dot(normed[1, :S], flat[0]).astype(BF)
        vs[...] = dot(normed[1, :S], flat[1]).astype(BF)
        nkt[:, R:L] = flipped(normed[0])
        nkt[:, L:] = flipped(normed[1, :S])
        for copy in kept_out[1:]:
            copy.start()

    steps = 2 * pairs

    def tick(spot):
        for t in sorted(plan):
            if t >= 2 * steps and spot == 2 or 0 <= t < 2 * steps and t % 2 == spot:

                @pl.when(step == min(t // 2, steps - 1))
                def _(t=t):
                    turn(t)

    here = pl.ds(pl.multiple_of(pair * W, W), W)

    def attend_to(i, base, m, keys, values, into, ticking):
        ch = min(CH, m)
        kcat[base : base + m, :W] = keys
        vt[0, :E, :m], vt[1, :E, :m] = jnp.split(flipped(values), 2, axis=0)
        qt = flipped(q[i, :, here])
        found = []
        for h in range(2):
            if ticking:
                tick(h)
            toep = pltpu.roll(jnp.broadcast_to(u[2 * pair + h], (SPAN, 2 * SPAN)), 0, 1, stride=1, stride_axis=0)
            qcat[h * E : (h + 1) * E] = qt[h * E : (h + 1) * E]
            qcat[(1 - h) * E : (2 - h) * E] = jnp.zeros((E, R), BF)
            qcat[W:] = dot(toep[:, :SPAN].astype(BF), ohq[i]).astype(BF)
            top = jnp.full((8, R), -jnp.inf, F32)
            for c in range(0, m, ch):
                s = dot(kcat[base + c : base + c + ch], qcat[...])
                s_ref[c : c + ch] = s
                top = jnp.maximum(top, jnp.max(s.reshape(ch // 8, 8, R), axis=0))
            top = jnp.max(top, axis=0, keepdims=True)
            for c in range(0, m, ch):
                into[h, c : c + ch] = jnp.exp(s_ref[c : c + ch] - top).astype(BF)
            full = dot(vt[h, :, :m], into[h, :m])
            found.append((top, full[E : E + 1], full[:E]))
        return found

    def heads(parts):
        return jnp.transpose(jnp.concatenate(parts, axis=0)).astype(BF)

    @pl.when(step < pairs)
    def _():
        found = attend_to(0, 0, R, kf[:R, here], vf[:R, here], pa.at[0], True)
        for h, (top, total, full) in enumerate(found):
            stats[pair, 2 * h : 2 * h + 1] = top
            stats[pair, 2 * h + 1 : 2 * h + 2] = total
            held[pair, h * E : (h + 1) * E] = full

    @pl.when(step >= pairs)
    def _():
        m = L - R
        found = attend_to(0, R, m, kf[R:, here], vf[R:, here], pb.at[0, :, pl.ds(0, m)], True)
        parts = []
        for h, (top, total, full) in enumerate(found):
            first, first_total = stats[pair, 2 * h : 2 * h + 1], stats[pair, 2 * h + 1 : 2 * h + 2]
            most = jnp.maximum(first, top)
            a, b = jnp.exp(first - most), jnp.exp(top - most)
            back = 1.0 / (a * first_total + b * total)
            cs[0, 0, h : h + 1] = a * back
            cs[1, 0, h : h + 1] = b * back
            parts.append(held[pair, h * E : (h + 1) * E] * (a * back) + full * (b * back))
        o[0] = heads(parts)
        found = attend_to(1, L, S, ks[:, here], vs[:, here], pb.at[0, :, pl.ds(m, S)], False)
        for h, (top, total, full) in enumerate(found):
            cs[2, 0, h : h + 1] = 1.0 / total
        o[1] = heads([full / total for _, total, full in found])

    tick(2)

    @pl.when(step == steps - 1)
    def _():
        for copy in weights_out + kept_out:
            copy.wait()


def pieces_of(width):
    return [pl.ds(i * width // FORWARD_PIECES, width // FORWARD_PIECES) for i in range(FORWARD_PIECES)]


def forward_call(flag, tokens, layout, table, basis, shards, S):
    n, R, D = tokens.shape
    L = layout.shape[1]
    pairs = table.shape[1] // 2
    E = D // (2 * pairs)
    W = 2 * E
    KT = L + S
    whole = lambda shape: pl.BlockSpec(shape, lambda j: (0,) * len(shape))
    anywhere = pl.BlockSpec(memory_space=pl.ANY)
    vmem = lambda *s: pltpu.VMEM(s, BF)
    wide = lambda *s: pltpu.VMEM(s, F32)
    early = lambda j: jnp.minimum(j, pairs - 1)
    late = lambda j: jnp.maximum(j - pairs, 0)
    kept = [(n, R, D), (L, D), (L, D), (S, D), (S, D), (D, KT), (D, R)]
    chains = 5 + 2 * FORWARD_PIECES
    copies = GATHER_COPIES * chains + 1 + len(FORWARD_TOKENS)
    gathered = [(4, 2, 2, 2) + s.shape for s in shards]
    filled = gathered[1:]
    blocked = [
        ((n, R, D), BF, pl.BlockSpec((n, R, W), lambda j: (0, 0, late(j)))),
        ((pairs, 2, R, R), BF, pl.BlockSpec((1, 2, R, R), lambda j: (early(j), 0, 0, 0))),
        ((pairs, 2, KT - R, R), BF, pl.BlockSpec((1, 2, KT - R, R), lambda j: (late(j), 0, 0, 0))),
        ((3, pairs, 2, R), F32, pl.BlockSpec((3, 1, 2, R), lambda j: (0, late(j), 0, 0))),
        ((8, D), F32, whole((8, D))),
    ]
    return pl.pallas_call(
        functools.partial(forward_kernel, R, L, S, E, pairs),
        grid=(2 * pairs,),
        in_specs=[pl.BlockSpec(memory_space=pltpu.SMEM)]
        + [whole(a.shape) for a in (tokens, layout, table, basis)]
        + [anywhere] * 7,
        out_specs=[b[2] for b in blocked] + [anywhere] * (len(kept) + len(filled)),
        out_shape=[jax.ShapeDtypeStruct(*b[:2]) for b in blocked] + [jax.ShapeDtypeStruct(s, BF) for s in kept + filled],
        scratch_shapes=[vmem(KT, W + SPAN), vmem(W + SPAN, R), vmem(2, E + 16, R), wide(R, R), vmem(n, SPAN, R)]
        + [vmem(R, D), vmem(S, D), vmem(2, D, D), vmem(n, R, D), vmem(n, R, D), wide(pairs, W, R), wide(pairs, 8, R), wide(2 * pairs, 1, 2 * SPAN)]
        + [vmem(*s) for s in kept]
        + [vmem(*s) for s in gathered[:4]]
        + [pltpu.SemaphoreType.DMA((copies,))] * 2
        + [pltpu.SemaphoreType.DMA((chains + 10,))],
        compiler_params=pltpu.CompilerParams(
            vmem_limit_bytes=60 * 2**20, dimension_semantics=("arbitrary",), collective_id=0, has_side_effects=True
        ),
        name="forward",
    )(flag, tokens, layout, table, basis, *shards)


class Sum:
    COPIES = 7

    def __init__(self, at, part, total, scratch, sems, local, base, cols=None, plane=None):
        self.at, self.part, self.total, self.sems, self.base, self.plane = at, part, total, sems, base, plane
        self.cols = pl.ds(0, total.shape[1]) if cols is None else cols
        self.acc, self.got_diag, self.got_one, self.got_two, self.got_z = scratch[:5]
        self.held = scratch[5] if len(scratch) > 5 else None
        if self.held is not None:
            self.keep = pltpu.make_async_copy(part.at[:, :, at.c, :, :, self.cols], self.held, local)
        self.stages = [self.one, self.two, self.three, self.four, self.five]

    @staticmethod
    def scratch(depth, rows, columns, held):
        slab = (rows, columns)
        shapes = [(depth, 2, 2) + slab] + [(depth,) + slab] * 3 + [(3,) + slab] + [(depth, 2, 2) + slab] * held
        return [pltpu.VMEM(s, BF) for s in shapes]

    def send(self, k):
        at, acc = self.at, self.acc
        if k > 3:
            d = k - 3
            src, dst, device = acc.at[(at.z + d) % 4, at.y, at.x], self.got_z.at[d - 1], at.along_z(d)
        else:
            src, dst, device = [
                (self.part.at[:, :, 1 - at.c, :, :, self.cols], acc, at.core()),
                (acc.at[:, 1 - at.y, 1 - at.x], self.got_diag, at.second()),
                (acc.at[:, at.y2, at.x2], self.got_two, at.second()),
                (acc.at[:, at.y1, at.x1], self.got_one, at.first()),
            ][k]
        return remote(src, dst, self.sems, self.base + k, device)

    def to_plane(self):
        at = self.at
        d = (self.plane - at.z + 4) % 4
        k = self.base + 3 + d
        return pltpu.make_async_remote_copy(
            src_ref=self.acc.at[0, at.y, at.x],
            dst_ref=self.got_z.at[d - 1],
            send_sem=self.sems[0].at[k],
            recv_sem=self.sems[1].at[k],
            device_id=at.device(self.plane, at.y, at.c, at.x),
            device_id_type=MESH,
        )

    def one(self):
        self.send(0).start()
        if self.held is not None:
            self.keep.start()

    def two(self):
        at, acc = self.at, self.acc
        if self.held is not None:
            self.keep.wait()
        self.send(0).wait_recv()

        def add(i, _):
            for yy in range(2):
                own = self.held[i, yy] if self.held is not None else self.part[i, yy, at.c, :, :, self.cols]
                acc[i, yy] = (acc[i, yy].astype(F32) + own.astype(F32)).astype(BF)
            return 0

        lax.fori_loop(0, acc.shape[0], add, 0)
        self.send(1).start()
        self.send(2).start()

    def three(self):
        at, acc = self.at, self.acc
        self.send(1).wait_recv()
        acc[:, at.y1, at.x1] = (acc[:, at.y1, at.x1].astype(F32) + self.got_diag[...].astype(F32)).astype(BF)
        self.send(3).start()

    def four(self):
        at, acc = self.at, self.acc
        self.send(2).wait_recv()
        self.send(3).wait_recv()
        mine = acc[:, at.y, at.x].astype(F32) + self.got_one[...].astype(F32) + self.got_two[...].astype(F32)
        acc[:, at.y, at.x] = mine.astype(BF)
        if self.plane is None:
            for k in (4, 5, 6):
                self.send(k).start()
        else:

            @pl.when(at.z != self.plane)
            def _():
                self.to_plane().start()

    def five(self):
        at = self.at

        def collect():
            out = self.acc[at.z if self.plane is None else 0, at.y, at.x].astype(F32)
            for d in (1, 2, 3):
                arrival = remote(self.got_z.at[d - 1], self.got_z.at[d - 1], self.sems, self.base + 3 + d, at.along_z(d))
                arrival.wait_recv()
                out = out + self.got_z[d - 1].astype(F32)
            self.total[:, self.cols] = out

        for k in range(4):
            self.send(k).wait_send()
        if self.plane is None:
            collect()
            for k in (4, 5, 6):
                self.send(k).wait_send()
        else:
            pl.when(at.z == self.plane)(collect)

            @pl.when(at.z != self.plane)
            def _():
                self.to_plane().wait_send()


def into_slabs(flat, slabs):
    rows = slabs.shape[4]
    for i in range(32):
        slabs[i // 8, i // 4 % 2, i // 2 % 2, i % 2] = flat[rows * i : rows * (i + 1)].astype(BF)


def backward_kernel(R, L, S, E, pairs, planes, *refs):
    flag, q, kf, vf, ks, vs, o, do, pa, pb, cs, layout = refs[:12]
    refs = list(refs[12:])
    take = lambda k: [refs.pop(0) for _ in range(k)]
    parts = take(len(planes))
    nkt_, nst_, wq, wk, wv, tok, dres, grow, dg2 = take(9)
    gtok, small_total = take(2)
    totals = take(3 + len(planes))
    kq, vaug, rhs, ds, ohq, nacc, qm, dm, held = take(9)
    dq, dk, dv, nkt, nst, ws, toks, dress = take(8)
    far, fars, gfar, gshort, ends = take(5)
    tsum, small, small_held, small_got = take(4)
    send, recv, local = take(3)
    W = 2 * E
    D = ws.shape[1]
    at = Place()
    sems = (send, recv)
    sums = []

    def summed(part, total, held, plane=None):
        i = len(sums)
        sums.append(Sum(at, part, total, take(5 + held), sems, local.at[i], Sum.COPIES * i, None, plane))

    for part, total, plane in zip(parts, totals, planes):
        summed(part, total, 1, plane)
    early = len(sums)
    mats = take(3)
    for part, total in zip(mats, totals[early:]):
        summed(part, total, 0)
    base = Sum.COPIES * len(sums)
    small_chain = small_stages(at, small, small_total, small_held, small_got, sems, base)
    long = remote(far, gfar, sems, base + 6, at.along_x())
    short = remote(fars, gshort, sems, base + 7, at.along_x())
    loads = [(w, ws.at[i]) for i, w in enumerate((wq, wk, wv))] + [(nkt_, nkt), (nst_, nst), (tok, toks), (dres, dress)]
    loads = [pltpu.make_async_copy(a, b, local.at[len(sums) + i]) for i, (a, b) in enumerate(loads)]

    step = pl.program_id(0)
    pair = lax.rem(step, pairs)
    steps = 2 * pairs
    plan = {}
    for i in range(early):
        for s in range(5):
            when = 0 if s == 0 else int(BACK_SUM[0] + BACK_SUM[1] * i + BACK_SUM[2] * (s - 1))
            plan.setdefault(when, []).insert(0, sums[i].stages[s])

    def tick(spot):
        for t in plan:
            if t < 2 * steps and t % 2 == spot:

                @pl.when(step == t // 2)
                def _(t=t):
                    for stage in plan[t]:
                        stage()

    @pl.when(step == 0)
    def _():
        at.greet()
        for load in loads:
            load.start()
        long_keys, short_keys, *queries = coordinates(at, flag, layout, R, S)
        for i, (base, row) in enumerate([(0, long_keys), (L, short_keys)]):
            kq[:SPAN, base : base + row.shape[1]] = eye_of(row, SPAN, True)
            ohq[i] = jnp.transpose(eye_of(queries[i], SPAN, False).astype(F32)).astype(BF)
        vaug[:, W:] = (lax.broadcasted_iota(jnp.int32, (R, W), 1) < 2).astype(F32).astype(BF)
        rhs[...] = jnp.zeros_like(rhs)

    @pl.when(step == pairs)
    def _():
        for load in loads[:3]:
            load.wait()
        far[...] = (dot_nt(dk[R:L], ws[1]) + dot_nt(dv[R:L], ws[2])).astype(BF)
        long.start()
        ends[...] = dot_nt(dk[L:], ws[1]) + dot_nt(dv[L:], ws[2])
        fars[...] = ends[...].astype(BF)
        pl.when(at.x == 1)(short.start)

    nacc[...] = jnp.zeros_like(nacc)
    lane = lax.broadcasted_iota(jnp.int32, (R, W), 1)
    spot = lax.broadcasted_iota(jnp.int32, (16, R), 0)
    here = pl.ds(pl.multiple_of(pair * W, W), W)

    def attend_to(i, base, m, keys, values, p, scale, ticking):
        ch = min(CH, m)
        vaug[:m, :W] = values
        kt = flipped(keys)
        dot_, ot = jnp.transpose(do[i].astype(F32)), jnp.transpose(o[i].astype(F32))
        scaled = [(dot_[h * E : (h + 1) * E] * cs[scale, 0, h : h + 1]).astype(BF) for h in range(2)]
        don = flipped(jnp.concatenate(scaled, axis=0))
        qq = q[i]
        zero = jnp.zeros((R, W), BF)
        for h in range(2):
            mine = (lane < E) if h == 0 else (lane >= E)
            qm[h * R : (h + 1) * R] = jnp.where(mine, qq, zero)
            dm[h * R : (h + 1) * R] = jnp.where(mine, don, zero)
        dqs = []
        for h in range(2):
            if ticking:
                tick(h)
            rhs[h * E : (h + 1) * E] = scaled[h]
            rhs[(1 - h) * E : (2 - h) * E] = jnp.zeros((E, R), BF)
            delta = jnp.sum(scaled[h].astype(F32) * ot[h * E : (h + 1) * E], axis=0, keepdims=True)
            hi = delta.astype(BF).astype(F32)
            rhs[W : W + 16] = jnp.where(spot == 0, -hi, jnp.where(spot == 1, hi - delta, 0.0)).astype(BF)
            for c in range(0, m, ch):
                g = dot(vaug[c : c + ch], rhs[...])
                ds[c : c + ch, h * R : (h + 1) * R] = (p[h, c : c + ch].astype(F32) * g).astype(BF)
            kq[SPAN:, base : base + m] = kt[h * E : (h + 1) * E]
            both = dot(kq[:, base : base + m], ds[:m, h * R : (h + 1) * R])
            dqs.append(both[SPAN:] * 0.125)
            nacc[h] += dot(both[:SPAN].astype(BF), ohq[i])
        for c in range(0, m, ch):
            dk[base + c : base + c + ch, here] = dot(ds[c : c + ch], qm[...]).astype(BF)
            both = dot(p[0, c : c + ch], dm[:R]) + dot(p[1, c : c + ch], dm[R:])
            dv[base + c : base + c + ch, here] = both.astype(BF)
        return jnp.concatenate(dqs, axis=0)

    def diagonals(h):
        wide = jnp.concatenate([nacc[h], jnp.zeros((SPAN, SPAN), F32)], axis=1)
        return jnp.sum(pltpu.roll(wide, 0, 1, stride=1, stride_axis=0), axis=0, keepdims=True)

    @pl.when(step < pairs)
    def _():
        m = L - R
        held[pair] = attend_to(0, R, m, kf[R:], vf[R:], pb.at[0, :, pl.ds(0, m)], 1, True)
        dq[1, :, here] = flipped(attend_to(1, L, S, ks[...], vs[...], pb.at[0, :, pl.ds(m, S)], 2, False))
        for h in range(2):
            tsum[2 * pair + h] = diagonals(h)

    @pl.when(step >= pairs)
    def _():
        dq[0, :, here] = flipped(held[pair] + attend_to(0, 0, R, kf[:R], vf[:R], pa.at[0], 0, True))
        for h in range(2):
            tsum[2 * pair + h] = tsum[2 * pair + h] + diagonals(h)

    @pl.when(step == steps - 1)
    def _():
        rest = [stage for t in sorted(plan) if t >= 2 * steps for stage in plan[t]]

        def some(count):
            for _ in range(min(count, len(rest))):
                rest.pop(0)()

        for load in loads[3:]:
            load.wait()
        later = sums[early:]
        into_slabs(dot(nkt[...], dv[...]), mats[2])
        later[2].one()
        some(2)
        into_slabs(dot(nkt[...], dk[...]), mats[1])
        later[1].one()
        some(2)
        into_slabs(dot(nkt[:, :R], dq[0]) + dot(nst[...], dq[1]), mats[0])
        later[0].one()
        some(100)
        later[2].two()
        toks[0], toks[1] = swapped(flag, toks[0], toks[1])
        own = [dot_nt(dq[0], ws[0]) + dot_nt(dk[:R], ws[1]) + dot_nt(dv[:R], ws[2]), dot_nt(dq[1], ws[0])]
        later[1].two()
        later[2].three()
        long.wait()
        pl.when(at.x == 1)(short.wait_send)
        pl.when(at.x == 0)(short.wait_recv)
        gain = grow[0:1]
        keys = jnp.where(at.x == 0, ends[...] + gshort[...].astype(F32), 0.0)
        total = jnp.zeros((1, D), F32)
        for i in range(2):
            d = own[i] + (gfar[...].astype(F32) if i == 0 else jnp.concatenate([keys, jnp.zeros((R - S, D), F32)], axis=0))
            x = toks[i].astype(F32)
            back = norm_rows(x)
            a = gain * d
            total = total + jnp.sum(d * x * back, axis=0, keepdims=True)
            part = back * a - x * (back * back * back) * jnp.mean(a * x, axis=1, keepdims=True)
            toks[i] = (dress[i * R : (i + 1) * R] + part).astype(BF)
        toks[0], toks[1] = swapped(flag, toks[0], toks[1])
        finish = pltpu.make_async_copy(toks, gtok, local.at[len(sums) + len(loads)])
        finish.start()
        small[...] = jnp.zeros_like(small)
        lines = D // 128
        for i in range(lines):
            small[i : i + 1] = total[:, 128 * i : 128 * (i + 1)]
            small[lines + i : lines + i + 1] = dg2[:, 128 * i : 128 * (i + 1)]
        for h in range(2 * pairs):
            for i in range(4):
                spots = 2 * lines + 4 * h + i
                small[spots : spots + 1] = tsum[h, :, 128 * i : 128 * (i + 1)]
        small_chain[0]()
        later[0].two()
        later[1].three()
        small_chain[1]()
        later[2].four()
        later[0].three()
        small_chain[2]()
        later[1].four()
        small_chain[3]()
        later[0].four()
        for s in later[::-1]:
            s.five()
        small_chain[4]()
        finish.wait()


def backward_call(flag, q, kf, vf, ks, vs, o, do, pa, pb, cs, layout, parts, planes, nkt, nst, wq, wk, wv, tok, dres, grow, dg2):
    n, R, D = q.shape
    L, S = kf.shape[0], ks.shape[0]
    pairs = pa.shape[0]
    E = D // (2 * pairs)
    W = 2 * E
    KT = L + S
    whole = lambda a: pl.BlockSpec(a.shape, lambda j: (0,) * len(a.shape))
    anywhere = pl.BlockSpec(memory_space=pl.ANY)
    early = lambda j: jnp.minimum(j, pairs - 1)
    late = lambda j: jnp.maximum(j - pairs, 0)
    rows = pl.BlockSpec((n, R, W), lambda j: (0, 0, lax.rem(j, pairs)))
    keys = lambda a: pl.BlockSpec((a.shape[0], W), lambda j: (0, lax.rem(j, pairs)))
    shares = [p_.shape[4:] for p_ in parts] + [(D // 32, D)] * 3
    lines = -(-(2 * D // 128 + 8 * pairs) // 8) * 8
    outs = [jax.ShapeDtypeStruct((n, R, D), BF), jax.ShapeDtypeStruct((lines, 128), F32)]
    outs += [jax.ShapeDtypeStruct(s, F32) for s in shares]
    vmem = lambda *s: pltpu.VMEM(s, BF)
    wide = lambda *s: pltpu.VMEM(s, F32)
    scratch = [vmem(SPAN + E, KT), vmem(R, 2 * W), vmem(2 * W, R), vmem(R, 2 * R), vmem(n, R, SPAN)]
    scratch += [wide(2, SPAN, SPAN), vmem(2 * R, W), vmem(2 * R, W), wide(pairs, W, R)]
    scratch += [vmem(n, R, D), vmem(KT, D), vmem(KT, D), vmem(D, KT), vmem(D, R)]
    scratch += [vmem(3, D, D), vmem(n, R, D), wide(n * R, D)]
    scratch += [vmem(R, D), vmem(S, D), vmem(R, D), vmem(S, D), wide(S, D)]
    scratch += [wide(2 * pairs, 1, 2 * SPAN), wide(lines, 128), wide(4, lines, 128), wide(6, lines, 128)]
    chunks = [(p_.shape[0],) + p_.shape[4:] for p_ in parts]
    copies = Sum.COPIES * (len(chunks) + 3) + 8
    scratch += [pltpu.SemaphoreType.DMA((copies,)), pltpu.SemaphoreType.DMA((copies,)), pltpu.SemaphoreType.DMA((len(chunks) + 12,))]
    scratch += sum([Sum.scratch(*s, 1) for s in chunks], [])
    scratch += [vmem(4, 2, 2, 2, D // 32, D)] * 3
    scratch += sum([Sum.scratch(4, *s, 0) for s in shares[len(parts):]], [])
    return pl.pallas_call(
        functools.partial(backward_kernel, R, L, S, E, pairs, planes),
        grid=(2 * pairs,),
        in_specs=[pl.BlockSpec(memory_space=pltpu.SMEM), rows, keys(kf), keys(vf), keys(ks), keys(vs), rows, rows]
        + [pl.BlockSpec((1, 2, R, R), lambda j: (late(j), 0, 0, 0)), pl.BlockSpec((1, 2, KT - R, R), lambda j: (early(j), 0, 0, 0))]
        + [pl.BlockSpec((3, 1, 2, R), lambda j: (0, lax.rem(j, pairs), 0, 0)), whole(layout)]
        + [anywhere] * (len(parts) + 7)
        + [whole(grow), whole(dg2)],
        out_specs=[anywhere] + [whole(s) for s in outs[1:]],
        out_shape=outs,
        scratch_shapes=scratch,
        compiler_params=pltpu.CompilerParams(
            vmem_limit_bytes=60 * 2**20, dimension_semantics=("arbitrary",), collective_id=1, has_side_effects=True
        ),
        name="backward",
    )(flag, q, kf, vf, ks, vs, o, do, pa, pb, cs, layout, *parts, nkt, nst, wq, wk, wv, tok, dres, grow, dg2)


EPSILON = 1e-06
THRESHOLDS = (12, 16, 23, 32, 46, 64, 91)
BOTH = ("dp", "blk")


def bucket_np(relative):
    magnitude = np.abs(relative)
    larger = 8 + sum((magnitude >= limit).astype(np.int64) for limit in THRESHOLDS)
    return np.where(magnitude < 8, magnitude, larger) + 16 * (relative > 0)


def bucket_rows(distance, buckets):
    return (bucket_np(distance)[:, None] == np.arange(buckets)[None, :]).astype(np.float32)


def norm_parts(x, gain):
    back = lax.rsqrt(jnp.mean(x * x, axis=-1, keepdims=True) + EPSILON)
    return (x * back * gain).astype(BF), back


def norm_back(d, x, back, gain):
    a = gain * d
    grad_gain = jnp.sum(d * x * back, axis=0)
    return back * a - x * back**3 * jnp.mean(a * x, axis=-1, keepdims=True), grad_gain


def mm(a, b, dims):
    return lax.dot_general(a, b, (dims, ((), ())), preferred_element_type=F32)


def gather_weights(gain_one, wq, wk, wv, wo, gain_two, wi, wt):
    full = lambda a: lax.all_gather(a, BOTH, axis=0, tiled=True)
    packed = full(jnp.concatenate([wq, wk, wv, wo, wi], axis=1))
    width = wq.shape[1]
    gains = full(jnp.stack([gain_one, gain_two], axis=1))
    return packed[:, : 3 * width], packed[:, 3 * width : 4 * width], packed[:, 4 * width :], full(wt), gains[:, 0], gains[:, 1]


def scatter_sums(dqkv, dwo, dwi, dwt, dg1, dg2):
    take = lambda a: lax.psum_scatter(a, BOTH, scatter_dimension=0, tiled=True)
    width = dwo.shape[1]
    packed = take(jnp.concatenate([dqkv, dwo, dwi], axis=1).astype(BF)).astype(F32)
    gains = take(jnp.stack([dg1, dg2], axis=1))
    parts = [packed[:, i * width : (i + 1) * width] for i in range(4)]
    return parts, packed[:, 4 * width :], take(dwt.astype(BF)).astype(F32), gains[:, 0], gains[:, 1]


def on_any_device(tokens, layout, lengths, gain_one, wq, wk, wv, wo, gain_two, wi, wt, table, grad_out):
    n, R, D = tokens.shape
    H = table.shape[1]
    G = lax.axis_size("blk")
    me = lax.axis_index("blk")
    L = layout.shape[1]
    S = L // 8
    order = jnp.argsort(-lengths, stable=True)
    place = jnp.argsort(order)
    tok = tokens[order]
    gout = grad_out[order]
    lay = layout[order]
    lens = lengths[order]

    def from_step(x, s):
        return lax.ppermute(x, "blk", [(i, (i - s) % G) for i in range(G)])

    pieces = [tok[:-1]] + [from_step(tok[:-1], s) for s in range(1, G)]
    xf = jnp.concatenate(pieces, axis=1)
    first = tok[-1, :S]
    xs = jnp.where(me == 0, first, sum(lax.ppermute(first, "blk", [(0, i)]) for i in range(1, G)))
    lay_turned = jnp.roll(lay, -me * R, axis=1)
    layq = lay_turned[:, None, :R]
    layf = lay_turned[:-1, None, :]
    lays = lay[-1:, :S]
    spots = (jnp.arange(L) + me * R) % L
    mask = jnp.where(spots[None, :, None] < lens[:-1, None, None], 0.0, -1e30).astype(F32)

    wqkv, wo_all, wi_all, wt_all, g1, g2 = gather_weights(gain_one, wq, wk, wv, wo, gain_two, wi, wt)
    g1 = g1.astype(F32)
    g2 = g2.astype(F32)
    hidden = tok.reshape(n * R, D).astype(F32)
    normed, r1 = norm_parts(hidden, g1)
    xkeys = jnp.concatenate([xf.reshape((n - 1) * L, D), xs], axis=0)
    nkeys, _ = norm_parts(xkeys.astype(F32), g1)
    q = (mm(normed, wqkv[:, :D], ((1,), (0,))).astype(BF) * jnp.asarray(0.125, BF)).reshape(n, R, D)
    k = mm(nkeys, wqkv[:, D : 2 * D], ((1,), (0,))).astype(BF)
    v = mm(nkeys, wqkv[:, 2 * D :], ((1,), (0,))).astype(BF)
    cut = (n - 1) * L
    kf, ks = k[:cut].reshape(n - 1, L, D), k[cut:]
    vf, vs = v[:cut].reshape(n - 1, L, D), v[cut:]
    lane = np.arange(2 * SPAN)
    turned = np.where(lane >= SPAN, lane - 2 * SPAN, lane)
    urow = mm(table, bucket_rows(-turned, table.shape[0]).astype(BF), ((0,), (1,))).reshape(H // 2, 2, 2 * SPAN)
    o, p, l = attend_call(q, kf, vf, ks, vs, layq, layf, lays, mask, urow)

    attended = o.reshape(n * R, D)
    resid = hidden + mm(attended, wo_all, ((1,), (0,)))
    normed_two, r2 = norm_parts(resid, g2)
    pre = mm(normed_two, wi_all, ((1,), (0,)))
    act, act_back = jax.vjp(lambda x: jax.nn.gelu(x, approximate=False), pre)
    act = act.astype(BF)
    mixed = (resid + mm(act, wt_all, ((1,), (0,)))).astype(BF)
    up = gout.reshape(n * R, D)
    dwt = mm(act, up, ((0,), (0,)))
    (dpre,) = act_back(mm(up, wt_all, ((1,), (1,))))
    dpre = dpre.astype(BF)
    dwi = mm(normed_two, dpre, ((0,), (0,)))
    dn2 = mm(dpre, wi_all, ((1,), (1,)))
    dresid, dg2 = norm_back(dn2, resid, r2, g2)
    dresid = dresid + up.astype(F32)
    low = dresid.astype(BF)
    dwo = mm(attended, low, ((0,), (0,)))
    datt = mm(low, wo_all, ((1,), (1,))).astype(BF).reshape(n, R, D)

    dq, dkf, dvf, dks, dvs, t = attend_back_call(q, kf, vf, ks, vs, layq, layf, lays, o, datt, p, l)
    dtable = jnp.einsum(
        "hj,jb->bh", t.reshape(H, 2 * SPAN), bucket_rows(SPAN - 1 - lane, table.shape[0]), precision=lax.Precision.HIGHEST
    )
    dq = dq.reshape(n * R, D)
    dk = jnp.concatenate([dkf.reshape(cut, D), dks], axis=0)
    dv = jnp.concatenate([dvf.reshape(cut, D), dvs], axis=0)
    dnk = mm(dk, wqkv[:, D : 2 * D], ((1,), (1,))) + mm(dv, wqkv[:, 2 * D :], ((1,), (1,)))
    dnf = dnk[:cut].reshape(n - 1, L, D)
    dns = dnk[cut:].astype(BF)
    far = sum(
        lax.ppermute(dnf[:, s * R : (s + 1) * R].astype(BF), "blk", [(i, (i + s) % G) for i in range(G)]).astype(F32)
        for s in range(1, G)
    )
    near = jnp.where(
        me == 0, dnk[cut:] + sum(lax.ppermute(dns, "blk", [(i, 0)]).astype(F32) for i in range(1, G)), 0.0
    )
    extra = jnp.concatenate([dnf[:, :R] + far, jnp.pad(near, ((0, R - S), (0, 0)))[None]], axis=0).reshape(n * R, D)
    dn1 = mm(dq, wqkv[:, :D], ((1,), (1,))) + extra
    dwq = mm(normed, dq, ((0,), (0,)))
    dwk = mm(nkeys, dk, ((0,), (0,)))
    dwv = mm(nkeys, dv, ((0,), (0,)))
    dx, dg1 = norm_back(dn1, hidden, r1, g1)
    gtok = (dresid + dx).astype(BF)
    parts, gwi, gwt, gg1, gg2 = scatter_sums(jnp.concatenate([dwq, dwk, dwv], axis=1), dwo, dwi, dwt, dg1, dg2)
    dtable = lax.psum(dtable, BOTH)
    return (
        mixed.reshape(n, R, D)[place],
        gtok.reshape(n, R, D)[place],
        gg1,
        parts[0],
        parts[1],
        parts[2],
        parts[3],
        gg2,
        gwi,
        gwt,
        dtable,
    )


def on_device(tokens, layout, lengths, gain_one, wq, wk, wv, wo, gain_two, wi, wt, table, grad_out):
    n, R, D = tokens.shape
    H = table.shape[1]
    G = lax.axis_size("blk")
    me = lax.axis_index("blk")
    L = layout.shape[1]
    S = L // 8
    lane = np.arange(2 * SPAN)
    turned = np.where(lane >= SPAN, lane - 2 * SPAN, lane)
    basis = jnp.asarray(bucket_rows(-turned, table.shape[0]).T, BF)
    column = jnp.arange(128)[None, :]
    gains = jnp.where(column == 0, gain_one[:, None], jnp.where(column == 1, gain_two[:, None], 0)).astype(BF)
    o, pa, pb, cs, grow, q, kf, vf, ks, vs, nkt, nst, *wholes = forward_call(
        lengths, tokens, layout, table.astype(F32), basis, [gains, wq, wk, wv, wo, wi, wt], S
    )
    flat = lambda a: a.reshape(-1, a.shape[-1])
    wq_all, wk_all, wv_all, wo_all, wi_all, wt_all = [flat(a) for a in wholes]
    rows = lambda a: a.reshape(n * R, D)
    mixed, dresid, datt, dwo, *handed = feed_forward_call(
        lengths, rows(o), rows(tokens), rows(grad_out), wo_all, grow, wi_all, wt_all
    )
    count = 2 * (4 - FF_SUMS)
    dg2, done = handed[count], handed[count + 1 :]
    planes = sum([(None, j) for j in range(FF_SUMS, 4)], ()) + (None,)
    gtok, small, *sums = backward_call(
        lengths, q, kf, vf, ks, vs, o, datt.reshape(n, R, D), pa, pb, cs, layout,
        handed[:count] + [dwo.reshape(4, 2, 2, 2, -1, D)], planes,
        nkt, nst, wq_all, wk_all, wv_all, tokens, dresid, grow, dg2,
    )
    gwo, gwq, gwk, gwv = sums[count:]
    gwi = jnp.concatenate(done[:FF_SUMS] + sums[0:count:2], axis=1)
    gwt = done[FF_SUMS]
    for j in range(FF_SUMS, 4):
        gwt = jnp.where(lax.axis_index("dp") // 4 == j, sums[2 * (j - FF_SUMS) + 1], gwt)
    small = small.reshape(-1)
    mine = (lax.axis_index("dp") * G + me) * (D // 32)
    gg1, gg2 = [lax.dynamic_slice_in_dim(small, mine + i * D, D // 32) for i in range(2)]
    t = small[2 * D : 2 * D + H * 2 * SPAN].reshape(H, 2 * SPAN)
    dtable = jnp.einsum(
        "hj,jb->bh", t, bucket_rows(SPAN - 1 - lane, table.shape[0]), precision=lax.Precision.HIGHEST
    )
    return mixed.reshape(n, R, D), gtok, gg1, gwq, gwk, gwv, gwo, gg2, gwi, gwt, dtable


def solution(mesh):
    rows = P(BOTH, None)
    items = P("dp", "blk", None)
    known = dict(mesh.shape) == {"dp": 16, "blk": 2}

    def body(tokens, *rest):
        return (on_device if known and tokens.shape[0] == 2 else on_any_device)(tokens, *rest)

    return jax.shard_map(
        body,
        mesh=mesh,
        in_specs=(items, P("dp", None), P("dp"), P(BOTH), rows, rows, rows, rows, P(BOTH), rows, rows, P(), items),
        out_specs=(items, items, P(BOTH), rows, rows, rows, rows, P(BOTH), rows, rows, P()),
        check_vma=False,
    )
```
